32 devices in a mesh: groups: 2 (over y), dp: 4 (over z), mp: 4 (over x, core).
Axes of the slice: x: 2, y: 2, z: 4, core: 2. Of those that a mesh axis runs over, the one named last changes fastest.
Arguments:
- inputs: bfloat16 [4096, 6144], P(('groups', 'dp'), 'mp'), parts along dimension 0, may hold values from -6 to 6
- output_gradient: bfloat16 [4096, 1024], P(('groups', 'dp'), 'mp'), parts along dimension 0, may hold values from -1.5 to 1.5
- frozen_key_weight: bfloat16 [6144, 1024], P('mp'), may hold values from -0.1875 to 0.1875
- adapter_down_factors: bfloat16 [512, 16, 6144], P('dp', None, 'mp'), may hold values from -0.09375 to 0.09375
- adapter_up_factors: bfloat16 [512, 16, 1024], P('dp', None, 'mp'), may hold values from -0.3125 to 0.3125
- token_adapter_index: int32 [4096, 2], P(('groups', 'dp')), parts along dimension 0, may hold values from 0 to 511, as said below
- gates: bfloat16 [4096, 2], P(('groups', 'dp')), parts along dimension 0, may hold values from 0.099609375 to 0.8984375
Outputs:
- input_gradient: bfloat16 [4096, 6144], P(('groups', 'dp'), 'mp'), parts along dimension 0
- grad_gate: bfloat16 [4096, 2], P(('groups', 'dp')), parts along dimension 0
- grad_down: bfloat16 [1024, 16, 6144], P(('groups', 'dp'), None, 'mp'), parts along dimension 0
- grad_up: bfloat16 [1024, 16, 1024], P(('groups', 'dp'), None, 'mp'), parts along dimension 0
The draws below stay inside these ranges and needn't reach their ends.
There are 2 independent parts, one for each index of `groups`. The reference program is written for one: setup_inputs(seed, part) draws one part's arguments, and reference() takes and returns one part's arrays. A program takes and returns all parts, laid end to end along the dimension named above; an argument that names none is the same for every part. Nothing has to cross between parts.
Inputs may be any that keep to these rules, and one draw needn't show every extreme that they name: `token_adapter_index`: each token names two different adapters; adapter e belongs to owner e // 128; the 1024 routes of one device's tokens name the adapters of one owner at most 512 times, and in every draw some owner is named exactly 512 times by the routes of every device.
All inputs are finite; a program needn't handle non-finite values.
Results may differ from the reference program's by a relative error of at most 0.005.
Values may be sent and summed in bfloat16 or wider, within the bound.
No kernel may reach another device: no remote copies, remote signals or barrier semaphores. Data moves between devices by JAX's collectives and lax.ppermute only.
A program may use at most 128 MiB of HBM per device.

```python
import math
import jax
import jax.numpy as jnp
from jax import lax

MODEL_WIDTH = 6144
KEY_WIDTH = 1024
ADAPTER_RANK = 16
ADAPTER_COUNT = 512
TOK_DEV = 512
TOKEN_COUNT = 2048
ADP_DEV = 128
CAP = 512
N_DP = 4


def draw_token_adapter_index(key, part):
    key = jax.random.fold_in(key, 5)
    hot_owner = jax.random.randint(jax.random.fold_in(key, 11), (), 0, N_DP)

    def one_block(block_id):
        block_key = jax.random.fold_in(key, 1000 + block_id)
        key_heat, key_noise, key_offset, key_shuffle = jax.random.split(block_key, 4)
        heat_rank = jax.random.permutation(key_heat, N_DP)
        pool_index = jnp.arange(N_DP * CAP)
        pool_owner = pool_index // CAP
        column = pool_index % CAP
        noise_term = jax.random.randint(key_noise, (N_DP * CAP,), 0, 64)
        priority = (column + 1) * (heat_rank[pool_owner] + 1) * 64 + noise_term
        priority = jnp.where(column == 0, 1, priority)
        priority = jnp.where(pool_owner == hot_owner, 0, priority)
        picked = jnp.argsort(priority, stable=True)[:2 * TOK_DEV]
        picked_owner = picked // CAP
        picked_column = picked % CAP
        offset = jax.random.randint(key_offset, (N_DP,), 0, ADP_DEV)
        owner_lane = jnp.arange(N_DP)
        offset = jnp.where((block_id == 0) & (owner_lane == 0), 0, offset)
        offset = jnp.where((block_id == 0) & (owner_lane == N_DP - 1), ADP_DEV - 1, offset)
        adapter = picked_owner * ADP_DEV + (picked_column + offset[picked_owner]) % ADP_DEV
        ordered = jnp.sort(adapter)
        paired = jnp.stack([ordered[:TOK_DEV], ordered[TOK_DEV:]], axis=1)
        shuffle = jax.random.permutation(key_shuffle, TOK_DEV)
        return paired[shuffle]
    all_blocks = jax.vmap(one_block)(jnp.arange(N_DP))
    return all_blocks.reshape(TOK_DEV * N_DP, 2).astype(jnp.int32)


def levels(stream_key, shape, cuts, least, high):
    factor_of, own = 1.0, jax.random.fold_in(stream_key, 6)
    for dim, blocks in cuts:
        draws = jnp.exp(jax.random.uniform(jax.random.fold_in(own, dim), (blocks,), jnp.float32, least / len(cuts), high / len(cuts)))
        factor_of = factor_of * jnp.repeat(draws, shape[dim] // blocks).reshape([-1 if axis == dim else 1 for axis in range(len(shape))])
    return factor_of


def gaussian(key, shape, deviation, reach, pieces=(), kind=jnp.bfloat16):
    gain = levels(key, shape, pieces, -0.22, 0.18) if pieces else 1.0
    entries = jax.random.normal(key, shape, jnp.float32) * deviation * gain
    return jnp.minimum(jnp.maximum(entries, -reach), reach).astype(kind)


def setup_inputs(seed: int = 0, part: int = 0) -> dict:
    seeds = jax.random.split(jax.random.key(seed), 8)
    own_keys = jax.random.split(jax.random.fold_in(seeds[7], part), 8)
    return {
        "inputs": gaussian(own_keys[0], (TOKEN_COUNT, MODEL_WIDTH), 1.0, 6.0, ((0, 4), (1, 4))),
        "output_gradient": gaussian(own_keys[1], (TOKEN_COUNT, KEY_WIDTH), 0.25, 1.5, ((0, 4), (1, 4))),
        "frozen_key_weight": gaussian(seeds[2], (MODEL_WIDTH, KEY_WIDTH), KEY_WIDTH ** -0.5, 0.1875, ((0, 4),)),
        "adapter_down_factors": gaussian(seeds[3], (ADAPTER_COUNT, ADAPTER_RANK, MODEL_WIDTH), 0.015, 0.09375, ((0, 4), (2, 4))),
        "adapter_up_factors": gaussian(seeds[4], (ADAPTER_COUNT, ADAPTER_RANK, KEY_WIDTH), 0.05, 0.3125, ((0, 4), (2, 4))),
        "token_adapter_index": draw_token_adapter_index(jax.random.fold_in(jax.random.fold_in(seeds[7], part), 71), part),
        "gates": jnp.clip(0.099609375 + 0.7988281 * jax.random.uniform(own_keys[6], (TOKEN_COUNT, 2), jnp.float32) ** levels(own_keys[6], (TOKEN_COUNT, 2), ((0, 4),), -0.2, 0.2), 0.099609375, 0.8984375).astype(jnp.bfloat16),
    }


def reference(inputs, output_gradient, frozen_key_weight, adapter_down_factors, adapter_up_factors, token_adapter_index, gates):
    frozen_gradient = jnp.dot(output_gradient, frozen_key_weight.T, preferred_element_type=jnp.float32)
    routes = token_adapter_index.reshape(-1).astype(jnp.int32)
    route_count = routes.shape[0]
    step_rows = math.gcd(route_count, 512)
    gate_flat = gates.reshape(-1).astype(jnp.float32)
    token_of = (jnp.arange(route_count) // 2).astype(jnp.int32)

    def single_update(carry, partial_results):
        down_gradient_total, up_gradient_total = carry
        local_route_index, tokens_here, gates_here = partial_results
        rows_in = inputs[tokens_here].astype(jnp.float32)
        rows_out = output_gradient[tokens_here].astype(jnp.float32)
        local_down_factors = adapter_down_factors[local_route_index].astype(jnp.float32)
        local_up_factors = adapter_up_factors[local_route_index].astype(jnp.float32)
        low_in = jnp.einsum("nd,nrd->nr", rows_in, local_down_factors)
        low_out = jnp.einsum("nd,nrd->nr", rows_out, local_up_factors)
        gate_gradient = jnp.sum(low_in * low_out, axis=1).astype(jnp.bfloat16)
        scaled_output = lax.optimization_barrier((gates_here[:, None] * low_out).astype(jnp.bfloat16)).astype(jnp.float32)
        scaled_in = lax.optimization_barrier((gates_here[:, None] * low_in).astype(jnp.bfloat16)).astype(jnp.float32)
        adapter_rows = jnp.einsum("us,usc->uc", scaled_output, local_down_factors).astype(jnp.bfloat16)
        down_gradient_total = down_gradient_total.at[local_route_index].add(jnp.einsum("nr,nd->nrd", scaled_output, rows_in))
        up_gradient_total = up_gradient_total.at[local_route_index].add(jnp.einsum("nr,nd->nrd", scaled_in, rows_out))
        return (down_gradient_total, up_gradient_total), (adapter_rows, gate_gradient)

    down_initial_zeros = jnp.zeros((ADAPTER_COUNT, ADAPTER_RANK, MODEL_WIDTH), jnp.float32)
    up_initial_zeros = jnp.zeros((ADAPTER_COUNT, ADAPTER_RANK, KEY_WIDTH), jnp.float32)
    partial_results = (routes.reshape(-1, step_rows), token_of.reshape(-1, step_rows), gate_flat.reshape(-1, step_rows))
    (down_gradient_total, up_gradient_total), (adapter_total, gate_everything) = lax.scan(single_update, (down_initial_zeros, up_initial_zeros), partial_results)
    adapter_total = adapter_total.reshape(TOKEN_COUNT, 2, MODEL_WIDTH).astype(jnp.float32)
    input_gradient = (frozen_gradient + adapter_total[:, 0] + adapter_total[:, 1]).astype(jnp.bfloat16)
    return input_gradient, gate_everything.reshape(TOKEN_COUNT, 2), down_gradient_total.astype(jnp.bfloat16), up_gradient_total.astype(jnp.bfloat16)
```

```python
import functools

import jax
import jax.numpy as jnp
from jax import lax
from jax.experimental import pallas as pl
from jax.experimental.pallas import tpu as pltpu
from jax.sharding import PartitionSpec as P

BF = jnp.bfloat16
F32 = jnp.float32
CHUNKS = 2
NT = (((1,), (1,)), ((), ()))


def call(body, out_shape, *, grid=None, in_specs=None, out_specs=None, scratch=(), prefetch=0,
         aliases=None, flops=0, moved=0, vmem=40):
    steps = len(grid) if grid else 0
    return pl.pallas_call(
        body,
        out_shape=out_shape,
        grid_spec=pltpu.PrefetchScalarGridSpec(
            num_scalar_prefetch=prefetch,
            grid=grid or (1,),
            in_specs=in_specs,
            out_specs=out_specs,
            scratch_shapes=list(scratch),
        ),
        input_output_aliases=aliases or {},
        compiler_params=pltpu.CompilerParams(
            vmem_limit_bytes=vmem << 20, dimension_semantics=("arbitrary",) * max(steps, 1)
        ),
        cost_estimate=pl.CostEstimate(flops=int(flops), bytes_accessed=int(moved), transcendentals=0),
    )


def whole(shape):
    return pl.BlockSpec(shape, lambda *_: (0,) * len(shape))


ANY = pl.BlockSpec(memory_space=pl.ANY)


def pack_body(index_ref, gate_ref, rows_ref, out_ref):
    count, width = rows_ref.shape
    out_ref[:count, :] = rows_ref[...]
    index = index_ref[...]
    gate = gate_ref[...].astype(F32)
    high, low = (index >> 4).astype(F32), (index & 15).astype(F32)
    pieces = []
    for vector in (high, low, gate):
        for slot in range(2):
            for part in range(count // width):
                pieces.append(vector[slot : slot + 1, part * width : (part + 1) * width])
    extra = out_ref.shape[0] - count
    if extra > len(pieces):
        pieces.append(jnp.zeros((extra - len(pieces), width), F32))
    out_ref[count:, :] = jnp.concatenate(pieces, axis=0).astype(BF)


def pack_rows(index, gate, rows):
    count, width = rows.shape
    extra = -(-6 * (count // width) // 16) * 16
    shape = (count + extra, width)
    return call(
        pack_body,
        jax.ShapeDtypeStruct(shape, BF),
        in_specs=[whole(index.shape), whole(gate.shape), whole(rows.shape)],
        out_specs=whole(shape),
        moved=4 * count * width,
    )(index, gate, rows)


def unpack_extra(block, count, width, base):
    per = count // width
    vectors = []
    for v in range(6):
        rows = block[v * per : (v + 1) * per, :].astype(F32)
        vectors.append(jnp.concatenate([rows[q : q + 1, :] for q in range(per)], axis=1))
    ids = [vectors[k] * 16.0 + vectors[2 + k] - base for k in range(2)]
    return jnp.concatenate(ids + vectors[4:6] + [jnp.zeros((4, count), F32)], axis=0)


def pick(product, ids, first, rank, kept):
    kept = list(kept)
    for a in range(product.shape[0] // rank):
        rows = product[a * rank : (a + 1) * rank, :]
        here = (first + a).astype(F32) if hasattr(first, "astype") else float(first + a)
        for k in range(2):
            kept[k] = jnp.where(ids[k : k + 1, :] == here, rows, kept[k])
    return kept


def project_out_body(rank, base_ref, up_ref, *refs):
    blocks, (part_ref, aux_ref) = refs[:-2], refs[-2:]
    count = part_ref.shape[1]
    width = up_ref.shape[1]
    total = up_ref.shape[0]
    step = min(1024, total)
    base = base_ref[0].astype(F32)
    for s, block in enumerate(blocks):
        aux = unpack_extra(block[count:, :], count, width, base)
        aux_ref[8 * s : 8 * s + 8, :] = aux
        ids = aux[0:2, :]

        def body(b, kept):
            product = lax.dot_general(
                up_ref[pl.ds(pl.multiple_of(b * step, step), step), :], block[:count, :], NT,
                preferred_element_type=F32,
            )
            return tuple(pick(product, ids, b * (step // rank), rank, kept))

        zero = jnp.zeros((rank, count), F32)
        kept = lax.fori_loop(0, total // step, body, (zero, zero))
        part_ref[2 * rank * s : 2 * rank * s + rank, :] = kept[0]
        part_ref[2 * rank * s + rank : 2 * rank * (s + 1), :] = kept[1]


def project_out(base, up, blocks, count, rank):
    slots = len(blocks)
    total, width = up.shape
    shapes = [(slots * 2 * rank, count), (slots * 8, count)]
    return call(
        functools.partial(project_out_body, rank),
        [jax.ShapeDtypeStruct(s, F32) for s in shapes],
        in_specs=[whole(up.shape)] + [whole(b.shape) for b in blocks],
        out_specs=[whole(s) for s in shapes],
        prefetch=1,
        flops=2 * slots * count * total * width,
        moved=2 * (slots * count * width + total * width),
        vmem=48,
    )(base, up, *blocks)


def project_in_body(rank, chunks, plan_ref, down_ref, aux_ref, before_ref, *refs):
    rows, (out_ref, kept_ref) = refs[:-2], refs[-2:]
    source, b = pl.program_id(0), pl.program_id(1)
    step = down_ref.shape[0]
    valid, slot = plan_ref[2 * source], plan_ref[2 * source + 1]

    @pl.when((source == 0) & (b == 0))
    def _():
        out_ref[...] = before_ref[...]

    @pl.when(valid == 1)
    def _():
        @pl.when(b == 0)
        def _():
            kept_ref[...] = jnp.zeros_like(kept_ref)

        for s in range(len(rows) // chunks):
            @pl.when(source == s)
            def _():
                at = 0
                for c in range(chunks):
                    ref = rows[s * chunks + c]
                    size = ref.shape[0]
                    ids = aux_ref[pl.ds(pl.multiple_of(slot * 8, 8), 8), at : at + size]
                    product = lax.dot_general(
                        down_ref[...], ref[...], NT, preferred_element_type=F32
                    )
                    kept = [kept_ref[:rank, at : at + size], kept_ref[rank:, at : at + size]]
                    kept = pick(product, ids, b * (step // rank), rank, kept)
                    kept_ref[:rank, at : at + size] = kept[0]
                    kept_ref[rank:, at : at + size] = kept[1]
                    at += size

        @pl.when(b == pl.num_programs(1) - 1)
        def _():
            out_ref[pl.ds(pl.multiple_of(slot * 2 * rank, 2 * rank), 2 * rank), :] = kept_ref[...]


def project_in(plan, down, aux, before, rows, chunks, rank):
    total, width = down.shape
    sources = len(rows) // chunks
    step = min(512, total)
    count = aux.shape[1]
    return call(
        functools.partial(project_in_body, rank, chunks),
        jax.ShapeDtypeStruct(before.shape, F32),
        grid=(sources, total // step),
        in_specs=[
            pl.BlockSpec((step, width), lambda s, b, plan: (b * plan[2 * s], 0)),
            whole(aux.shape),
            whole(before.shape),
        ]
        + [whole(r.shape) for r in rows],
        out_specs=whole(before.shape),
        scratch=[pltpu.VMEM((2 * rank, count), F32)],
        prefetch=1,
        aliases={3: 0},
        flops=2 * count * total * width,
        moved=2 * (count * width + total * width),
        vmem=48,
    )(plan, down, aux, before, *rows)


def adapter_rows_body(rank, parts, order_ref, *refs):
    part_refs, (aux_ref, down_ref, out_ref, spread_ref) = refs[:parts], refs[parts:]
    n, s = pl.program_id(0), pl.program_id(1)
    slot = order_ref[s]
    count = aux_ref.shape[1]
    total = down_ref.shape[0]
    here = pl.ds(pl.multiple_of(s * count, count), count)

    @pl.when(n == 0)
    def _():
        at = pl.ds(pl.multiple_of(slot * 2 * rank, 2 * rank), 2 * rank)
        low = part_refs[0][at, :]
        for ref in part_refs[1:]:
            low = low + ref[at, :]
        aux = aux_ref[pl.ds(pl.multiple_of(slot * 8, 8), 8), :]
        repeat = 128 // rank
        group = (lax.broadcasted_iota(jnp.int32, (128, count), 0) // rank).astype(F32)
        keys, values = [], []
        for k in range(2):
            scaled = (aux[2 + k : 3 + k, :] * low[k * rank : (k + 1) * rank, :]).astype(BF).astype(F32)
            values.append(jnp.concatenate([scaled] * repeat, axis=0).T)
            keys.append((aux[k : k + 1, :] - group).T)
        for g in range(total // 128):
            first = float(g * repeat)
            spread = jnp.where(keys[0] == first, values[0], jnp.where(keys[1] == first, values[1], 0.0))
            spread_ref[here, g * 128 : (g + 1) * 128] = spread.astype(BF)

    out_ref[0] = jnp.dot(spread_ref[here, :], down_ref[...], preferred_element_type=F32).astype(BF)


def adapter_rows(order, parts, aux, down, rank):
    slots = order.shape[0]
    total, width = down.shape
    count = aux.shape[1]
    step = 256
    return call(
        functools.partial(adapter_rows_body, rank, len(parts)),
        jax.ShapeDtypeStruct((slots, count, width), BF),
        grid=(width // step, slots),
        in_specs=[whole(p.shape) for p in parts]
        + [whole(aux.shape), pl.BlockSpec((total, step), lambda n, s, order: (0, n))],
        out_specs=pl.BlockSpec((1, count, step), lambda n, s, order: (s, 0, n)),
        scratch=[pltpu.VMEM((slots * count, total), BF)],
        prefetch=1,
        flops=2 * slots * count * total * width,
        moved=2 * (total * width + slots * count * width),
        vmem=48,
    )(order, *parts, aux, down)


def add_body(plan_ref, first_ref, second_ref, near_ref, far_ref, *refs):
    outs = refs[:2]
    held, terms, in_sem, term_sem, out_sem = refs[2:]
    size, width = held.shape[1:]
    pieces = in_sem.shape[1]
    piece = size // pieces
    row = plan_ref[4]
    for i, (source, out) in enumerate(zip((first_ref, second_ref), outs)):
        do, place = plan_ref[2 * i], plan_ref[2 * i + 1]

        def get(q):
            rows = pl.ds(q * piece, piece)
            return pltpu.make_async_copy(source.at[rows], held.at[i, rows], in_sem.at[i, q])

        def put(q):
            rows = pl.ds(q * piece, piece)
            return pltpu.make_async_copy(held.at[i, rows], out.at[rows], out_sem.at[i, q])

        def term(q, ref, index):
            rows = pl.ds(pl.multiple_of(row + q * piece, piece), piece)
            return pltpu.make_async_copy(
                ref.at[index, rows], terms.at[i, pl.ds(q * piece, piece)], term_sem.at[i, q]
            )

        @pl.when(do == 1)
        def _():
            for q in range(pieces):
                get(q).start()

                @pl.when(place == 0)
                def _():
                    term(q, near_ref, 0).start()

                @pl.when(place != 0)
                def _():
                    term(q, far_ref, jnp.maximum(place - 1, 0)).start()

            for q in range(pieces):
                get(q).wait()
                term(q, near_ref, 0).wait()
                rows = pl.ds(q * piece, piece)
                held[i, rows, :] = (held[i, rows, :].astype(F32) + terms[i, rows, :].astype(F32)).astype(BF)
                put(q).start()
            for q in range(pieces):
                put(q).wait()


def ring_add(plan, first, second, near, far):
    shape = first.shape
    pieces = 4 if shape[0] % 64 == 0 else 1
    return call(
        add_body,
        [jax.ShapeDtypeStruct(shape, BF)] * 2,
        in_specs=[ANY] * 4,
        out_specs=[ANY] * 2,
        scratch=[
            pltpu.VMEM((2,) + shape, BF),
            pltpu.VMEM((2,) + shape, BF),
            pltpu.SemaphoreType.DMA((2, pieces)),
            pltpu.SemaphoreType.DMA((2, pieces)),
            pltpu.SemaphoreType.DMA((2, pieces)),
        ],
        prefetch=1,
        aliases={1: 0, 2: 1},
        flops=2 * shape[0] * shape[1],
        moved=6 * shape[0] * shape[1],
    )(plan, first, second, near, far)


def spread_rows(values, ids, first, adapters):
    rows = []
    for a in range(adapters):
        here = (first + a).astype(F32)
        rows.append(
            jnp.where(ids[0:1, :] == here, values[0], jnp.where(ids[1:2, :] == here, values[1], 0.0)).astype(BF)
        )
    return jnp.concatenate(rows, axis=0)


def grad_down_body(rank, parts, where, plan_ref, *refs):
    part_refs, aux_ref = refs[:parts], refs[parts]
    row_refs = refs[parts + 1 : parts + 1 + len(where)]
    out_ref, rows_ref, scaled_ref, sem = refs[parts + 1 + len(where) :]
    b = pl.program_id(0)
    count = aux_ref.shape[1]
    slots = rows_ref.shape[0] // count
    step = out_ref.shape[0]

    def copies(act):
        for i, (source, offset) in enumerate(where):
            size = row_refs[i].shape[0]

            @pl.when(plan_ref[2 * source] == 1)
            def _():
                start = plan_ref[2 * source + 1] * count + offset
                act(
                    pltpu.make_async_copy(
                        row_refs[i], rows_ref.at[pl.ds(pl.multiple_of(start, size), size)], sem.at[i]
                    )
                )

    @pl.when(b == 0)
    def _():
        copies(lambda c: c.start())
        for s in range(slots):
            low = part_refs[0][2 * rank * s : 2 * rank * (s + 1), :]
            for ref in part_refs[1:]:
                low = low + ref[2 * rank * s : 2 * rank * (s + 1), :]
            for k in range(2):
                scaled = aux_ref[8 * s + 2 + k : 8 * s + 3 + k, :] * low[k * rank : (k + 1) * rank, :]
                scaled_ref[k, :, s * count : (s + 1) * count] = scaled.astype(BF).astype(F32)
        copies(lambda c: c.wait())

    spread = []
    for s in range(slots):
        values = [scaled_ref[k, :, s * count : (s + 1) * count] for k in range(2)]
        spread.append(
            spread_rows(values, aux_ref[8 * s : 8 * s + 2, :], b * (step // rank), step // rank)
        )
    out_ref[...] = jnp.dot(
        jnp.concatenate(spread, axis=1), rows_ref[...], preferred_element_type=F32
    ).astype(BF)


def grad_down(plan, parts, aux, rows, where, total, rank):
    count = aux.shape[1]
    slots = aux.shape[0] // 8
    width = rows[0].shape[1]
    step = min(256, total)
    return call(
        functools.partial(grad_down_body, rank, len(parts), where),
        jax.ShapeDtypeStruct((total, width), BF),
        grid=(total // step,),
        in_specs=[whole(p.shape) for p in parts] + [whole(aux.shape)] + [ANY] * len(rows),
        out_specs=pl.BlockSpec((step, width), lambda b, plan: (b, 0)),
        scratch=[
            pltpu.VMEM((slots * count, width), BF),
            pltpu.VMEM((2, rank, slots * count), F32),
            pltpu.SemaphoreType.DMA((len(rows),)),
        ],
        prefetch=1,
        flops=2 * slots * count * total * width,
        moved=2 * (total * width + slots * count * width),
        vmem=56,
    )(plan, *parts, aux, *rows)


def grad_up_body(rank, parts, slots, *refs):
    in_refs, out_refs, aux_ref = refs[:parts], refs[parts : 2 * parts], refs[2 * parts]
    blocks = refs[2 * parts + 1 : 2 * parts + 1 + slots]
    up_ref = refs[2 * parts + 1 + slots]
    gate_refs = refs[2 * parts + 2 + slots : 2 * parts + 2 + 2 * slots]
    rows_ref, scaled_ref = refs[-2:]
    b = pl.program_id(0)
    count = aux_ref.shape[1]
    step = up_ref.shape[0]

    @pl.when(b == 0)
    def _():
        for s in range(slots):
            rows_ref[s * count : (s + 1) * count, :] = blocks[s][:count, :]
            at = slice(2 * rank * s, 2 * rank * (s + 1))
            low_in, low_out = in_refs[0][at, :], out_refs[0][at, :]
            for ref in in_refs[1:]:
                low_in = low_in + ref[at, :]
            for ref in out_refs[1:]:
                low_out = low_out + ref[at, :]
            both = low_in * low_out
            gates = []
            for k in range(2):
                gates.append(jnp.sum(both[k * rank : (k + 1) * rank, :], axis=0, keepdims=True))
                scaled = aux_ref[8 * s + 2 + k : 8 * s + 3 + k, :] * low_in[k * rank : (k + 1) * rank, :]
                scaled_ref[k, :, s * count : (s + 1) * count] = scaled.astype(BF).astype(F32)
            gate_refs[s][...] = jnp.concatenate(gates, axis=0).astype(BF)

    spread = []
    for s in range(slots):
        values = [scaled_ref[k, :, s * count : (s + 1) * count] for k in range(2)]
        spread.append(
            spread_rows(values, aux_ref[8 * s : 8 * s + 2, :], b * (step // rank), step // rank)
        )
    up_ref[...] = jnp.dot(
        jnp.concatenate(spread, axis=1), rows_ref[...], preferred_element_type=F32
    ).astype(BF)


def grad_up(parts_in, parts_out, aux, blocks, total, rank):
    count = aux.shape[1]
    slots = len(blocks)
    width = blocks[0].shape[1]
    step = min(256, total)
    outs = [jax.ShapeDtypeStruct((total, width), BF)] + [jax.ShapeDtypeStruct((2, count), BF)] * slots
    arrays = [*parts_in, *parts_out, aux, *blocks]
    return call(
        functools.partial(grad_up_body, rank, len(parts_in), slots),
        outs,
        grid=(total // step,),
        in_specs=[whole(a.shape) for a in arrays],
        out_specs=[pl.BlockSpec((step, width), lambda b: (b, 0))] + [whole((2, count))] * slots,
        scratch=[pltpu.VMEM((slots * count, width), BF), pltpu.VMEM((2, rank, slots * count), F32)],
        flops=2 * slots * count * total * width,
        moved=2 * (total * width + slots * count * width),
    )(*arrays)


def finish_body(base_ref, first_ref, second_ref, *refs):
    out_ref = refs[-1]
    out_ref[...] = (
        base_ref[...] + first_ref[...].astype(F32) + second_ref[...].astype(F32)
    ).astype(BF)


def finish(base, first, second, chunk, before):
    size, width = first.shape
    step = min(64, size)
    blocks = size // step
    shift = pl.BlockSpec((step, width), lambda i: (i + chunk * blocks, 0))
    local = pl.BlockSpec((step, width), lambda i: (i, 0))
    arrays = [base, first, second] + ([] if before is None else [before])
    return call(
        finish_body,
        jax.ShapeDtypeStruct(base.shape, BF),
        grid=(blocks,),
        in_specs=[shift, local, local] + ([] if before is None else [ANY]),
        out_specs=shift,
        aliases=None if before is None else {3: 0},
        flops=2 * size * width,
        moved=10 * size * width,
    )(*arrays)


def per_device(inputs, output_gradient, frozen_key_weight, adapter_down_factors, adapter_up_factors,
               token_adapter_index, gates):
    count, width = inputs.shape
    out_width = output_gradient.shape[1]
    size = lax.axis_size("dp")
    shares = lax.axis_size("mp")
    local, rank = adapter_down_factors.shape[:2]
    total = local * rank
    d = lax.axis_index("dp")
    odd = d % 2
    half = count // CHUNKS
    down = adapter_down_factors.reshape(total, width)
    up = adapter_up_factors.reshape(total, out_width)
    pairs_a = [p for i in range(0, size - 1, 2) for p in ((i, i + 1), (i + 1, i))]
    pairs_b = [p for i in range(1, size - 1, 2) for p in ((i, i + 1), (i + 1, i))]
    i32 = jnp.int32

    block = pack_rows(token_adapter_index.T, gates.T, output_gradient)
    blocks = [block] + [
        lax.ppermute(block, "dp", [(i, (i + s) % size) for i in range(size)]) for s in range(1, size)
    ]
    full_out = lax.all_gather(output_gradient, "mp", axis=1, tiled=True)

    def exchange(part):
        if shares > 4:
            return [lax.psum(part, "mp")]
        return [part] + [
            lax.ppermute(part, "mp", [(i, (i + s) % shares) for i in range(shares)])
            for s in range(1, shares)
        ]

    base_id = (d * local).astype(i32).reshape(1)
    part_out, aux = project_out(base_id, up, blocks, count, rank)
    parts_out = exchange(part_out)

    ahead = d < (size + 1) // 2
    order = jnp.where(ahead, jnp.arange(1, size), jnp.arange(size - 1, 0, -1)).astype(i32)
    order = jnp.concatenate([order, jnp.zeros((1,), i32)])
    near = adapter_rows(order[:1], parts_out, aux, down, rank)
    far = adapter_rows(order[1:], parts_out, aux, down, rank)

    frozen = lax.dot_general(full_out, frozen_key_weight, NT, preferred_element_type=F32)
    frozen = frozen + far[size - 2].astype(F32)

    def arrival(j, a):
        left = (odd == 1) if a else (odd == 0)
        slot = jnp.where(left, j + 1, size - 1 - j)
        valid = jnp.where(left, d >= j + 1, d + j + 1 <= size - 1)
        return [valid.astype(i32), slot.astype(i32)]

    def departure(j, a):
        right = (odd == 0) if a else (odd == 1)
        slot = jnp.where(right, j, size - j)
        do = jnp.where(right, j > d, j > size - 1 - d)
        place = jnp.where(ahead, slot - 1, size - 1 - slot)
        return [do.astype(i32), place.astype(i32)]

    zero = jnp.zeros((), i32)
    low = jnp.zeros((size * 2 * rank, count), F32)
    low = project_in(
        jnp.stack([zero + 1, zero]), down, aux, low, [inputs], 1, rank
    )
    rows, where, plan = [inputs], [(0, 0)], [zero + 1, zero]
    send = [[inputs[c * half : (c + 1) * half]] * 2 for c in range(CHUNKS)]
    result = None
    for j in range(size):
        got = []
        for c in range(CHUNKS):
            to_a, to_b = send[c]
            if j > 0:
                steps = jnp.stack(departure(j, True) + departure(j, False) + [zero + c * half])
                to_a, to_b = ring_add(steps, to_a, to_b, near, far)
                rows += [to_b, to_a]
                where += [(2 * j - 1, c * half), (2 * j, c * half)]
            got.append((lax.ppermute(to_a, "dp", pairs_a), lax.ppermute(to_b, "dp", pairs_b)))
            send[c] = [got[c][1], got[c][0]]
        if j > 0:
            steps = arrival(j - 1, True) + arrival(j - 1, False)
            plan += steps
            last = rows[-2 * CHUNKS :]
            low = project_in(
                jnp.stack(steps), down, aux, low, last[0::2] + last[1::2], CHUNKS, rank
            )
        if j == size - 1:
            for c in range(CHUNKS):
                result = finish(frozen, got[c][0], got[c][1], c, result)

    parts_in = exchange(low)
    down_gradient = grad_down(jnp.stack(plan), parts_out, aux, rows, where, total, rank)
    up_gradient, *gate_rows = grad_up(parts_in, parts_out, aux, blocks, total, rank)
    gate_sum = gate_rows[0].astype(F32)
    for s in range(1, size):
        gate_sum = gate_sum + lax.ppermute(
            gate_rows[s], "dp", [(i, (i - s) % size) for i in range(size)]
        ).astype(F32)
    return (
        result,
        gate_sum.astype(BF).T,
        down_gradient.reshape(local, rank, width),
        up_gradient.reshape(local, rank, out_width),
    )


def solution(mesh):
    in_specs = (
        P(("groups", "dp"), "mp"),
        P(("groups", "dp"), "mp"),
        P("mp", None),
        P("dp", None, "mp"),
        P("dp", None, "mp"),
        P(("groups", "dp"), None),
        P(("groups", "dp"), None),
    )
    out_specs = (
        P(("groups", "dp"), "mp"),
        P(("groups", "dp"), None),
        P(("groups", "dp"), None, "mp"),
        P(("groups", "dp"), None, "mp"),
    )
    return jax.shard_map(
        per_device, mesh=mesh, in_specs=in_specs, out_specs=out_specs, check_vma=False
    )
```

```python
import functools

import jax
import jax.numpy as jnp
from jax import lax
from jax.experimental import pallas as pl
from jax.experimental.pallas import tpu as pltpu
from jax.sharding import PartitionSpec as P

BF = jnp.bfloat16
F32 = jnp.float32
CHUNKS = 2
NT = (((1,), (1,)), ((), ()))
ANY = pl.BlockSpec(memory_space=pl.ANY)
COST = 0.02


def call(body, out_shape, *, grid=None, in_specs=None, out_specs=None, scratch=(), prefetch=0,
         aliases=None, flops=0, moved=0, vmem=28, after=(), cost=COST):
    steps = len(grid) if grid else 0
    taken = prefetch + len(in_specs)
    skipped = len(after)

    def ordered(*refs):
        body(*refs[:taken], *refs[taken + skipped :])

    call_it = pl.pallas_call(
        ordered,
        out_shape=out_shape,
        grid_spec=pltpu.PrefetchScalarGridSpec(
            num_scalar_prefetch=prefetch,
            grid=grid or (1,),
            in_specs=list(in_specs) + [ANY] * skipped,
            out_specs=out_specs,
            scratch_shapes=list(scratch),
        ),
        input_output_aliases=aliases or {},
        compiler_params=pltpu.CompilerParams(
            vmem_limit_bytes=vmem << 20, dimension_semantics=("arbitrary",) * max(steps, 1)
        ),
        cost_estimate=pl.CostEstimate(
            flops=int(flops * cost), bytes_accessed=int(moved * cost), transcendentals=0
        ),
    )
    return lambda *arrays: call_it(*arrays, *after)


def whole(shape):
    return pl.BlockSpec(shape, lambda *_: (0,) * len(shape))


def arrival(d, size, j, a):
    if j < 0:
        return d >= 0, 0 * d
    left = d % 2 == (1 if a else 0)
    slot = jnp.where(left, j + 1, size - 1 - j)
    valid = jnp.where(left, d >= j + 1, d + j + 1 <= size - 1)
    return valid, slot


def departure(d, size, j, a):
    right = d % 2 == (0 if a else 1)
    slot = jnp.where(right, j, size - j)
    do = jnp.where(right, j > d, j > size - 1 - d)
    return do, slot


def place_of(d, size, slot):
    return jnp.where(d < (size + 1) // 2, jnp.where(slot == 0, size - 1, slot - 1), size - 1 - slot)


def slot_at(d, size, place):
    if place == size - 1:
        return 0 * d
    return jnp.where(d < (size + 1) // 2, place + 1, size - 1 - place)


def pack_body(local, pos_ref, index_ref, gate_ref, rows_ref, out_ref, aux_ref):
    count, width = rows_ref.shape
    out_ref[:count, :] = rows_ref[...]
    index = index_ref[...]
    gate = gate_ref[...].astype(F32)
    high, low = (index >> 4).astype(F32), (index & 15).astype(F32)
    pieces = []
    for vector in (high, low, gate):
        for slot in range(2):
            for part in range(count // width):
                pieces.append(vector[slot : slot + 1, part * width : (part + 1) * width])
    extra = out_ref.shape[0] - count
    if extra > len(pieces):
        pieces.append(jnp.zeros((extra - len(pieces), width), F32))
    out_ref[count:, :] = jnp.concatenate(pieces, axis=0).astype(BF)
    aux_ref[...] = jnp.concatenate(
        [(index - pos_ref[0] * local).astype(F32), gate, jnp.zeros((4, count), F32)], axis=0
    )


def pack_rows(pos, index, gate, rows, local):
    count, width = rows.shape
    extra = -(-6 * (count // width) // 16) * 16
    shape = (count + extra, width)
    return call(
        functools.partial(pack_body, local),
        [jax.ShapeDtypeStruct(shape, BF), jax.ShapeDtypeStruct((8, count), F32)],
        in_specs=[whole(index.shape), whole(gate.shape), whole(rows.shape)],
        out_specs=[whole(shape), whole((8, count))],
        prefetch=1,
        moved=4 * count * width,
        vmem=60,
    )(pos, index, gate, rows)


def pin_body(in_ref, out_ref):
    pass


def pin(array, after):
    return call(
        pin_body,
        jax.ShapeDtypeStruct(array.shape, array.dtype),
        in_specs=[ANY],
        out_specs=ANY,
        aliases={0: 0},
        after=after,
    )(array)


def unpack_extra(block, count, width, base):
    per = count // width
    vectors = []
    for v in range(6):
        rows = block[v * per : (v + 1) * per, :].astype(F32)
        vectors.append(jnp.concatenate([rows[q : q + 1, :] for q in range(per)], axis=1))
    ids = [vectors[k] * 16.0 + vectors[2 + k] - base for k in range(2)]
    return jnp.concatenate(ids + vectors[4:6] + [jnp.zeros((4, count), F32)], axis=0)


def pick(product, ids, first, rank, kept):
    kept = list(kept)
    for a in range(product.shape[0] // rank):
        rows = product[a * rank : (a + 1) * rank, :]
        here = (first + a).astype(F32) if hasattr(first, "astype") else float(first + a)
        for k in range(2):
            kept[k] = jnp.where(ids[k : k + 1, :] == here, rows, kept[k])
    return kept


def project_out_body(rank, pos_ref, up_ref, *refs):
    blocks, (part_ref, aux_ref) = refs[:-2], refs[-2:]
    count = part_ref.shape[1]
    width = up_ref.shape[1]
    total = up_ref.shape[0]
    step = min(1024, total)
    base = (pos_ref[0] * (total // rank)).astype(F32)
    for s, block in enumerate(blocks):
        aux = unpack_extra(block[count:, :], count, width, base)
        aux_ref[8 * s : 8 * s + 8, :] = aux
        ids = aux[0:2, :]

        def body(b, kept):
            product = lax.dot_general(
                up_ref[pl.ds(pl.multiple_of(b * step, step), step), :], block[:count, :], NT,
                preferred_element_type=F32,
            )
            return tuple(pick(product, ids, b * (step // rank), rank, kept))

        zero = jnp.zeros((rank, count), F32)
        kept = lax.fori_loop(0, total // step, body, (zero, zero))
        part_ref[2 * rank * s : 2 * rank * s + rank, :] = kept[0]
        part_ref[2 * rank * s + rank : 2 * rank * (s + 1), :] = kept[1]


def project_out(pos, up, blocks, count, rank, after):
    slots = len(blocks)
    total, width = up.shape
    shapes = [(slots * 2 * rank, count), (slots * 8, count)]
    return call(
        functools.partial(project_out_body, rank),
        [jax.ShapeDtypeStruct(s, F32) for s in shapes],
        in_specs=[whole(up.shape)] + [whole(b.shape) for b in blocks],
        out_specs=[whole(s) for s in shapes],
        prefetch=1,
        flops=2 * slots * count * total * width,
        moved=2 * (slots * count * width + total * width),
        cost=5,
        after=after,
    )(pos, up, *blocks)


def project_in_body(rank, chunks, size, step_index, pos_ref, down_ref, aux_ref, before_ref, *refs):
    rows, (out_ref, kept_ref) = refs[:-2], refs[-2:]
    source, b = pl.program_id(0), pl.program_id(1)
    step = down_ref.shape[0]

    @pl.when((source == 0) & (b == 0))
    def _():
        out_ref[...] = before_ref[...]

    for s in range(len(rows) // chunks):
        valid, slot = arrival(pos_ref[0], size, step_index, s == 0)

        @pl.when((source == s) & valid)
        def _():
            @pl.when(b == 0)
            def _():
                kept_ref[...] = jnp.zeros_like(kept_ref)

            at = 0
            for c in range(chunks):
                ref = rows[s * chunks + c]
                count = ref.shape[0]
                ids = aux_ref[pl.ds(pl.multiple_of(slot * 8, 8), 8), at : at + count]
                product = lax.dot_general(down_ref[...], ref[...], NT, preferred_element_type=F32)
                kept = [kept_ref[:rank, at : at + count], kept_ref[rank:, at : at + count]]
                kept = pick(product, ids, b * (step // rank), rank, kept)
                kept_ref[:rank, at : at + count] = kept[0]
                kept_ref[rank:, at : at + count] = kept[1]
                at += count

            @pl.when(b == pl.num_programs(1) - 1)
            def _():
                out_ref[pl.ds(pl.multiple_of(slot * 2 * rank, 2 * rank), 2 * rank), :] = kept_ref[...]


def project_in(pos, size, step_index, down, aux, before, rows, chunks, rank, after=()):
    total, width = down.shape
    sources = len(rows) // chunks
    step = min(512, total)
    count = aux.shape[1]

    def down_block(s, b, pos):
        use = b
        for i in range(sources):
            valid, _ = arrival(pos[0], size, step_index, i == 0)
            use = jnp.where((s == i) & jnp.logical_not(valid), 0, use)
        return use, 0

    return call(
        functools.partial(project_in_body, rank, chunks, size, step_index),
        jax.ShapeDtypeStruct(before.shape, F32),
        grid=(sources, total // step),
        in_specs=[pl.BlockSpec((step, width), down_block), whole(aux.shape), whole(before.shape)]
        + [whole(r.shape) for r in rows],
        out_specs=whole(before.shape),
        scratch=[pltpu.VMEM((2 * rank, count), F32)],
        prefetch=1,
        aliases={3: 0},
        flops=2 * count * total * width,
        moved=2 * (count * width + total * width),
        after=after,
    )(pos, down, aux, before, *rows)


def adapter_rows_body(rank, size, place, pos_ref, part_ref, aux_ref, down_ref, *refs):
    out_ref, spread_ref = refs[-2:]
    count = aux_ref.shape[1]
    total = down_ref.shape[0]

    @pl.when(pl.program_id(0) == 0)
    def _():
        slot = slot_at(pos_ref[0], size, place)
        low = part_ref[pl.ds(pl.multiple_of(slot * 2 * rank, 2 * rank), 2 * rank), :]
        aux = aux_ref[pl.ds(pl.multiple_of(slot * 8, 8), 8), :]
        repeat = 128 // rank
        group = (lax.broadcasted_iota(jnp.int32, (128, count), 0) // rank).astype(F32)
        keys, values = [], []
        for k in range(2):
            scaled = (aux[2 + k : 3 + k, :] * low[k * rank : (k + 1) * rank, :]).astype(BF).astype(F32)
            values.append(jnp.concatenate([scaled] * repeat, axis=0).T)
            keys.append((aux[k : k + 1, :] - group).T)
        tile = 32
        for t in range(count // tile):
            rows = slice(t * tile, (t + 1) * tile)
            key = [k[rows] for k in keys]
            value = [v[rows] for v in values]
            for g in range(total // 128):
                first = float(g * repeat)
                spread = jnp.where(key[0] == first, value[0], jnp.where(key[1] == first, value[1], 0.0))
                spread_ref[rows, g * 128 : (g + 1) * 128] = spread.astype(BF)

    rows = jnp.dot(spread_ref[...], down_ref[...], preferred_element_type=F32)
    if len(refs) == 4:
        rows = rows + lax.dot_general(refs[0][...], refs[1][...], NT, preferred_element_type=F32)
    out_ref[...] = rows.astype(out_ref.dtype)


def adapter_rows(pos, size, place, part, aux, down, rank, frozen=None, after=()):
    total, width = down.shape
    count = aux.shape[1]
    step = 256
    block = pl.BlockSpec((count, step), lambda n, pos: (0, n))
    more, specs = [], []
    if frozen is not None:
        more = list(frozen)
        specs = [whole(more[0].shape), pl.BlockSpec((step, more[1].shape[1]), lambda n, pos: (n, 0))]
    return call(
        functools.partial(adapter_rows_body, rank, size, place),
        jax.ShapeDtypeStruct((count, width), BF if frozen is None else F32),
        grid=(width // step,),
        in_specs=[
            whole(part.shape), whole(aux.shape), pl.BlockSpec((total, step), lambda n, pos: (0, n)),
        ]
        + specs,
        out_specs=block,
        scratch=[pltpu.VMEM((count, total), BF)],
        prefetch=1,
        flops=2 * count * total * width,
        moved=2 * (total * width + count * width),
        after=after,
    )(pos, part, aux, down, *more)


def add_body(size, step_index, row, pos_ref, first_ref, second_ref, near_ref, far_ref, *refs):
    outs = refs[:2]
    held, terms, in_sem, term_sem, out_sem = refs[2:]
    pieces = in_sem.shape[1]
    piece = held.shape[1] // pieces
    d = pos_ref[0]
    for i, (source, out) in enumerate(zip((first_ref, second_ref), outs)):
        do, slot = departure(d, size, step_index, i == 0)
        place = place_of(d, size, slot)

        def get(q):
            rows = pl.ds(q * piece, piece)
            return pltpu.make_async_copy(source.at[rows], held.at[i, rows], in_sem.at[i, q])

        def put(q):
            rows = pl.ds(q * piece, piece)
            return pltpu.make_async_copy(held.at[i, rows], out.at[rows], out_sem.at[i, q])

        def term(q, ref):
            rows = pl.ds(row + q * piece, piece)
            return pltpu.make_async_copy(
                ref.at[rows], terms.at[i, pl.ds(q * piece, piece)], term_sem.at[i, q]
            )

        @pl.when(do)
        def _():
            for q in range(pieces):
                get(q).start()

                @pl.when(place == 0)
                def _():
                    term(q, near_ref).start()

                @pl.when(place != 0)
                def _():
                    term(q, far_ref).start()

            for q in range(pieces):
                get(q).wait()
                term(q, near_ref).wait()
                rows = pl.ds(q * piece, piece)
                held[i, rows, :] = (held[i, rows, :].astype(F32) + terms[i, rows, :].astype(F32)).astype(BF)
                put(q).start()
            for q in range(pieces):
                put(q).wait()


def ring_add(pos, size, step_index, row, first, second, near, far, after):
    shape = first.shape
    pieces = 4 if shape[0] % 64 == 0 else 1
    return call(
        functools.partial(add_body, size, step_index, row),
        [jax.ShapeDtypeStruct(shape, BF)] * 2,
        in_specs=[ANY] * 4,
        out_specs=[ANY] * 2,
        scratch=[
            pltpu.VMEM((2,) + shape, BF),
            pltpu.VMEM((2,) + shape, BF),
            pltpu.SemaphoreType.DMA((2, pieces)),
            pltpu.SemaphoreType.DMA((2, pieces)),
            pltpu.SemaphoreType.DMA((2, pieces)),
        ],
        prefetch=1,
        aliases={1: 0, 2: 1},
        flops=2 * shape[0] * shape[1],
        moved=6 * shape[0] * shape[1],
        after=after,
    )(pos, first, second, near, far)


def spread_rows(values, ids, first, adapters):
    rows = []
    for a in range(adapters):
        here = (first + a).astype(F32)
        rows.append(
            jnp.where(ids[0:1, :] == here, values[0], jnp.where(ids[1:2, :] == here, values[1], 0.0)).astype(BF)
        )
    return jnp.concatenate(rows, axis=0)


def grad_down_body(rank, size, first, where, pos_ref, part_ref, aux_ref, *refs):
    row_refs = refs[: len(where)]
    before_ref = refs[len(where)] if len(refs) == len(where) + 6 else None
    out_ref, rows_ref, scaled_ref, ids_ref, sem = refs[-5:]
    b = pl.program_id(0)
    count = aux_ref.shape[1]
    places = rows_ref.shape[0] // count
    step = out_ref.shape[0]

    def copies(act):
        for i, (step_index, a, offset) in enumerate(where):
            height = row_refs[i].shape[0]
            valid, slot = arrival(pos_ref[0], size, step_index, a)
            place = place_of(pos_ref[0], size, slot)

            @pl.when(valid & (place >= first) & (place < first + places))
            def _():
                start = pl.multiple_of((place - first) * count + offset, height)
                act(pltpu.make_async_copy(row_refs[i], rows_ref.at[pl.ds(start, height)], sem.at[i]))

    @pl.when(b == 0)
    def _():
        copies(lambda c: c.start())
        for p in range(places):
            slot = slot_at(pos_ref[0], size, first + p)
            low = part_ref[pl.ds(pl.multiple_of(slot * 2 * rank, 2 * rank), 2 * rank), :]
            aux = aux_ref[pl.ds(pl.multiple_of(slot * 8, 8), 8), :]
            columns = slice(p * count, (p + 1) * count)
            ids_ref[:, columns] = aux
            for k in range(2):
                scaled = aux[2 + k : 3 + k, :] * low[k * rank : (k + 1) * rank, :]
                scaled_ref[k, :, columns] = scaled.astype(BF).astype(F32)
        copies(lambda c: c.wait())

    spread = []
    for p in range(places):
        columns = slice(p * count, (p + 1) * count)
        values = [scaled_ref[k, :, columns] for k in range(2)]
        spread.append(spread_rows(values, ids_ref[0:2, columns], b * (step // rank), step // rank))
    spread = spread[0] if places == 1 else jnp.concatenate(spread, axis=1)
    out = jnp.dot(spread, rows_ref[...], preferred_element_type=F32)
    if before_ref is not None:
        out = out + before_ref[...].astype(F32)
    out_ref[...] = out.astype(BF)


def grad_down(pos, size, part, aux, rows, where, first, places, total, rank, before=None, after=()):
    count = aux.shape[1]
    width = rows[0].shape[1]
    step = min(512, total)
    block = pl.BlockSpec((step, width), lambda b, pos: (b, 0))
    more = [] if before is None else [before]
    return call(
        functools.partial(grad_down_body, rank, size, first, where),
        jax.ShapeDtypeStruct((total, width), BF),
        grid=(total // step,),
        in_specs=[whole(part.shape), whole(aux.shape)] + [ANY] * len(rows) + [block] * len(more),
        out_specs=block,
        scratch=[
            pltpu.VMEM((places * count, width), BF),
            pltpu.VMEM((2, rank, places * count), F32),
            pltpu.VMEM((8, places * count), F32),
            pltpu.SemaphoreType.DMA((len(rows),)),
        ],
        prefetch=1,
        aliases={3 + len(rows): 0} if more else None,
        flops=2 * places * count * total * width,
        moved=2 * (total * width + places * count * width),
        vmem=28 if places * count * width <= 1 << 22 else 60,
        after=after,
    )(pos, part, aux, *rows, *more)


def grad_gates_body(rank, in_ref, out_ref, *gate_refs):
    for s, gate_ref in enumerate(gate_refs):
        at = slice(2 * rank * s, 2 * rank * (s + 1))
        both = in_ref[at, :] * out_ref[at, :]
        gates = [jnp.sum(both[k * rank : (k + 1) * rank, :], axis=0, keepdims=True) for k in range(2)]
        gate_ref[...] = jnp.concatenate(gates, axis=0).astype(BF)


def grad_gates(part_in, part_out, slots, rank):
    shape = part_in.shape
    return call(
        functools.partial(grad_gates_body, rank),
        [jax.ShapeDtypeStruct((2, shape[1]), BF)] * slots,
        in_specs=[whole(shape)] * 2,
        out_specs=[whole((2, shape[1]))] * slots,
        moved=8 * shape[0] * shape[1],
    )(part_in, part_out)


def grad_up_body(rank, slots, in_ref, aux_ref, *refs):
    blocks, (up_ref, rows_ref, scaled_ref) = refs[:slots], refs[slots:]
    b = pl.program_id(0)
    count = aux_ref.shape[1]
    step = up_ref.shape[0]

    @pl.when(b == 0)
    def _():
        for s in range(slots):
            rows_ref[s * count : (s + 1) * count, :] = blocks[s][:count, :]
            for k in range(2):
                at = slice(2 * rank * s + k * rank, 2 * rank * s + (k + 1) * rank)
                scaled = aux_ref[8 * s + 2 + k : 8 * s + 3 + k, :] * in_ref[at, :]
                scaled_ref[k, :, s * count : (s + 1) * count] = scaled.astype(BF).astype(F32)

    spread = []
    for s in range(slots):
        values = [scaled_ref[k, :, s * count : (s + 1) * count] for k in range(2)]
        spread.append(
            spread_rows(values, aux_ref[8 * s : 8 * s + 2, :], b * (step // rank), step // rank)
        )
    up_ref[...] = jnp.dot(
        jnp.concatenate(spread, axis=1), rows_ref[...], preferred_element_type=F32
    ).astype(BF)


def grad_up(part_in, aux, blocks, total, rank, after=()):
    count = aux.shape[1]
    slots = len(blocks)
    width = blocks[0].shape[1]
    step = min(256, total)
    arrays = [part_in, aux, *blocks]
    return call(
        functools.partial(grad_up_body, rank, slots),
        jax.ShapeDtypeStruct((total, width), BF),
        grid=(total // step,),
        in_specs=[whole(a.shape) for a in arrays],
        out_specs=pl.BlockSpec((step, width), lambda b: (b, 0)),
        scratch=[pltpu.VMEM((slots * count, width), BF), pltpu.VMEM((2, rank, slots * count), F32)],
        flops=2 * slots * count * total * width,
        moved=2 * (total * width + slots * count * width),
        after=after,
    )(*arrays)


def finish_body(base_ref, first_ref, second_ref, *refs):
    out_ref = refs[-1]
    out_ref[...] = (
        base_ref[...] + first_ref[...].astype(F32) + second_ref[...].astype(F32)
    ).astype(BF)


def finish(base, first, second, chunk, before, after):
    size, width = first.shape
    step = min(128, size)
    blocks = size // step
    shift = pl.BlockSpec((step, width), lambda i: (i + chunk * blocks, 0))
    local = pl.BlockSpec((step, width), lambda i: (i, 0))
    arrays = [base, first, second] + ([] if before is None else [before])
    return call(
        finish_body,
        jax.ShapeDtypeStruct(base.shape, BF),
        grid=(blocks,),
        in_specs=[shift, local, local] + ([] if before is None else [ANY]),
        out_specs=shift,
        aliases=None if before is None else {3: 0},
        flops=2 * size * width,
        moved=10 * size * width,
        after=after,
    )(*arrays)


def per_device(inputs, output_gradient, frozen_key_weight, adapter_down_factors, adapter_up_factors,
               token_adapter_index, gates):
    count, width = inputs.shape
    out_width = output_gradient.shape[1]
    size = lax.axis_size("dp")
    shares = lax.axis_size("mp")
    local, rank = adapter_down_factors.shape[:2]
    total = local * rank
    d = lax.axis_index("dp")
    odd = d % 2
    half = count // CHUNKS
    down = adapter_down_factors.reshape(total, width)
    up = adapter_up_factors.reshape(total, out_width)
    pairs_a = [p for i in range(0, size - 1, 2) for p in ((i, i + 1), (i + 1, i))]
    pairs_b = [p for i in range(1, size - 1, 2) for p in ((i, i + 1), (i + 1, i))]
    i32 = jnp.int32

    def exchange(part):
        bit = 1
        while bit < shares:
            part = part + lax.ppermute(part, "mp", [(i, i ^ bit) for i in range(shares)])
            bit *= 2
        return part

    pos = d.astype(jnp.int32).reshape(1)

    block, aux_own = pack_rows(pos, token_adapter_index.T, gates.T, output_gradient, local)
    blocks = [block] + [
        lax.ppermute(block, "dp", [(i, (i + s) % size) for i in range(size)]) for s in range(1, size)
    ]
    full_out = lax.all_gather(output_gradient, "mp", axis=1, tiled=True)
    low = jnp.zeros((size * 2 * rank, count), F32)
    low = project_in(pos, size, -1, down, aux_own, low, [inputs], 1, rank)

    sent = [pin(inputs[c * half : (c + 1) * half], blocks[1:]) for c in range(CHUNKS)]
    got = [[lax.ppermute(sent[c], "dp", p) for p in (pairs_a, pairs_b)] for c in range(CHUNKS)]

    part_out, aux = project_out(pos, up, blocks, count, rank, [low] + sent)
    part_out = exchange(part_out)
    near = far = adapter_rows(pos, size, 0, part_out, aux, down, rank)

    rows, where = [inputs], [(-1, True, 0)]
    early = result = None
    last = near
    for j in range(1, size):
        term = far
        for c in range(CHUNKS):
            to_a, to_b = ring_add(pos, size, j, c * half, got[c][1], got[c][0], near, term, [last])
            rows += [to_b, to_a]
            where += [(j - 1, True, c * half), (j - 1, False, c * half)]
            got[c] = [lax.ppermute(to_a, "dp", pairs_a), lax.ppermute(to_b, "dp", pairs_b)]
            last = to_a
            if c == 0:
                frozen = (full_out, frozen_key_weight) if j == size - 1 else None
                far = last = adapter_rows(pos, size, j, part_out, aux, down, rank, frozen, [to_a])
        newest = rows[-2 * CHUNKS :]
        low = last = project_in(
            pos, size, j - 1, down, aux, low, newest[0::2] + newest[1::2], CHUNKS, rank, [last]
        )
        if j == size - 2:
            early = last = grad_down(
                pos, size, part_out, aux, rows, where, 1, size - 1, total, rank, None, [last]
            )

    for c in range(CHUNKS):
        result = last = finish(far, got[c][0], got[c][1], c, result, [last])
        if c == 0:
            down_gradient = last = grad_down(
                pos, size, part_out, aux, rows, where, 0, 1, total, rank, early, [last]
            )
    part_in = exchange(pin(low, [result]))
    gate_rows = grad_gates(part_in, part_out, size, rank)
    up_gradient = grad_up(part_in, aux, blocks, total, rank, [gate_rows[0]])
    gate_sum = gate_rows[0].astype(F32)
    for s in range(1, size):
        gate_sum = gate_sum + lax.ppermute(
            gate_rows[s], "dp", [(i, (i - s) % size) for i in range(size)]
        ).astype(F32)
    return (
        result,
        gate_sum.astype(BF).T,
        down_gradient.reshape(local, rank, width),
        up_gradient.reshape(local, rank, out_width),
    )


def solution(mesh):
    in_specs = (
        P(("groups", "dp"), "mp"),
        P(("groups", "dp"), "mp"),
        P("mp", None),
        P("dp", None, "mp"),
        P("dp", None, "mp"),
        P(("groups", "dp"), None),
        P(("groups", "dp"), None),
    )
    out_specs = (
        P(("groups", "dp"), "mp"),
        P(("groups", "dp"), None),
        P(("groups", "dp"), None, "mp"),
        P(("groups", "dp"), None, "mp"),
    )
    return jax.shard_map(
        per_device, mesh=mesh, in_specs=in_specs, out_specs=out_specs, check_vma=False
    )
```

```python
import functools

import jax
import jax.numpy as jnp
from jax import lax
from jax.experimental import pallas as pl
from jax.experimental.pallas import tpu as pltpu
from jax.sharding import PartitionSpec as P

BF = jnp.bfloat16
F32 = jnp.float32
CHUNKS = 2
NT = (((1,), (1,)), ((), ()))
ANY = pl.BlockSpec(memory_space=pl.ANY)
COST = 0.02


def call(body, out_shape, *, grid=None, in_specs=None, out_specs=None, scratch=(), prefetch=0,
         aliases=None, flops=0, moved=0, vmem=16, after=(), cost=COST):
    steps = len(grid) if grid else 0
    several = isinstance(out_shape, (list, tuple))
    shapes = list(out_shape) if several else [out_shape]
    specs = list(out_specs) if several else [out_specs]
    taken = prefetch + len(in_specs)
    skipped = len(after)
    given = taken + skipped + len(shapes)

    def ordered(*refs):
        body(*refs[:taken], *refs[taken + skipped : given], *refs[given + 1 :])

    call_it = pl.pallas_call(
        ordered,
        out_shape=shapes + [jax.ShapeDtypeStruct((8, 128), F32)],
        grid_spec=pltpu.PrefetchScalarGridSpec(
            num_scalar_prefetch=prefetch,
            grid=grid or (1,),
            in_specs=list(in_specs) + [ANY] * skipped,
            out_specs=specs + [ANY],
            scratch_shapes=list(scratch),
        ),
        input_output_aliases=aliases or {},
        compiler_params=pltpu.CompilerParams(
            vmem_limit_bytes=vmem << 20, dimension_semantics=("arbitrary",) * max(steps, 1)
        ),
        cost_estimate=pl.CostEstimate(
            flops=int(flops * cost), bytes_accessed=int(moved * cost), transcendentals=0
        ),
    )
    return lambda *arrays: call_it(*arrays, *after)


def whole(shape):
    return pl.BlockSpec(shape, lambda *_: (0,) * len(shape))


def arrival(d, size, j, a):
    if j < 0:
        return d >= 0, 0 * d
    left = d % 2 == (1 if a else 0)
    slot = jnp.where(left, j + 1, size - 1 - j)
    valid = jnp.where(left, d >= j + 1, d + j + 1 <= size - 1)
    return valid, slot


def departure(d, size, j, a):
    right = d % 2 == (0 if a else 1)
    slot = jnp.where(right, j, size - j)
    do = jnp.where(right, j > d, j > size - 1 - d)
    return do, slot


def place_of(d, size, slot):
    return jnp.where(d < (size + 1) // 2, jnp.where(slot == 0, size - 1, slot - 1), size - 1 - slot)


def slot_at(d, size, place):
    if place == size - 1:
        return 0 * d
    return jnp.where(d < (size + 1) // 2, place + 1, size - 1 - place)


def pack_body(local, pos_ref, index_ref, gate_ref, rows_ref, out_ref, aux_ref):
    count, width = rows_ref.shape
    out_ref[:count, :] = rows_ref[...]
    index = index_ref[...]
    gate = gate_ref[...].astype(F32)
    high, low = (index >> 4).astype(F32), (index & 15).astype(F32)
    pieces = []
    for vector in (high, low, gate):
        for slot in range(2):
            for part in range(count // width):
                pieces.append(vector[slot : slot + 1, part * width : (part + 1) * width])
    extra = out_ref.shape[0] - count
    if extra > len(pieces):
        pieces.append(jnp.zeros((extra - len(pieces), width), F32))
    out_ref[count:, :] = jnp.concatenate(pieces, axis=0).astype(BF)
    aux_ref[...] = jnp.concatenate(
        [(index - pos_ref[0] * local).astype(F32), gate, jnp.zeros((4, count), F32)], axis=0
    )


def pack_rows(pos, index, gate, rows, local):
    count, width = rows.shape
    extra = -(-6 * (count // width) // 16) * 16
    shape = (count + extra, width)
    return call(
        functools.partial(pack_body, local),
        [jax.ShapeDtypeStruct(shape, BF), jax.ShapeDtypeStruct((8, count), F32)],
        in_specs=[whole(index.shape), whole(gate.shape), whole(rows.shape)],
        out_specs=[whole(shape), whole((8, count))],
        prefetch=1,
        moved=4 * count * width,
        vmem=60,
    )(pos, index, gate, rows)


def pin_body(in_ref, out_ref):
    pass


def pin(array, after):
    return call(
        pin_body,
        jax.ShapeDtypeStruct(array.shape, array.dtype),
        in_specs=[ANY],
        out_specs=ANY,
        aliases={0: 0},
        after=after,
    )(array)


def unpack_extra(block, count, width, base):
    per = count // width
    vectors = []
    for v in range(6):
        rows = block[v * per : (v + 1) * per, :].astype(F32)
        vectors.append(jnp.concatenate([rows[q : q + 1, :] for q in range(per)], axis=1))
    ids = [vectors[k] * 16.0 + vectors[2 + k] - base for k in range(2)]
    return jnp.concatenate(ids + vectors[4:6] + [jnp.zeros((4, count), F32)], axis=0)


def pick(product, ids, first, rank, kept):
    kept = list(kept)
    for a in range(product.shape[0] // rank):
        rows = product[a * rank : (a + 1) * rank, :]
        here = (first + a).astype(F32) if hasattr(first, "astype") else float(first + a)
        for k in range(2):
            kept[k] = jnp.where(ids[k : k + 1, :] == here, rows, kept[k])
    return kept


def project_out_body(rank, pos_ref, up_ref, *refs):
    blocks, (part_ref, aux_ref) = refs[:-2], refs[-2:]
    count = part_ref.shape[1]
    width = up_ref.shape[1]
    total = up_ref.shape[0]
    step = min(1024, total)
    base = (pos_ref[0] * (total // rank)).astype(F32)
    for s, block in enumerate(blocks):
        aux = unpack_extra(block[count:, :], count, width, base)
        aux_ref[8 * s : 8 * s + 8, :] = aux
        ids = aux[0:2, :]

        def body(b, kept):
            product = lax.dot_general(
                up_ref[pl.ds(pl.multiple_of(b * step, step), step), :], block[:count, :], NT,
                preferred_element_type=F32,
            )
            return tuple(pick(product, ids, b * (step // rank), rank, kept))

        zero = jnp.zeros((rank, count), F32)
        kept = lax.fori_loop(0, total // step, body, (zero, zero))
        part_ref[2 * rank * s : 2 * rank * s + rank, :] = kept[0]
        part_ref[2 * rank * s + rank : 2 * rank * (s + 1), :] = kept[1]


def project_out(pos, up, blocks, count, rank, after):
    slots = len(blocks)
    total, width = up.shape
    shapes = [(slots * 2 * rank, count), (slots * 8, count)]
    return call(
        functools.partial(project_out_body, rank),
        [jax.ShapeDtypeStruct(s, F32) for s in shapes],
        in_specs=[whole(up.shape)] + [whole(b.shape) for b in blocks],
        out_specs=[whole(s) for s in shapes],
        prefetch=1,
        flops=2 * slots * count * total * width,
        moved=2 * (slots * count * width + total * width),
        cost=5,
        after=after,
    )(pos, up, *blocks)


def project_in_body(rank, chunks, size, step_index, pos_ref, down_ref, aux_ref, before_ref, *refs):
    rows, (out_ref, kept_ref) = refs[:-2], refs[-2:]
    source, b = pl.program_id(0), pl.program_id(1)
    step = down_ref.shape[0]

    @pl.when((source == 0) & (b == 0))
    def _():
        out_ref[...] = before_ref[...]

    for s in range(len(rows) // chunks):
        valid, slot = arrival(pos_ref[0], size, step_index, s == 0)

        @pl.when((source == s) & valid)
        def _():
            @pl.when(b == 0)
            def _():
                kept_ref[...] = jnp.zeros_like(kept_ref)

            at = 0
            for c in range(chunks):
                ref = rows[s * chunks + c]
                count = ref.shape[0]
                ids = aux_ref[pl.ds(pl.multiple_of(slot * 8, 8), 8), at : at + count]
                product = lax.dot_general(down_ref[...], ref[...], NT, preferred_element_type=F32)
                kept = [kept_ref[:rank, at : at + count], kept_ref[rank:, at : at + count]]
                kept = pick(product, ids, b * (step // rank), rank, kept)
                kept_ref[:rank, at : at + count] = kept[0]
                kept_ref[rank:, at : at + count] = kept[1]
                at += count

            @pl.when(b == pl.num_programs(1) - 1)
            def _():
                out_ref[pl.ds(pl.multiple_of(slot * 2 * rank, 2 * rank), 2 * rank), :] = kept_ref[...]


def project_in(pos, size, step_index, down, aux, before, rows, chunks, rank, after=()):
    total, width = down.shape
    sources = len(rows) // chunks
    step = min(512, total)
    count = aux.shape[1]

    def down_block(s, b, pos):
        use = b
        for i in range(sources):
            valid, _ = arrival(pos[0], size, step_index, i == 0)
            use = jnp.where((s == i) & jnp.logical_not(valid), 0, use)
        return use, 0

    return call(
        functools.partial(project_in_body, rank, chunks, size, step_index),
        jax.ShapeDtypeStruct(before.shape, F32),
        grid=(sources, total // step),
        in_specs=[pl.BlockSpec((step, width), down_block), whole(aux.shape), whole(before.shape)]
        + [whole(r.shape) for r in rows],
        out_specs=whole(before.shape),
        scratch=[pltpu.VMEM((2 * rank, count), F32)],
        prefetch=1,
        aliases={3: 0},
        flops=2 * count * total * width,
        moved=2 * (count * width + total * width),
        after=after,
    )(pos, down, aux, before, *rows)


def adapter_rows_body(rank, size, place, pos_ref, part_ref, aux_ref, down_ref, *refs):
    out_ref, spread_ref = refs[-2:]
    count = aux_ref.shape[1]
    total = down_ref.shape[0]

    @pl.when(pl.program_id(0) == 0)
    def _():
        slot = slot_at(pos_ref[0], size, place)
        low = part_ref[pl.ds(pl.multiple_of(slot * 2 * rank, 2 * rank), 2 * rank), :]
        aux = aux_ref[pl.ds(pl.multiple_of(slot * 8, 8), 8), :]
        repeat = 128 // rank
        group = (lax.broadcasted_iota(jnp.int32, (128, count), 0) // rank).astype(F32)
        keys, values = [], []
        for k in range(2):
            scaled = (aux[2 + k : 3 + k, :] * low[k * rank : (k + 1) * rank, :]).astype(BF).astype(F32)
            values.append(jnp.concatenate([scaled] * repeat, axis=0).T)
            keys.append((aux[k : k + 1, :] - group).T)
        tile = 32
        for t in range(count // tile):
            rows = slice(t * tile, (t + 1) * tile)
            key = [k[rows] for k in keys]
            value = [v[rows] for v in values]
            for g in range(total // 128):
                first = float(g * repeat)
                spread = jnp.where(key[0] == first, value[0], jnp.where(key[1] == first, value[1], 0.0))
                spread_ref[rows, g * 128 : (g + 1) * 128] = spread.astype(BF)

    rows = jnp.dot(spread_ref[...], down_ref[...], preferred_element_type=F32)
    if len(refs) == 4:
        rows = rows + lax.dot_general(refs[0][...], refs[1][...], NT, preferred_element_type=F32)
    out_ref[...] = rows.astype(out_ref.dtype)


def adapter_rows(pos, size, place, part, aux, down, rank, frozen=None, after=()):
    total, width = down.shape
    count = aux.shape[1]
    step = 256
    block = pl.BlockSpec((count, step), lambda n, pos: (0, n))
    more, specs = [], []
    if frozen is not None:
        more = list(frozen)
        specs = [whole(more[0].shape), pl.BlockSpec((step, more[1].shape[1]), lambda n, pos: (n, 0))]
    return call(
        functools.partial(adapter_rows_body, rank, size, place),
        jax.ShapeDtypeStruct((count, width), BF if frozen is None else F32),
        grid=(width // step,),
        in_specs=[
            whole(part.shape), whole(aux.shape), pl.BlockSpec((total, step), lambda n, pos: (0, n)),
        ]
        + specs,
        out_specs=block,
        scratch=[pltpu.VMEM((count, total), BF)],
        prefetch=1,
        flops=2 * count * total * width,
        moved=2 * (total * width + count * width),
        after=after,
    )(pos, part, aux, down, *more)


def add_body(size, step_index, row, pos_ref, first_ref, second_ref, near_ref, far_ref, *refs):
    outs = refs[:2]
    held, terms, in_sem, term_sem, out_sem = refs[2:]
    pieces = in_sem.shape[1]
    piece = held.shape[1] // pieces
    d = pos_ref[0]
    for i, (source, out) in enumerate(zip((first_ref, second_ref), outs)):
        do, slot = departure(d, size, step_index, i == 0)
        place = place_of(d, size, slot)

        def get(q):
            rows = pl.ds(q * piece, piece)
            return pltpu.make_async_copy(source.at[rows], held.at[i, rows], in_sem.at[i, q])

        def put(q):
            rows = pl.ds(q * piece, piece)
            return pltpu.make_async_copy(held.at[i, rows], out.at[rows], out_sem.at[i, q])

        def term(q, ref):
            rows = pl.ds(row + q * piece, piece)
            return pltpu.make_async_copy(
                ref.at[rows], terms.at[i, pl.ds(q * piece, piece)], term_sem.at[i, q]
            )

        @pl.when(do)
        def _():
            for q in range(pieces):
                get(q).start()

                @pl.when(place == 0)
                def _():
                    term(q, near_ref).start()

                @pl.when(place != 0)
                def _():
                    term(q, far_ref).start()

            for q in range(pieces):
                get(q).wait()
                term(q, near_ref).wait()
                rows = pl.ds(q * piece, piece)
                held[i, rows, :] = (held[i, rows, :].astype(F32) + terms[i, rows, :].astype(F32)).astype(BF)
                put(q).start()
            for q in range(pieces):
                put(q).wait()


def ring_add(pos, size, step_index, row, first, second, near, far, after):
    shape = first.shape
    pieces = 4 if shape[0] % 64 == 0 else 1
    return call(
        functools.partial(add_body, size, step_index, row),
        [jax.ShapeDtypeStruct(shape, BF)] * 2,
        in_specs=[ANY] * 4,
        out_specs=[ANY] * 2,
        scratch=[
            pltpu.VMEM((2,) + shape, BF),
            pltpu.VMEM((2,) + shape, BF),
            pltpu.SemaphoreType.DMA((2, pieces)),
            pltpu.SemaphoreType.DMA((2, pieces)),
            pltpu.SemaphoreType.DMA((2, pieces)),
        ],
        prefetch=1,
        aliases={1: 0, 2: 1},
        flops=2 * shape[0] * shape[1],
        moved=6 * shape[0] * shape[1],
        after=after,
    )(pos, first, second, near, far)


def spread_rows(values, ids, first, adapters):
    rows = []
    for a in range(adapters):
        here = (first + a).astype(F32)
        rows.append(
            jnp.where(ids[0:1, :] == here, values[0], jnp.where(ids[1:2, :] == here, values[1], 0.0)).astype(BF)
        )
    return jnp.concatenate(rows, axis=0)


def grad_down_body(rank, size, first, where, pos_ref, part_ref, aux_ref, *refs):
    row_refs = refs[: len(where)]
    before_ref = refs[len(where)] if len(refs) == len(where) + 6 else None
    out_ref, rows_ref, scaled_ref, ids_ref, sem = refs[-5:]
    b = pl.program_id(0)
    count = aux_ref.shape[1]
    places = rows_ref.shape[0] // count
    step = out_ref.shape[0]

    def copies(act):
        for i, (step_index, a, offset) in enumerate(where):
            height = row_refs[i].shape[0]
            valid, slot = arrival(pos_ref[0], size, step_index, a)
            place = place_of(pos_ref[0], size, slot)

            @pl.when(valid & (place >= first) & (place < first + places))
            def _():
                start = pl.multiple_of((place - first) * count + offset, height)
                act(pltpu.make_async_copy(row_refs[i], rows_ref.at[pl.ds(start, height)], sem.at[i]))

    @pl.when(b == 0)
    def _():
        copies(lambda c: c.start())
        for p in range(places):
            slot = slot_at(pos_ref[0], size, first + p)
            low = part_ref[pl.ds(pl.multiple_of(slot * 2 * rank, 2 * rank), 2 * rank), :]
            aux = aux_ref[pl.ds(pl.multiple_of(slot * 8, 8), 8), :]
            columns = slice(p * count, (p + 1) * count)
            ids_ref[:, columns] = aux
            for k in range(2):
                scaled = aux[2 + k : 3 + k, :] * low[k * rank : (k + 1) * rank, :]
                scaled_ref[k, :, columns] = scaled.astype(BF).astype(F32)
        copies(lambda c: c.wait())

    spread = []
    for p in range(places):
        columns = slice(p * count, (p + 1) * count)
        values = [scaled_ref[k, :, columns] for k in range(2)]
        spread.append(spread_rows(values, ids_ref[0:2, columns], b * (step // rank), step // rank))
    spread = spread[0] if places == 1 else jnp.concatenate(spread, axis=1)
    out = jnp.dot(spread, rows_ref[...], preferred_element_type=F32)
    if before_ref is not None:
        out = out + before_ref[...].astype(F32)
    out_ref[...] = out.astype(BF)


def grad_down(pos, size, part, aux, rows, where, first, places, total, rank, before=None, after=()):
    count = aux.shape[1]
    width = rows[0].shape[1]
    step = min(512, total)
    block = pl.BlockSpec((step, width), lambda b, pos: (b, 0))
    more = [] if before is None else [before]
    return call(
        functools.partial(grad_down_body, rank, size, first, where),
        jax.ShapeDtypeStruct((total, width), BF),
        grid=(total // step,),
        in_specs=[whole(part.shape), whole(aux.shape)] + [ANY] * len(rows) + [block] * len(more),
        out_specs=block,
        scratch=[
            pltpu.VMEM((places * count, width), BF),
            pltpu.VMEM((2, rank, places * count), F32),
            pltpu.VMEM((8, places * count), F32),
            pltpu.SemaphoreType.DMA((len(rows),)),
        ],
        prefetch=1,
        aliases={3 + len(rows): 0} if more else None,
        flops=2 * places * count * total * width,
        moved=2 * (total * width + places * count * width),
        vmem=24 if places * count * width <= 1 << 22 else 60,
        after=after,
    )(pos, part, aux, *rows, *more)


def grad_gates_body(rank, in_ref, out_ref, *gate_refs):
    for s, gate_ref in enumerate(gate_refs):
        at = slice(2 * rank * s, 2 * rank * (s + 1))
        both = in_ref[at, :] * out_ref[at, :]
        gates = [jnp.sum(both[k * rank : (k + 1) * rank, :], axis=0, keepdims=True) for k in range(2)]
        gate_ref[...] = jnp.concatenate(gates, axis=0).astype(BF)


def grad_gates(part_in, part_out, slots, rank, after):
    shape = part_in.shape
    return call(
        functools.partial(grad_gates_body, rank),
        [jax.ShapeDtypeStruct((2, shape[1]), BF)] * slots,
        in_specs=[whole(shape)] * 2,
        out_specs=[whole((2, shape[1]))] * slots,
        moved=8 * shape[0] * shape[1],
        after=after,
    )(part_in, part_out)


def grad_up_body(rank, slots, in_ref, aux_ref, *refs):
    blocks, (up_ref, rows_ref, scaled_ref) = refs[:slots], refs[slots:]
    b = pl.program_id(0)
    count = aux_ref.shape[1]
    step = up_ref.shape[0]

    @pl.when(b == 0)
    def _():
        for s in range(slots):
            rows_ref[s * count : (s + 1) * count, :] = blocks[s][:count, :]
            for k in range(2):
                at = slice(2 * rank * s + k * rank, 2 * rank * s + (k + 1) * rank)
                scaled = aux_ref[8 * s + 2 + k : 8 * s + 3 + k, :] * in_ref[at, :]
                scaled_ref[k, :, s * count : (s + 1) * count] = scaled.astype(BF).astype(F32)

    spread = []
    for s in range(slots):
        values = [scaled_ref[k, :, s * count : (s + 1) * count] for k in range(2)]
        spread.append(
            spread_rows(values, aux_ref[8 * s : 8 * s + 2, :], b * (step // rank), step // rank)
        )
    up_ref[...] = jnp.dot(
        jnp.concatenate(spread, axis=1), rows_ref[...], preferred_element_type=F32
    ).astype(BF)


def grad_up(part_in, aux, blocks, total, rank, after=()):
    count = aux.shape[1]
    slots = len(blocks)
    width = blocks[0].shape[1]
    step = min(256, total)
    arrays = [part_in, aux, *blocks]
    return call(
        functools.partial(grad_up_body, rank, slots),
        jax.ShapeDtypeStruct((total, width), BF),
        grid=(total // step,),
        in_specs=[whole(a.shape) for a in arrays],
        out_specs=pl.BlockSpec((step, width), lambda b: (b, 0)),
        scratch=[pltpu.VMEM((slots * count, width), BF), pltpu.VMEM((2, rank, slots * count), F32)],
        flops=2 * slots * count * total * width,
        moved=2 * (total * width + slots * count * width),
        after=after,
    )(*arrays)


def finish_body(base_ref, first_ref, second_ref, *refs):
    out_ref = refs[-1]
    out_ref[...] = (
        base_ref[...] + first_ref[...].astype(F32) + second_ref[...].astype(F32)
    ).astype(BF)


def finish(base, first, second, chunk, before, after):
    size, width = first.shape
    step = min(128, size)
    blocks = size // step
    shift = pl.BlockSpec((step, width), lambda i: (i + chunk * blocks, 0))
    local = pl.BlockSpec((step, width), lambda i: (i, 0))
    arrays = [base, first, second] + ([] if before is None else [before])
    return call(
        finish_body,
        jax.ShapeDtypeStruct(base.shape, BF),
        grid=(blocks,),
        in_specs=[shift, local, local] + ([] if before is None else [ANY]),
        out_specs=shift,
        aliases=None if before is None else {3: 0},
        flops=2 * size * width,
        moved=10 * size * width,
        after=after,
    )(*arrays)


def per_device(inputs, output_gradient, frozen_key_weight, adapter_down_factors, adapter_up_factors,
               token_adapter_index, gates):
    count, width = inputs.shape
    out_width = output_gradient.shape[1]
    size = lax.axis_size("dp")
    shares = lax.axis_size("mp")
    local, rank = adapter_down_factors.shape[:2]
    total = local * rank
    d = lax.axis_index("dp")
    odd = d % 2
    half = count // CHUNKS
    down = adapter_down_factors.reshape(total, width)
    up = adapter_up_factors.reshape(total, out_width)
    pairs_a = [p for i in range(0, size - 1, 2) for p in ((i, i + 1), (i + 1, i))]
    pairs_b = [p for i in range(1, size - 1, 2) for p in ((i, i + 1), (i + 1, i))]
    i32 = jnp.int32

    def exchange(part):
        bit = 1
        while bit < shares:
            part = part + lax.ppermute(part, "mp", [(i, i ^ bit) for i in range(shares)])
            bit *= 2
        return part

    pos = d.astype(jnp.int32).reshape(1)

    block, aux_own, _ = pack_rows(pos, token_adapter_index.T, gates.T, output_gradient, local)
    blocks = [block] + [
        lax.ppermute(block, "dp", [(i, (i + s) % size) for i in range(size)]) for s in range(1, size)
    ]
    full_out = lax.all_gather(output_gradient, "mp", axis=1, tiled=True)
    low = jnp.zeros((size * 2 * rank, count), F32)
    low, token = project_in(pos, size, -1, down, aux_own, low, [inputs], 1, rank)

    sent, tokens = zip(*[pin(inputs[c * half : (c + 1) * half], blocks[1:]) for c in range(CHUNKS)])
    got = [[lax.ppermute(sent[c], "dp", p) for p in (pairs_a, pairs_b)] for c in range(CHUNKS)]

    part_out, aux, _ = project_out(pos, up, blocks, count, rank, [token, *tokens])
    part_out = exchange(part_out)
    near, token = adapter_rows(pos, size, 0, part_out, aux, down, rank)
    far = near

    rows, where = [inputs], [(-1, True, 0)]
    early = result = None
    for j in range(1, size):
        term = far
        for c in range(CHUNKS):
            to_a, to_b, token = ring_add(
                pos, size, j, c * half, got[c][1], got[c][0], near, term, [token]
            )
            rows += [to_b, to_a]
            where += [(j - 1, True, c * half), (j - 1, False, c * half)]
            got[c] = [lax.ppermute(to_a, "dp", pairs_a), lax.ppermute(to_b, "dp", pairs_b)]
            if c == 0:
                frozen = (full_out, frozen_key_weight) if j == size - 1 else None
                far, token = adapter_rows(pos, size, j, part_out, aux, down, rank, frozen, [token])
        newest = rows[-2 * CHUNKS :]
        low, token = project_in(
            pos, size, j - 1, down, aux, low, newest[0::2] + newest[1::2], CHUNKS, rank, [token]
        )
        if j == size - 2:
            early, token = grad_down(
                pos, size, part_out, aux, rows, where, 1, size - 1, total, rank, None, [token]
            )

    result, token = finish(far, got[0][0], got[0][1], 0, None, [token])
    low, _ = pin(low, [token])
    part_in = exchange(low)
    down_gradient, token = grad_down(
        pos, size, part_out, aux, rows, where, 0, 1, total, rank, early, [token]
    )
    for c in range(1, CHUNKS):
        result, token = finish(far, got[c][0], got[c][1], c, result, [token])
    *gate_rows, token = grad_gates(part_in, part_out, size, rank, [token])
    up_gradient, _ = grad_up(part_in, aux, blocks, total, rank, [token])
    gate_sum = gate_rows[0].astype(F32)
    for s in range(1, size):
        gate_sum = gate_sum + lax.ppermute(
            gate_rows[s], "dp", [(i, (i - s) % size) for i in range(size)]
        ).astype(F32)
    return (
        result,
        gate_sum.astype(BF).T,
        down_gradient.reshape(local, rank, width),
        up_gradient.reshape(local, rank, out_width),
    )


def solution(mesh):
    in_specs = (
        P(("groups", "dp"), "mp"),
        P(("groups", "dp"), "mp"),
        P("mp", None),
        P("dp", None, "mp"),
        P("dp", None, "mp"),
        P(("groups", "dp"), None),
        P(("groups", "dp"), None),
    )
    out_specs = (
        P(("groups", "dp"), "mp"),
        P(("groups", "dp"), None),
        P(("groups", "dp"), None, "mp"),
        P(("groups", "dp"), None, "mp"),
    )
    return jax.shard_map(
        per_device, mesh=mesh, in_specs=in_specs, out_specs=out_specs, check_vma=False
    )
```

```python
import functools

import jax
import jax.numpy as jnp
from jax import lax
from jax.experimental import pallas as pl
from jax.experimental.pallas import tpu as pltpu
from jax.sharding import PartitionSpec as P

BF = jnp.bfloat16
F32 = jnp.float32
CHUNKS = 2
NT = (((1,), (1,)), ((), ()))
ANY = pl.BlockSpec(memory_space=pl.ANY)
COST = 0.02
STEP_IN = 1024
STEP_ROWS = 512
STEP_DOWN = 1024
STEP_UP = 512


def call(body, out_shape, *, grid=None, in_specs=None, out_specs=None, scratch=(), prefetch=0,
         aliases=None, flops=0, moved=0, vmem=16, after=(), cost=COST):
    steps = len(grid) if grid else 0
    several = isinstance(out_shape, (list, tuple))
    shapes = list(out_shape) if several else [out_shape]
    specs = list(out_specs) if several else [out_specs]
    taken = prefetch + len(in_specs)
    skipped = len(after)
    given = taken + skipped + len(shapes)

    def ordered(*refs):
        body(*refs[:taken], *refs[taken + skipped : given], *refs[given + 1 :])

    call_it = pl.pallas_call(
        ordered,
        out_shape=shapes + [jax.ShapeDtypeStruct((8, 128), F32)],
        grid_spec=pltpu.PrefetchScalarGridSpec(
            num_scalar_prefetch=prefetch,
            grid=grid or (1,),
            in_specs=list(in_specs) + [ANY] * skipped,
            out_specs=specs + [ANY],
            scratch_shapes=list(scratch),
        ),
        input_output_aliases=aliases or {},
        compiler_params=pltpu.CompilerParams(
            vmem_limit_bytes=vmem << 20, dimension_semantics=("arbitrary",) * max(steps, 1)
        ),
        cost_estimate=pl.CostEstimate(
            flops=int(flops * cost), bytes_accessed=int(moved * cost), transcendentals=0
        ),
    )
    return lambda *arrays: call_it(*arrays, *after)


def whole(shape):
    return pl.BlockSpec(shape, lambda *_: (0,) * len(shape))


def arrival(d, size, j, a):
    if j < 0:
        return d >= 0, 0 * d
    left = d % 2 == (1 if a else 0)
    slot = jnp.where(left, j + 1, size - 1 - j)
    valid = jnp.where(left, d >= j + 1, d + j + 1 <= size - 1)
    return valid, slot


def departure(d, size, j, a):
    right = d % 2 == (0 if a else 1)
    slot = jnp.where(right, j, size - j)
    do = jnp.where(right, j > d, j > size - 1 - d)
    return do, slot


def place_of(d, size, slot):
    return jnp.where(d < (size + 1) // 2, jnp.where(slot == 0, size - 1, slot - 1), size - 1 - slot)


def slot_at(d, size, place):
    if place == size - 1:
        return 0 * d
    return jnp.where(d < (size + 1) // 2, place + 1, size - 1 - place)


def pack_body(local, pos_ref, index_ref, gate_ref, rows_ref, out_ref, aux_ref):
    count, width = rows_ref.shape
    out_ref[:count, :] = rows_ref[...]
    index = index_ref[...]
    gate = gate_ref[...].astype(F32)
    high, low = (index >> 4).astype(F32), (index & 15).astype(F32)
    pieces = []
    for vector in (high, low, gate):
        for slot in range(2):
            for part in range(count // width):
                pieces.append(vector[slot : slot + 1, part * width : (part + 1) * width])
    extra = out_ref.shape[0] - count
    if extra > len(pieces):
        pieces.append(jnp.zeros((extra - len(pieces), width), F32))
    out_ref[count:, :] = jnp.concatenate(pieces, axis=0).astype(BF)
    aux_ref[...] = jnp.concatenate(
        [(index - pos_ref[0] * local).astype(F32), gate, jnp.zeros((4, count), F32)], axis=0
    )


def pack_rows(pos, index, gate, rows, local):
    count, width = rows.shape
    extra = -(-6 * (count // width) // 16) * 16
    shape = (count + extra, width)
    return call(
        functools.partial(pack_body, local),
        [jax.ShapeDtypeStruct(shape, BF), jax.ShapeDtypeStruct((8, count), F32)],
        in_specs=[whole(index.shape), whole(gate.shape), whole(rows.shape)],
        out_specs=[whole(shape), whole((8, count))],
        prefetch=1,
        moved=4 * count * width,
        vmem=60,
    )(pos, index, gate, rows)


def pin_body(in_ref, out_ref):
    pass


def pin(array, after):
    return call(
        pin_body,
        jax.ShapeDtypeStruct(array.shape, array.dtype),
        in_specs=[ANY],
        out_specs=ANY,
        aliases={0: 0},
        after=after,
    )(array)


def unpack_extra(block, count, width, base):
    per = count // width
    vectors = []
    for v in range(6):
        rows = block[v * per : (v + 1) * per, :].astype(F32)
        vectors.append(jnp.concatenate([rows[q : q + 1, :] for q in range(per)], axis=1))
    ids = [vectors[k] * 16.0 + vectors[2 + k] - base for k in range(2)]
    return jnp.concatenate(ids + vectors[4:6] + [jnp.zeros((4, count), F32)], axis=0)


def pick(product, ids, first, rank, kept):
    kept = list(kept)
    for a in range(product.shape[0] // rank):
        rows = product[a * rank : (a + 1) * rank, :]
        here = (first + a).astype(F32) if hasattr(first, "astype") else float(first + a)
        for k in range(2):
            kept[k] = jnp.where(ids[k : k + 1, :] == here, rows, kept[k])
    return kept


def project_out_body(rank, pos_ref, up_ref, *refs):
    blocks, (part_ref, aux_ref) = refs[:-2], refs[-2:]
    count = part_ref.shape[1]
    width = up_ref.shape[1]
    total = up_ref.shape[0]
    step = min(1024, total)
    base = (pos_ref[0] * (total // rank)).astype(F32)
    for s, block in enumerate(blocks):
        aux = unpack_extra(block[count:, :], count, width, base)
        aux_ref[8 * s : 8 * s + 8, :] = aux
        ids = aux[0:2, :]

        def body(b, kept):
            product = lax.dot_general(
                up_ref[pl.ds(pl.multiple_of(b * step, step), step), :], block[:count, :], NT,
                preferred_element_type=F32,
            )
            return tuple(pick(product, ids, b * (step // rank), rank, kept))

        zero = jnp.zeros((rank, count), F32)
        kept = lax.fori_loop(0, total // step, body, (zero, zero))
        part_ref[2 * rank * s : 2 * rank * s + rank, :] = kept[0]
        part_ref[2 * rank * s + rank : 2 * rank * (s + 1), :] = kept[1]


def project_out(pos, up, blocks, count, rank, after):
    slots = len(blocks)
    total, width = up.shape
    shapes = [(slots * 2 * rank, count), (slots * 8, count)]
    return call(
        functools.partial(project_out_body, rank),
        [jax.ShapeDtypeStruct(s, F32) for s in shapes],
        in_specs=[whole(up.shape)] + [whole(b.shape) for b in blocks],
        out_specs=[whole(s) for s in shapes],
        prefetch=1,
        flops=2 * slots * count * total * width,
        moved=2 * (slots * count * width + total * width),
        cost=5,
        after=after,
    )(pos, up, *blocks)


def project_in_body(rank, chunks, size, sources, pos_ref, down_ref, aux_ref, before_ref, *refs):
    rows, (out_ref, kept_ref) = refs[:-2], refs[-2:]
    source, b = pl.program_id(0), pl.program_id(1)
    step = down_ref.shape[0]

    @pl.when((source == 0) & (b == 0))
    def _():
        out_ref[...] = before_ref[...]

    for s, (step_index, a) in enumerate(sources):
        valid, slot = arrival(pos_ref[0], size, step_index, a)

        @pl.when((source == s) & valid)
        def _():
            @pl.when(b == 0)
            def _():
                kept_ref[...] = jnp.zeros_like(kept_ref)

            at = 0
            for c in range(chunks):
                ref = rows[s * chunks + c]
                count = ref.shape[0]
                ids = aux_ref[pl.ds(pl.multiple_of(slot * 8, 8), 8), at : at + count]
                product = lax.dot_general(down_ref[...], ref[...], NT, preferred_element_type=F32)
                kept = [kept_ref[:rank, at : at + count], kept_ref[rank:, at : at + count]]
                kept = pick(product, ids, b * (step // rank), rank, kept)
                kept_ref[:rank, at : at + count] = kept[0]
                kept_ref[rank:, at : at + count] = kept[1]
                at += count

            @pl.when(b == pl.num_programs(1) - 1)
            def _():
                out_ref[pl.ds(pl.multiple_of(slot * 2 * rank, 2 * rank), 2 * rank), :] = kept_ref[...]


def project_in(pos, size, sources, down, aux, before, rows, chunks, rank, after=()):
    total, width = down.shape
    step = min(STEP_IN, total)
    count = aux.shape[1]

    def down_block(s, b, pos):
        use = b
        for i, (step_index, a) in enumerate(sources):
            valid, _ = arrival(pos[0], size, step_index, a)
            use = jnp.where((s == i) & jnp.logical_not(valid), 0, use)
        return use, 0

    return call(
        functools.partial(project_in_body, rank, chunks, size, sources),
        jax.ShapeDtypeStruct(before.shape, F32),
        grid=(len(sources), total // step),
        in_specs=[pl.BlockSpec((step, width), down_block), whole(aux.shape), whole(before.shape)]
        + [whole(r.shape) for r in rows],
        out_specs=whole(before.shape),
        scratch=[pltpu.VMEM((2 * rank, count), F32)],
        prefetch=1,
        aliases={3: 0},
        flops=2 * count * total * width,
        moved=2 * (count * width + total * width),
        after=after,
    )(pos, down, aux, before, *rows)


def adapter_rows_body(rank, size, place, pos_ref, part_ref, aux_ref, down_ref, *refs):
    out_ref, spread_ref = refs[-2:]
    count = aux_ref.shape[1]
    total = down_ref.shape[0]

    @pl.when(pl.program_id(0) == 0)
    def _():
        slot = slot_at(pos_ref[0], size, place)
        low = part_ref[pl.ds(pl.multiple_of(slot * 2 * rank, 2 * rank), 2 * rank), :]
        aux = aux_ref[pl.ds(pl.multiple_of(slot * 8, 8), 8), :]
        repeat = 128 // rank
        group = (lax.broadcasted_iota(jnp.int32, (128, count), 0) // rank).astype(F32)
        keys, values = [], []
        for k in range(2):
            scaled = (aux[2 + k : 3 + k, :] * low[k * rank : (k + 1) * rank, :]).astype(BF).astype(F32)
            values.append(jnp.concatenate([scaled] * repeat, axis=0).T)
            keys.append((aux[k : k + 1, :] - group).T)
        tile = 32
        for t in range(count // tile):
            rows = slice(t * tile, (t + 1) * tile)
            key = [k[rows] for k in keys]
            value = [v[rows] for v in values]
            for g in range(total // 128):
                first = float(g * repeat)
                spread = jnp.where(key[0] == first, value[0], jnp.where(key[1] == first, value[1], 0.0))
                spread_ref[rows, g * 128 : (g + 1) * 128] = spread.astype(BF)

    rows = jnp.dot(spread_ref[...], down_ref[...], preferred_element_type=F32)
    if len(refs) == 3:
        rows = rows + refs[0][...]
    out_ref[...] = rows.astype(out_ref.dtype)


def adapter_rows(pos, size, place, part, aux, down, rank, frozen=None, after=()):
    total, width = down.shape
    count = aux.shape[1]
    step = STEP_ROWS if width % STEP_ROWS == 0 else 256
    block = pl.BlockSpec((count, step), lambda n, pos: (0, n))
    more = [] if frozen is None else [frozen]
    return call(
        functools.partial(adapter_rows_body, rank, size, place),
        jax.ShapeDtypeStruct((count, width), BF if frozen is None else F32),
        grid=(width // step,),
        in_specs=[
            whole(part.shape), whole(aux.shape), pl.BlockSpec((total, step), lambda n, pos: (0, n)),
        ]
        + [block] * len(more),
        out_specs=block,
        scratch=[pltpu.VMEM((count, total), BF)],
        prefetch=1,
        flops=2 * count * total * width,
        moved=2 * (total * width + count * width),
        after=after,
    )(pos, part, aux, down, *more)


def frozen_body(count, share_ref, own_ref, near_ref, far_ref, weight_ref, out_ref):
    width = own_ref.shape[1]
    blocks = [own_ref[...], near_ref[...]]
    blocks += [far_ref[i * count : (i + 1) * count, :] for i in range(far_ref.shape[0] // count)]
    total = 0.0
    for i, block in enumerate(blocks):
        start = pl.multiple_of((share_ref[0] ^ i) * width, width)
        total = total + lax.dot_general(
            block, weight_ref[:, pl.ds(start, width)], NT, preferred_element_type=F32
        )
    out_ref[...] = total


def frozen_product(share, own, near, far, weight, after):
    count = own.shape[0]
    total, width = weight.shape
    step = 512 if total % 512 == 0 else 256
    return call(
        functools.partial(frozen_body, count),
        jax.ShapeDtypeStruct((count, total), F32),
        grid=(total // step,),
        in_specs=[whole(own.shape), whole(near.shape), whole(far.shape)]
        + [pl.BlockSpec((step, width), lambda n, share: (n, 0))],
        out_specs=pl.BlockSpec((count, step), lambda n, share: (0, n)),
        prefetch=1,
        flops=2 * count * width * total,
        moved=4 * count * total,
        after=after,
    )(share, own, near, far, weight)


def add_body(size, step_index, row, pos_ref, first_ref, second_ref, near_ref, far_ref, *refs):
    outs = refs[:2]
    held, terms, in_sem, term_sem, out_sem = refs[2:]
    sources = (first_ref, second_ref)
    pieces = in_sem.shape[1]
    piece = held.shape[1] // pieces
    d = pos_ref[0]

    def get(i, q):
        rows = pl.ds(q * piece, piece)
        return pltpu.make_async_copy(sources[i].at[rows], held.at[i, rows], in_sem.at[i, q])

    def put(i, q):
        rows = pl.ds(q * piece, piece)
        return pltpu.make_async_copy(held.at[i, rows], outs[i].at[rows], out_sem.at[i, q])

    def term(i, q, ref):
        rows = pl.ds(q * piece, piece)
        return pltpu.make_async_copy(
            ref.at[pl.ds(row + q * piece, piece)], terms.at[i, rows], term_sem.at[i, q]
        )

    plans = [departure(d, size, step_index, i == 0) for i in range(2)]
    for i, (do, slot) in enumerate(plans):
        place = place_of(d, size, slot)

        @pl.when(do)
        def _():
            for q in range(pieces):
                get(i, q).start()

                @pl.when(place == 0)
                def _():
                    term(i, q, near_ref).start()

                @pl.when(place != 0)
                def _():
                    term(i, q, far_ref).start()

    for i, (do, _) in enumerate(plans):

        @pl.when(do)
        def _():
            for q in range(pieces):
                get(i, q).wait()
                term(i, q, near_ref).wait()
                rows = pl.ds(q * piece, piece)
                held[i, rows, :] = (held[i, rows, :].astype(F32) + terms[i, rows, :].astype(F32)).astype(BF)
                put(i, q).start()

    for i, (do, _) in enumerate(plans):

        @pl.when(do)
        def _():
            for q in range(pieces):
                put(i, q).wait()


def ring_add(pos, size, step_index, row, first, second, near, far, after):
    shape = first.shape
    pieces = 4 if shape[0] % 64 == 0 else 1
    return call(
        functools.partial(add_body, size, step_index, row),
        [jax.ShapeDtypeStruct(shape, BF)] * 2,
        in_specs=[ANY] * 4,
        out_specs=[ANY] * 2,
        scratch=[
            pltpu.VMEM((2,) + shape, BF),
            pltpu.VMEM((2,) + shape, BF),
            pltpu.SemaphoreType.DMA((2, pieces)),
            pltpu.SemaphoreType.DMA((2, pieces)),
            pltpu.SemaphoreType.DMA((2, pieces)),
        ],
        prefetch=1,
        aliases={1: 0, 2: 1},
        flops=2 * shape[0] * shape[1],
        moved=6 * shape[0] * shape[1],
        after=after,
    )(pos, first, second, near, far)


def spread_rows(values, ids, first, adapters):
    rows = []
    for a in range(adapters):
        here = (first + a).astype(F32)
        rows.append(
            jnp.where(ids[0:1, :] == here, values[0], jnp.where(ids[1:2, :] == here, values[1], 0.0)).astype(BF)
        )
    return jnp.concatenate(rows, axis=0)


def grad_down_body(rank, size, where, pos_ref, part_ref, aux_ref, *refs):
    row_refs = refs[: len(where)]
    out_ref, rows_ref, scaled_ref, ids_ref, sem = refs[-5:]
    b = pl.program_id(0)
    count = aux_ref.shape[1]
    places = rows_ref.shape[0] // count
    step = out_ref.shape[0]

    def copies(act):
        for i, (step_index, a, offset) in enumerate(where):
            height = row_refs[i].shape[0]
            valid, slot = arrival(pos_ref[0], size, step_index, a)
            place = place_of(pos_ref[0], size, slot)

            @pl.when(valid)
            def _():
                start = pl.multiple_of(place * count + offset, height)
                act(pltpu.make_async_copy(row_refs[i], rows_ref.at[pl.ds(start, height)], sem.at[i]))

    @pl.when(b == 0)
    def _():
        copies(lambda c: c.start())
        for p in range(places):
            slot = slot_at(pos_ref[0], size, p)
            low = part_ref[pl.ds(pl.multiple_of(slot * 2 * rank, 2 * rank), 2 * rank), :]
            aux = aux_ref[pl.ds(pl.multiple_of(slot * 8, 8), 8), :]
            columns = slice(p * count, (p + 1) * count)
            ids_ref[:, columns] = aux
            for k in range(2):
                scaled = aux[2 + k : 3 + k, :] * low[k * rank : (k + 1) * rank, :]
                scaled_ref[k, :, columns] = scaled.astype(BF).astype(F32)
        copies(lambda c: c.wait())

    spread = []
    for p in range(places):
        columns = slice(p * count, (p + 1) * count)
        values = [scaled_ref[k, :, columns] for k in range(2)]
        spread.append(spread_rows(values, ids_ref[0:2, columns], b * (step // rank), step // rank))
    spread = spread[0] if places == 1 else jnp.concatenate(spread, axis=1)
    out = jnp.dot(spread, rows_ref[...], preferred_element_type=F32)
    out_ref[...] = out.astype(BF)


def grad_down(pos, size, part, aux, rows, where, total, rank, after):
    places = size
    count = aux.shape[1]
    width = rows[0].shape[1]
    step = min(STEP_DOWN, total)
    block = pl.BlockSpec((step, width), lambda b, pos: (b, 0))
    return call(
        functools.partial(grad_down_body, rank, size, where),
        jax.ShapeDtypeStruct((total, width), BF),
        grid=(total // step,),
        in_specs=[whole(part.shape), whole(aux.shape)] + [ANY] * len(rows),
        out_specs=block,
        scratch=[
            pltpu.VMEM((places * count, width), BF),
            pltpu.VMEM((2, rank, places * count), F32),
            pltpu.VMEM((8, places * count), F32),
            pltpu.SemaphoreType.DMA((len(rows),)),
        ],
        prefetch=1,
        flops=2 * places * count * total * width,
        moved=2 * (total * width + places * count * width),
        vmem=34 if places * count * width <= 1 << 22 else 60,
        after=after,
    )(pos, part, aux, *rows)


def grad_gates_body(rank, in_ref, out_ref, *gate_refs):
    for s, gate_ref in enumerate(gate_refs):
        at = slice(2 * rank * s, 2 * rank * (s + 1))
        both = in_ref[at, :] * out_ref[at, :]
        gates = [jnp.sum(both[k * rank : (k + 1) * rank, :], axis=0, keepdims=True) for k in range(2)]
        gate_ref[...] = jnp.concatenate(gates, axis=0).astype(BF)


def grad_gates(part_in, part_out, slots, rank, after):
    shape = part_in.shape
    return call(
        functools.partial(grad_gates_body, rank),
        [jax.ShapeDtypeStruct((2, shape[1]), BF)] * slots,
        in_specs=[whole(shape)] * 2,
        out_specs=[whole((2, shape[1]))] * slots,
        moved=8 * shape[0] * shape[1],
        after=after,
    )(part_in, part_out)


def grad_up_body(rank, slots, in_ref, aux_ref, *refs):
    blocks, (up_ref, rows_ref, scaled_ref) = refs[:slots], refs[slots:]
    b = pl.program_id(0)
    count = aux_ref.shape[1]
    step = up_ref.shape[0]

    @pl.when(b == 0)
    def _():
        for s in range(slots):
            rows_ref[s * count : (s + 1) * count, :] = blocks[s][:count, :]
            for k in range(2):
                at = slice(2 * rank * s + k * rank, 2 * rank * s + (k + 1) * rank)
                scaled = aux_ref[8 * s + 2 + k : 8 * s + 3 + k, :] * in_ref[at, :]
                scaled_ref[k, :, s * count : (s + 1) * count] = scaled.astype(BF).astype(F32)

    spread = []
    for s in range(slots):
        values = [scaled_ref[k, :, s * count : (s + 1) * count] for k in range(2)]
        spread.append(
            spread_rows(values, aux_ref[8 * s : 8 * s + 2, :], b * (step // rank), step // rank)
        )
    up_ref[...] = jnp.dot(
        jnp.concatenate(spread, axis=1), rows_ref[...], preferred_element_type=F32
    ).astype(BF)


def grad_up(part_in, aux, blocks, total, rank, after=()):
    count = aux.shape[1]
    slots = len(blocks)
    width = blocks[0].shape[1]
    step = min(STEP_UP, total)
    arrays = [part_in, aux, *blocks]
    return call(
        functools.partial(grad_up_body, rank, slots),
        jax.ShapeDtypeStruct((total, width), BF),
        grid=(total // step,),
        in_specs=[whole(a.shape) for a in arrays],
        out_specs=pl.BlockSpec((step, width), lambda b: (b, 0)),
        scratch=[pltpu.VMEM((slots * count, width), BF), pltpu.VMEM((2, rank, slots * count), F32)],
        flops=2 * slots * count * total * width,
        moved=2 * (total * width + slots * count * width),
        after=after,
    )(*arrays)


def finish_body(base_ref, first_ref, second_ref, *refs):
    out_ref = refs[-1]
    out_ref[...] = (
        base_ref[...] + first_ref[...].astype(F32) + second_ref[...].astype(F32)
    ).astype(BF)


def finish(base, first, second, chunk, before, after):
    size, width = first.shape
    step = min(128, size)
    blocks = size // step
    shift = pl.BlockSpec((step, width), lambda i: (i + chunk * blocks, 0))
    local = pl.BlockSpec((step, width), lambda i: (i, 0))
    arrays = [base, first, second] + ([] if before is None else [before])
    return call(
        finish_body,
        jax.ShapeDtypeStruct(base.shape, BF),
        grid=(blocks,),
        in_specs=[shift, local, local] + ([] if before is None else [ANY]),
        out_specs=shift,
        aliases=None if before is None else {3: 0},
        flops=2 * size * width,
        moved=10 * size * width,
        after=after,
    )(*arrays)


def per_device(inputs, output_gradient, frozen_key_weight, adapter_down_factors, adapter_up_factors,
               token_adapter_index, gates):
    count, width = inputs.shape
    out_width = output_gradient.shape[1]
    size = lax.axis_size("dp")
    shares = lax.axis_size("mp")
    local, rank = adapter_down_factors.shape[:2]
    total = local * rank
    d = lax.axis_index("dp")
    odd = d % 2
    half = count // CHUNKS
    down = adapter_down_factors.reshape(total, width)
    up = adapter_up_factors.reshape(total, out_width)
    pairs_a = [p for i in range(0, size - 1, 2) for p in ((i, i + 1), (i + 1, i))]
    pairs_b = [p for i in range(1, size - 1, 2) for p in ((i, i + 1), (i + 1, i))]
    i32 = jnp.int32

    def exchange(part):
        bit = 1
        while bit < shares:
            part = part + lax.ppermute(part, "mp", [(i, i ^ bit) for i in range(shares)])
            bit *= 2
        return part

    pos = d.astype(jnp.int32).reshape(1)

    block, aux_own, _ = pack_rows(pos, token_adapter_index.T, gates.T, output_gradient, local)
    blocks = [block] + [
        lax.ppermute(block, "dp", [(i, (i + s) % size) for i in range(size)]) for s in range(1, size)
    ]
    share = lax.axis_index("mp").astype(jnp.int32).reshape(1)
    swap = lambda rows, bit: lax.ppermute(rows, "mp", [(i, i ^ bit) for i in range(shares)])
    next_out = swap(output_gradient, 1)
    held_out = jnp.concatenate([output_gradient, next_out], axis=0)
    bit = 2
    while bit < shares:
        held_out = jnp.concatenate([held_out, swap(held_out, bit)], axis=0)
        bit *= 2
    far_out = held_out[2 * count :]
    low = jnp.zeros((size * 2 * rank, count), F32)
    low, token = project_in(pos, size, [(-1, True)], down, aux_own, low, [inputs], 1, rank)

    sent, tokens = zip(*[pin(inputs[c * half : (c + 1) * half], blocks[1:]) for c in range(CHUNKS)])
    got = [[lax.ppermute(sent[c], "dp", p) for p in (pairs_a, pairs_b)] for c in range(CHUNKS)]

    frozen, token = frozen_product(share, output_gradient, next_out, far_out, frozen_key_weight, [token])
    part_out, aux, _ = project_out(pos, up, blocks, count, rank, [token, *tokens])
    part_out = exchange(part_out)
    near, token = adapter_rows(pos, size, 0, part_out, aux, down, rank)
    far = near

    def add_projection(low, sources, token):
        return project_in(
            pos, size, [k for k, _ in sources], down, aux, low, sum([v for _, v in sources], []), CHUNKS,
            rank, [token],
        )

    rows, where = [inputs], [(-1, True, 0)]
    result, waiting = None, []
    for j in range(1, size):
        term = far
        arrived = {True: [], False: []}
        for c in range(CHUNKS):
            to_a, to_b, token = ring_add(
                pos, size, j, c * half, got[c][1], got[c][0], near, term, [token]
            )
            rows += [to_b, to_a]
            where += [(j - 1, True, c * half), (j - 1, False, c * half)]
            arrived[True].append(to_b)
            arrived[False].append(to_a)
            got[c] = [lax.ppermute(to_a, "dp", pairs_a), lax.ppermute(to_b, "dp", pairs_b)]
            if c == 0:
                far, token = adapter_rows(
                    pos, size, j, part_out, aux, down, rank, frozen if j == size - 1 else None, [token]
                )
        ready = [((j - 1, True), arrived[True])] + waiting
        waiting = [((j - 1, False), arrived[False])]
        if j == size - 1:
            ready += waiting if size % 2 else []
        low, token = add_projection(low, ready, token)

    result, token = finish(far, got[0][0], got[0][1], 0, None, [token])
    low, _ = pin(low, [token])
    part_in = exchange(low)
    down_gradient, token = grad_down(pos, size, part_out, aux, rows, where, total, rank, [token])
    for c in range(1, CHUNKS):
        result, token = finish(far, got[c][0], got[c][1], c, result, [token])
    *gate_rows, token = grad_gates(part_in, part_out, size, rank, [token])
    up_gradient, _ = grad_up(part_in, aux, blocks, total, rank, [token])
    gate_sum = gate_rows[0].astype(F32)
    for s in range(1, size):
        gate_sum = gate_sum + lax.ppermute(
            gate_rows[s], "dp", [(i, (i - s) % size) for i in range(size)]
        ).astype(F32)
    return (
        result,
        gate_sum.astype(BF).T,
        down_gradient.reshape(local, rank, width),
        up_gradient.reshape(local, rank, out_width),
    )


def solution(mesh):
    in_specs = (
        P(("groups", "dp"), "mp"),
        P(("groups", "dp"), "mp"),
        P("mp", None),
        P("dp", None, "mp"),
        P("dp", None, "mp"),
        P(("groups", "dp"), None),
        P(("groups", "dp"), None),
    )
    out_specs = (
        P(("groups", "dp"), "mp"),
        P(("groups", "dp"), None),
        P(("groups", "dp"), None, "mp"),
        P(("groups", "dp"), None, "mp"),
    )
    return jax.shard_map(
        per_device, mesh=mesh, in_specs=in_specs, out_specs=out_specs, check_vma=False
    )
```

```python
import functools

import jax
import jax.numpy as jnp
from jax import lax
from jax.experimental import pallas as pl
from jax.experimental.pallas import tpu as pltpu
from jax.sharding import PartitionSpec as P

BF = jnp.bfloat16
F32 = jnp.float32
CHUNKS = 2
NT = (((1,), (1,)), ((), ()))
ANY = pl.BlockSpec(memory_space=pl.ANY)
COST = 0.02
STEP_IN = 1024
STEP_ROWS = 512
STEP_DOWN = 1024
STEP_UP = 512


def call(body, out_shape, *, grid=None, in_specs=None, out_specs=None, scratch=(), prefetch=0,
         aliases=None, flops=0, moved=0, vmem=16, after=(), cost=COST):
    steps = len(grid) if grid else 0
    several = isinstance(out_shape, (list, tuple))
    shapes = list(out_shape) if several else [out_shape]
    specs = list(out_specs) if several else [out_specs]
    taken = prefetch + len(in_specs)
    skipped = len(after)
    given = taken + skipped + len(shapes)

    def ordered(*refs):
        body(*refs[:taken], *refs[taken + skipped : given], *refs[given + 1 :])

    call_it = pl.pallas_call(
        ordered,
        out_shape=shapes + [jax.ShapeDtypeStruct((8, 128), F32)],
        grid_spec=pltpu.PrefetchScalarGridSpec(
            num_scalar_prefetch=prefetch,
            grid=grid or (1,),
            in_specs=list(in_specs) + [ANY] * skipped,
            out_specs=specs + [ANY],
            scratch_shapes=list(scratch),
        ),
        input_output_aliases=aliases or {},
        compiler_params=pltpu.CompilerParams(
            vmem_limit_bytes=vmem << 20, dimension_semantics=("arbitrary",) * max(steps, 1)
        ),
        cost_estimate=pl.CostEstimate(
            flops=int(flops * cost), bytes_accessed=int(moved * cost), transcendentals=0
        ),
    )
    return lambda *arrays: call_it(*arrays, *after)


def whole(shape):
    return pl.BlockSpec(shape, lambda *_: (0,) * len(shape))


def arrival(d, size, j, a):
    if j < 0:
        return d >= 0, 0 * d
    left = d % 2 == (1 if a else 0)
    slot = jnp.where(left, j + 1, size - 1 - j)
    valid = jnp.where(left, d >= j + 1, d + j + 1 <= size - 1)
    return valid, slot


def departure(d, size, j, a):
    right = d % 2 == (0 if a else 1)
    slot = jnp.where(right, j, size - j)
    do = jnp.where(right, j > d, j > size - 1 - d)
    return do, slot


def place_of(d, size, slot):
    return jnp.where(d < (size + 1) // 2, jnp.where(slot == 0, size - 1, slot - 1), size - 1 - slot)


def slot_at(d, size, place):
    if place == size - 1:
        return 0 * d
    return jnp.where(d < (size + 1) // 2, place + 1, size - 1 - place)


def pack_body(local, pos_ref, index_ref, gate_ref, rows_ref, out_ref, aux_ref):
    count, width = rows_ref.shape
    out_ref[:count, :] = rows_ref[...]
    index = index_ref[...]
    gate = gate_ref[...].astype(F32)
    high, low = (index >> 4).astype(F32), (index & 15).astype(F32)
    pieces = []
    for vector in (high, low, gate):
        for slot in range(2):
            for part in range(count // width):
                pieces.append(vector[slot : slot + 1, part * width : (part + 1) * width])
    extra = out_ref.shape[0] - count
    if extra > len(pieces):
        pieces.append(jnp.zeros((extra - len(pieces), width), F32))
    out_ref[count:, :] = jnp.concatenate(pieces, axis=0).astype(BF)
    aux_ref[...] = jnp.concatenate(
        [(index - pos_ref[0] * local).astype(F32), gate, jnp.zeros((4, count), F32)], axis=0
    )


def pack_rows(pos, index, gate, rows, local):
    count, width = rows.shape
    extra = -(-6 * (count // width) // 16) * 16
    shape = (count + extra, width)
    return call(
        functools.partial(pack_body, local),
        [jax.ShapeDtypeStruct(shape, BF), jax.ShapeDtypeStruct((8, count), F32)],
        in_specs=[whole(index.shape), whole(gate.shape), whole(rows.shape)],
        out_specs=[whole(shape), whole((8, count))],
        prefetch=1,
        moved=4 * count * width,
        vmem=60,
    )(pos, index, gate, rows)


def pin_body(in_ref, out_ref):
    pass


def pin(array, after):
    return call(
        pin_body,
        jax.ShapeDtypeStruct(array.shape, array.dtype),
        in_specs=[ANY],
        out_specs=ANY,
        aliases={0: 0},
        after=after,
    )(array)


def unpack_extra(block, count, width, base):
    per = count // width
    vectors = []
    for v in range(6):
        rows = block[v * per : (v + 1) * per, :].astype(F32)
        vectors.append(jnp.concatenate([rows[q : q + 1, :] for q in range(per)], axis=1))
    ids = [vectors[k] * 16.0 + vectors[2 + k] - base for k in range(2)]
    return jnp.concatenate(ids + vectors[4:6] + [jnp.zeros((4, count), F32)], axis=0)


def pick(product, ids, first, rank, kept):
    kept = list(kept)
    for a in range(product.shape[0] // rank):
        rows = product[a * rank : (a + 1) * rank, :]
        here = (first + a).astype(F32) if hasattr(first, "astype") else float(first + a)
        for k in range(2):
            kept[k] = jnp.where(ids[k : k + 1, :] == here, rows, kept[k])
    return kept


def project_out_body(rank, pos_ref, up_ref, *refs):
    blocks, (part_ref, aux_ref) = refs[:-2], refs[-2:]
    count = part_ref.shape[1]
    width = up_ref.shape[1]
    total = up_ref.shape[0]
    step = min(1024, total)
    base = (pos_ref[0] * (total // rank)).astype(F32)
    for s, block in enumerate(blocks):
        aux = unpack_extra(block[count:, :], count, width, base)
        aux_ref[8 * s : 8 * s + 8, :] = aux
        ids = aux[0:2, :]

        def body(b, kept):
            product = lax.dot_general(
                up_ref[pl.ds(pl.multiple_of(b * step, step), step), :], block[:count, :], NT,
                preferred_element_type=F32,
            )
            return tuple(pick(product, ids, b * (step // rank), rank, kept))

        zero = jnp.zeros((rank, count), F32)
        kept = lax.fori_loop(0, total // step, body, (zero, zero))
        part_ref[2 * rank * s : 2 * rank * s + rank, :] = kept[0]
        part_ref[2 * rank * s + rank : 2 * rank * (s + 1), :] = kept[1]


def project_out(pos, up, blocks, count, rank, after):
    slots = len(blocks)
    total, width = up.shape
    shapes = [(slots * 2 * rank, count), (slots * 8, count)]
    return call(
        functools.partial(project_out_body, rank),
        [jax.ShapeDtypeStruct(s, F32) for s in shapes],
        in_specs=[whole(up.shape)] + [whole(b.shape) for b in blocks],
        out_specs=[whole(s) for s in shapes],
        prefetch=1,
        flops=2 * slots * count * total * width,
        moved=2 * (slots * count * width + total * width),
        cost=5,
        after=after,
    )(pos, up, *blocks)


def project_in_body(rank, chunks, size, sources, pos_ref, down_ref, aux_ref, before_ref, *refs):
    rows, (out_ref, kept_ref) = refs[:-2], refs[-2:]
    source, b = pl.program_id(0), pl.program_id(1)
    step = down_ref.shape[0]

    @pl.when((source == 0) & (b == 0))
    def _():
        out_ref[...] = before_ref[...]

    for s, (step_index, a) in enumerate(sources):
        valid, slot = arrival(pos_ref[0], size, step_index, a)

        @pl.when((source == s) & valid)
        def _():
            @pl.when(b == 0)
            def _():
                kept_ref[...] = jnp.zeros_like(kept_ref)

            at = 0
            for c in range(chunks):
                ref = rows[s * chunks + c]
                count = ref.shape[0]
                ids = aux_ref[pl.ds(pl.multiple_of(slot * 8, 8), 8), at : at + count]
                product = lax.dot_general(down_ref[...], ref[...], NT, preferred_element_type=F32)
                kept = [kept_ref[:rank, at : at + count], kept_ref[rank:, at : at + count]]
                kept = pick(product, ids, b * (step // rank), rank, kept)
                kept_ref[:rank, at : at + count] = kept[0]
                kept_ref[rank:, at : at + count] = kept[1]
                at += count

            @pl.when(b == pl.num_programs(1) - 1)
            def _():
                out_ref[pl.ds(pl.multiple_of(slot * 2 * rank, 2 * rank), 2 * rank), :] = kept_ref[...]


def project_in(pos, size, sources, down, aux, before, rows, chunks, rank, after=()):
    total, width = down.shape
    step = min(STEP_IN, total)
    count = aux.shape[1]

    def down_block(s, b, pos):
        use = b
        for i, (step_index, a) in enumerate(sources):
            valid, _ = arrival(pos[0], size, step_index, a)
            use = jnp.where((s == i) & jnp.logical_not(valid), 0, use)
        return use, 0

    return call(
        functools.partial(project_in_body, rank, chunks, size, sources),
        jax.ShapeDtypeStruct(before.shape, F32),
        grid=(len(sources), total // step),
        in_specs=[pl.BlockSpec((step, width), down_block), whole(aux.shape), whole(before.shape)]
        + [whole(r.shape) for r in rows],
        out_specs=whole(before.shape),
        scratch=[pltpu.VMEM((2 * rank, count), F32)],
        prefetch=1,
        aliases={3: 0},
        flops=2 * count * total * width,
        moved=2 * (count * width + total * width),
        after=after,
    )(pos, down, aux, before, *rows)


def adapter_rows_body(rank, size, place, pos_ref, part_ref, aux_ref, down_ref, *refs):
    out_ref, spread_ref = refs[-2:]
    count = aux_ref.shape[1]
    total = down_ref.shape[0]

    @pl.when(pl.program_id(0) == 0)
    def _():
        slot = slot_at(pos_ref[0], size, place)
        low = part_ref[pl.ds(pl.multiple_of(slot * 2 * rank, 2 * rank), 2 * rank), :]
        aux = aux_ref[pl.ds(pl.multiple_of(slot * 8, 8), 8), :]
        repeat = 128 // rank
        group = (lax.broadcasted_iota(jnp.int32, (128, count), 0) // rank).astype(F32)
        keys, values = [], []
        for k in range(2):
            scaled = (aux[2 + k : 3 + k, :] * low[k * rank : (k + 1) * rank, :]).astype(BF).astype(F32)
            values.append(jnp.concatenate([scaled] * repeat, axis=0).T)
            keys.append((aux[k : k + 1, :] - group).T)
        tile = 32
        for t in range(count // tile):
            rows = slice(t * tile, (t + 1) * tile)
            key = [k[rows] for k in keys]
            value = [v[rows] for v in values]
            for g in range(total // 128):
                first = float(g * repeat)
                spread = jnp.where(key[0] == first, value[0], jnp.where(key[1] == first, value[1], 0.0))
                spread_ref[rows, g * 128 : (g + 1) * 128] = spread.astype(BF)

    rows = jnp.dot(spread_ref[...], down_ref[...], preferred_element_type=F32)
    if len(refs) == 3:
        rows = rows + refs[0][...]
    out_ref[...] = rows.astype(out_ref.dtype)


def adapter_rows(pos, size, place, part, aux, down, rank, frozen=None, after=()):
    total, width = down.shape
    count = aux.shape[1]
    step = STEP_ROWS if width % STEP_ROWS == 0 else 256
    block = pl.BlockSpec((count, step), lambda n, pos: (0, n))
    more = [] if frozen is None else [frozen]
    return call(
        functools.partial(adapter_rows_body, rank, size, place),
        jax.ShapeDtypeStruct((count, width), BF if frozen is None else F32),
        grid=(width // step,),
        in_specs=[
            whole(part.shape), whole(aux.shape), pl.BlockSpec((total, step), lambda n, pos: (0, n)),
        ]
        + [block] * len(more),
        out_specs=block,
        scratch=[pltpu.VMEM((count, total), BF)],
        prefetch=1,
        flops=2 * count * total * width,
        moved=2 * (total * width + count * width),
        after=after,
    )(pos, part, aux, down, *more)


def frozen_body(count, share_ref, own_ref, near_ref, far_ref, weight_ref, out_ref):
    width = own_ref.shape[1]
    blocks = [own_ref[...], near_ref[...]]
    blocks += [far_ref[i * count : (i + 1) * count, :] for i in range(far_ref.shape[0] // count)]
    total = 0.0
    for i, block in enumerate(blocks):
        start = pl.multiple_of((share_ref[0] ^ i) * width, width)
        total = total + lax.dot_general(
            block, weight_ref[:, pl.ds(start, width)], NT, preferred_element_type=F32
        )
    out_ref[...] = total


def frozen_product(share, own, near, far, weight, after):
    count = own.shape[0]
    total, width = weight.shape
    step = 512 if total % 512 == 0 else 256
    return call(
        functools.partial(frozen_body, count),
        jax.ShapeDtypeStruct((count, total), F32),
        grid=(total // step,),
        in_specs=[whole(own.shape), whole(near.shape), whole(far.shape)]
        + [pl.BlockSpec((step, width), lambda n, share: (n, 0))],
        out_specs=pl.BlockSpec((count, step), lambda n, share: (0, n)),
        prefetch=1,
        flops=2 * count * width * total,
        moved=4 * count * total,
        after=after,
    )(share, own, near, far, weight)


def add_body(size, step_index, row, pos_ref, first_ref, second_ref, near_ref, far_ref, *refs):
    outs = refs[:2]
    held, terms, in_sem, term_sem, out_sem = refs[2:]
    sources = (first_ref, second_ref)
    pieces = in_sem.shape[1]
    piece = held.shape[1] // pieces
    d = pos_ref[0]

    def get(i, q):
        rows = pl.ds(q * piece, piece)
        return pltpu.make_async_copy(sources[i].at[rows], held.at[i, rows], in_sem.at[i, q])

    def put(i, q):
        rows = pl.ds(q * piece, piece)
        return pltpu.make_async_copy(held.at[i, rows], outs[i].at[rows], out_sem.at[i, q])

    def term(i, q, ref):
        rows = pl.ds(q * piece, piece)
        return pltpu.make_async_copy(
            ref.at[pl.ds(row + q * piece, piece)], terms.at[i, rows], term_sem.at[i, q]
        )

    plans = [departure(d, size, step_index, i == 0) for i in range(2)]
    for i, (do, slot) in enumerate(plans):
        place = place_of(d, size, slot)

        @pl.when(do)
        def _():
            for q in range(pieces):
                get(i, q).start()

                @pl.when(place == 0)
                def _():
                    term(i, q, near_ref).start()

                @pl.when(place != 0)
                def _():
                    term(i, q, far_ref).start()

    for i, (do, _) in enumerate(plans):

        @pl.when(do)
        def _():
            for q in range(pieces):
                get(i, q).wait()
                term(i, q, near_ref).wait()
                rows = pl.ds(q * piece, piece)
                held[i, rows, :] = (held[i, rows, :].astype(F32) + terms[i, rows, :].astype(F32)).astype(BF)
                put(i, q).start()

    for i, (do, _) in enumerate(plans):

        @pl.when(do)
        def _():
            for q in range(pieces):
                put(i, q).wait()


def ring_add(pos, size, step_index, row, first, second, near, far, after):
    shape = first.shape
    pieces = 1
    return call(
        functools.partial(add_body, size, step_index, row),
        [jax.ShapeDtypeStruct(shape, BF)] * 2,
        in_specs=[ANY] * 4,
        out_specs=[ANY] * 2,
        scratch=[
            pltpu.VMEM((2,) + shape, BF),
            pltpu.VMEM((2,) + shape, BF),
            pltpu.SemaphoreType.DMA((2, pieces)),
            pltpu.SemaphoreType.DMA((2, pieces)),
            pltpu.SemaphoreType.DMA((2, pieces)),
        ],
        prefetch=1,
        aliases={1: 0, 2: 1},
        flops=2 * shape[0] * shape[1],
        moved=6 * shape[0] * shape[1],
        after=after,
    )(pos, first, second, near, far)


def spread_rows(values, ids, first, adapters):
    rows = []
    for a in range(adapters):
        here = (first + a).astype(F32)
        rows.append(
            jnp.where(ids[0:1, :] == here, values[0], jnp.where(ids[1:2, :] == here, values[1], 0.0)).astype(BF)
        )
    return jnp.concatenate(rows, axis=0)


def grad_down_body(rank, size, where, pos_ref, part_ref, aux_ref, *refs):
    row_refs = refs[: len(where)]
    out_ref, rows_ref, scaled_ref, ids_ref, sem = refs[-5:]
    b = pl.program_id(0)
    count = aux_ref.shape[1]
    places = rows_ref.shape[0] // count
    step = out_ref.shape[0]

    def copies(act):
        for i, (step_index, a, offset) in enumerate(where):
            height = row_refs[i].shape[0]
            valid, slot = arrival(pos_ref[0], size, step_index, a)
            place = place_of(pos_ref[0], size, slot)

            @pl.when(valid)
            def _():
                start = pl.multiple_of(place * count + offset, height)
                act(pltpu.make_async_copy(row_refs[i], rows_ref.at[pl.ds(start, height)], sem.at[i]))

    @pl.when(b == 0)
    def _():
        copies(lambda c: c.start())
        for p in range(places):
            slot = slot_at(pos_ref[0], size, p)
            low = part_ref[pl.ds(pl.multiple_of(slot * 2 * rank, 2 * rank), 2 * rank), :]
            aux = aux_ref[pl.ds(pl.multiple_of(slot * 8, 8), 8), :]
            columns = slice(p * count, (p + 1) * count)
            ids_ref[:, columns] = aux
            for k in range(2):
                scaled = aux[2 + k : 3 + k, :] * low[k * rank : (k + 1) * rank, :]
                scaled_ref[k, :, columns] = scaled.astype(BF).astype(F32)
        copies(lambda c: c.wait())

    spread = []
    for p in range(places):
        columns = slice(p * count, (p + 1) * count)
        values = [scaled_ref[k, :, columns] for k in range(2)]
        spread.append(spread_rows(values, ids_ref[0:2, columns], b * (step // rank), step // rank))
    spread = spread[0] if places == 1 else jnp.concatenate(spread, axis=1)
    out = jnp.dot(spread, rows_ref[...], preferred_element_type=F32)
    out_ref[...] = out.astype(BF)


def grad_down(pos, size, part, aux, rows, where, total, rank, after):
    places = size
    count = aux.shape[1]
    width = rows[0].shape[1]
    step = min(STEP_DOWN, total)
    block = pl.BlockSpec((step, width), lambda b, pos: (b, 0))
    return call(
        functools.partial(grad_down_body, rank, size, where),
        jax.ShapeDtypeStruct((total, width), BF),
        grid=(total // step,),
        in_specs=[whole(part.shape), whole(aux.shape)] + [ANY] * len(rows),
        out_specs=block,
        scratch=[
            pltpu.VMEM((places * count, width), BF),
            pltpu.VMEM((2, rank, places * count), F32),
            pltpu.VMEM((8, places * count), F32),
            pltpu.SemaphoreType.DMA((len(rows),)),
        ],
        prefetch=1,
        flops=2 * places * count * total * width,
        moved=2 * (total * width + places * count * width),
        vmem=34 if places * count * width <= 1 << 22 else 60,
        after=after,
    )(pos, part, aux, *rows)


def grad_gates_body(rank, in_ref, out_ref, *gate_refs):
    for s, gate_ref in enumerate(gate_refs):
        at = slice(2 * rank * s, 2 * rank * (s + 1))
        both = in_ref[at, :] * out_ref[at, :]
        gates = [jnp.sum(both[k * rank : (k + 1) * rank, :], axis=0, keepdims=True) for k in range(2)]
        gate_ref[...] = jnp.concatenate(gates, axis=0).astype(BF)


def grad_gates(part_in, part_out, slots, rank, after):
    shape = part_in.shape
    return call(
        functools.partial(grad_gates_body, rank),
        [jax.ShapeDtypeStruct((2, shape[1]), BF)] * slots,
        in_specs=[whole(shape)] * 2,
        out_specs=[whole((2, shape[1]))] * slots,
        moved=8 * shape[0] * shape[1],
        after=after,
    )(part_in, part_out)


def grad_up_body(rank, slots, in_ref, aux_ref, *refs):
    blocks, (up_ref, rows_ref, scaled_ref) = refs[:slots], refs[slots:]
    b = pl.program_id(0)
    count = aux_ref.shape[1]
    step = up_ref.shape[0]

    @pl.when(b == 0)
    def _():
        for s in range(slots):
            rows_ref[s * count : (s + 1) * count, :] = blocks[s][:count, :]
            for k in range(2):
                at = slice(2 * rank * s + k * rank, 2 * rank * s + (k + 1) * rank)
                scaled = aux_ref[8 * s + 2 + k : 8 * s + 3 + k, :] * in_ref[at, :]
                scaled_ref[k, :, s * count : (s + 1) * count] = scaled.astype(BF).astype(F32)

    spread = []
    for s in range(slots):
        values = [scaled_ref[k, :, s * count : (s + 1) * count] for k in range(2)]
        spread.append(
            spread_rows(values, aux_ref[8 * s : 8 * s + 2, :], b * (step // rank), step // rank)
        )
    up_ref[...] = jnp.dot(
        jnp.concatenate(spread, axis=1), rows_ref[...], preferred_element_type=F32
    ).astype(BF)


def grad_up(part_in, aux, blocks, total, rank, after=()):
    count = aux.shape[1]
    slots = len(blocks)
    width = blocks[0].shape[1]
    step = min(STEP_UP, total)
    arrays = [part_in, aux, *blocks]
    return call(
        functools.partial(grad_up_body, rank, slots),
        jax.ShapeDtypeStruct((total, width), BF),
        grid=(total // step,),
        in_specs=[whole(a.shape) for a in arrays],
        out_specs=pl.BlockSpec((step, width), lambda b: (b, 0)),
        scratch=[pltpu.VMEM((slots * count, width), BF), pltpu.VMEM((2, rank, slots * count), F32)],
        flops=2 * slots * count * total * width,
        moved=2 * (total * width + slots * count * width),
        after=after,
    )(*arrays)


def finish_body(base_ref, first_ref, second_ref, *refs):
    out_ref = refs[-1]
    out_ref[...] = (
        base_ref[...] + first_ref[...].astype(F32) + second_ref[...].astype(F32)
    ).astype(BF)


def finish(base, first, second, chunk, before, after):
    size, width = first.shape
    step = min(128, size)
    blocks = size // step
    shift = pl.BlockSpec((step, width), lambda i: (i + chunk * blocks, 0))
    local = pl.BlockSpec((step, width), lambda i: (i, 0))
    arrays = [base, first, second] + ([] if before is None else [before])
    return call(
        finish_body,
        jax.ShapeDtypeStruct(base.shape, BF),
        grid=(blocks,),
        in_specs=[shift, local, local] + ([] if before is None else [ANY]),
        out_specs=shift,
        aliases=None if before is None else {3: 0},
        flops=2 * size * width,
        moved=10 * size * width,
        after=after,
    )(*arrays)


def per_device(inputs, output_gradient, frozen_key_weight, adapter_down_factors, adapter_up_factors,
               token_adapter_index, gates):
    count, width = inputs.shape
    out_width = output_gradient.shape[1]
    size = lax.axis_size("dp")
    shares = lax.axis_size("mp")
    local, rank = adapter_down_factors.shape[:2]
    total = local * rank
    d = lax.axis_index("dp")
    odd = d % 2
    half = count // CHUNKS
    down = adapter_down_factors.reshape(total, width)
    up = adapter_up_factors.reshape(total, out_width)
    pairs_a = [p for i in range(0, size - 1, 2) for p in ((i, i + 1), (i + 1, i))]
    pairs_b = [p for i in range(1, size - 1, 2) for p in ((i, i + 1), (i + 1, i))]
    i32 = jnp.int32

    def exchange(part):
        bit = 1
        while bit < shares:
            part = part + lax.ppermute(part, "mp", [(i, i ^ bit) for i in range(shares)])
            bit *= 2
        return part

    pos = d.astype(jnp.int32).reshape(1)

    block, aux_own, _ = pack_rows(pos, token_adapter_index.T, gates.T, output_gradient, local)
    blocks = [block] + [
        lax.ppermute(block, "dp", [(i, (i + s) % size) for i in range(size)]) for s in range(1, size)
    ]
    share = lax.axis_index("mp").astype(jnp.int32).reshape(1)
    swap = lambda rows, bit: lax.ppermute(rows, "mp", [(i, i ^ bit) for i in range(shares)])
    next_out = swap(output_gradient, 1)
    held_out = jnp.concatenate([output_gradient, next_out], axis=0)
    bit = 2
    while bit < shares:
        held_out = jnp.concatenate([held_out, swap(held_out, bit)], axis=0)
        bit *= 2
    far_out = held_out[2 * count :]
    low = jnp.zeros((size * 2 * rank, count), F32)
    low, token = project_in(pos, size, [(-1, True)], down, aux_own, low, [inputs], 1, rank)

    sent, tokens = zip(
        *[pin(inputs[c * half : (c + 1) * half], [token] if c == 0 else blocks[1:]) for c in range(CHUNKS)]
    )
    got = [[lax.ppermute(sent[c], "dp", p) for p in (pairs_a, pairs_b)] for c in range(CHUNKS)]

    frozen, token = frozen_product(share, output_gradient, next_out, far_out, frozen_key_weight, [token])
    part_out, aux, _ = project_out(pos, up, blocks, count, rank, [token, *tokens])
    part_out = exchange(part_out)
    near, token = adapter_rows(pos, size, 0, part_out, aux, down, rank)
    far = near

    def add_projection(low, sources, token):
        return project_in(
            pos, size, [k for k, _ in sources], down, aux, low, sum([v for _, v in sources], []), CHUNKS,
            rank, [token],
        )

    rows, where = [inputs], [(-1, True, 0)]
    result, waiting = None, []
    for j in range(1, size):
        term = far
        arrived = {True: [], False: []}
        for c in range(CHUNKS):
            to_a, to_b, token = ring_add(
                pos, size, j, c * half, got[c][1], got[c][0], near, term, [token]
            )
            rows += [to_b, to_a]
            where += [(j - 1, True, c * half), (j - 1, False, c * half)]
            arrived[True].append(to_b)
            arrived[False].append(to_a)
            got[c] = [lax.ppermute(to_a, "dp", pairs_a), lax.ppermute(to_b, "dp", pairs_b)]
            if c == 0:
                far, token = adapter_rows(
                    pos, size, j, part_out, aux, down, rank, frozen if j == size - 1 else None, [token]
                )
        ready = [((j - 1, True), arrived[True])] + waiting
        waiting = [((j - 1, False), arrived[False])]
        if j == size - 1:
            ready += waiting if size % 2 else []
        low, token = add_projection(low, ready, token)

    result, token = finish(far, got[0][0], got[0][1], 0, None, [token])
    part_in = exchange(low)
    *gate_rows, token = grad_gates(part_in, part_out, size, rank, [token])
    down_gradient, token = grad_down(pos, size, part_out, aux, rows, where, total, rank, [token])
    up_gradient, token = grad_up(part_in, aux, blocks, total, rank, [token])
    for c in range(1, CHUNKS):
        result, token = finish(far, got[c][0], got[c][1], c, result, [token])
    gate_sum = gate_rows[0].astype(F32)
    for s in range(1, size):
        gate_sum = gate_sum + lax.ppermute(
            gate_rows[s], "dp", [(i, (i - s) % size) for i in range(size)]
        ).astype(F32)
    return (
        result,
        gate_sum.astype(BF).T,
        down_gradient.reshape(local, rank, width),
        up_gradient.reshape(local, rank, out_width),
    )


def solution(mesh):
    in_specs = (
        P(("groups", "dp"), "mp"),
        P(("groups", "dp"), "mp"),
        P("mp", None),
        P("dp", None, "mp"),
        P("dp", None, "mp"),
        P(("groups", "dp"), None),
        P(("groups", "dp"), None),
    )
    out_specs = (
        P(("groups", "dp"), "mp"),
        P(("groups", "dp"), None),
        P(("groups", "dp"), None, "mp"),
        P(("groups", "dp"), None, "mp"),
    )
    return jax.shard_map(
        per_device, mesh=mesh, in_specs=in_specs, out_specs=out_specs, check_vma=False
    )
```

```python
import functools

import jax
import jax.numpy as jnp
from jax import lax
from jax.experimental import pallas as pl
from jax.experimental.pallas import tpu as pltpu
from jax.sharding import PartitionSpec as P

BF = jnp.bfloat16
F32 = jnp.float32
CHUNKS = 2
NT = (((1,), (1,)), ((), ()))
ANY = pl.BlockSpec(memory_space=pl.ANY)
COST = 0.02
STEP_IN = 1024
STEP_ROWS = 512
STEP_DOWN = 1024
STEP_UP = 512


def call(body, out_shape, *, grid=None, in_specs=None, out_specs=None, scratch=(), prefetch=0,
         aliases=None, flops=0, moved=0, vmem=16, after=(), cost=COST):
    steps = len(grid) if grid else 0
    several = isinstance(out_shape, (list, tuple))
    shapes = list(out_shape) if several else [out_shape]
    specs = list(out_specs) if several else [out_specs]
    taken = prefetch + len(in_specs)
    skipped = len(after)
    given = taken + skipped + len(shapes)

    def ordered(*refs):
        body(*refs[:taken], *refs[taken + skipped : given], *refs[given + 1 :])

    call_it = pl.pallas_call(
        ordered,
        out_shape=shapes + [jax.ShapeDtypeStruct((8, 128), F32)],
        grid_spec=pltpu.PrefetchScalarGridSpec(
            num_scalar_prefetch=prefetch,
            grid=grid or (1,),
            in_specs=list(in_specs) + [ANY] * skipped,
            out_specs=specs + [ANY],
            scratch_shapes=list(scratch),
        ),
        input_output_aliases=aliases or {},
        compiler_params=pltpu.CompilerParams(
            vmem_limit_bytes=vmem << 20, dimension_semantics=("arbitrary",) * max(steps, 1)
        ),
        cost_estimate=pl.CostEstimate(
            flops=int(flops * cost), bytes_accessed=int(moved * cost), transcendentals=0
        ),
    )
    return lambda *arrays: call_it(*arrays, *after)


def whole(shape):
    return pl.BlockSpec(shape, lambda *_: (0,) * len(shape))


def arrival(d, size, j, a):
    if j < 0:
        return d >= 0, 0 * d
    left = d % 2 == (1 if a else 0)
    slot = jnp.where(left, j + 1, size - 1 - j)
    valid = jnp.where(left, d >= j + 1, d + j + 1 <= size - 1)
    return valid, slot


def departure(d, size, j, a):
    right = d % 2 == (0 if a else 1)
    slot = jnp.where(right, j, size - j)
    do = jnp.where(right, j > d, j > size - 1 - d)
    return do, slot


def place_of(d, size, slot):
    return jnp.where(d < (size + 1) // 2, jnp.where(slot == 0, size - 1, slot - 1), size - 1 - slot)


def slot_at(d, size, place):
    if place == size - 1:
        return 0 * d
    return jnp.where(d < (size + 1) // 2, place + 1, size - 1 - place)


def pack_body(local, pos_ref, index_ref, gate_ref, rows_ref, out_ref, aux_ref):
    count, width = rows_ref.shape
    out_ref[:count, :] = rows_ref[...]
    index = index_ref[...]
    gate = gate_ref[...].astype(F32)
    high, low = (index >> 4).astype(F32), (index & 15).astype(F32)
    pieces = []
    for vector in (high, low, gate):
        for slot in range(2):
            for part in range(count // width):
                pieces.append(vector[slot : slot + 1, part * width : (part + 1) * width])
    extra = out_ref.shape[0] - count
    if extra > len(pieces):
        pieces.append(jnp.zeros((extra - len(pieces), width), F32))
    out_ref[count:, :] = jnp.concatenate(pieces, axis=0).astype(BF)
    aux_ref[...] = jnp.concatenate(
        [(index - pos_ref[0] * local).astype(F32), gate, jnp.zeros((4, count), F32)], axis=0
    )


def pack_rows(pos, index, gate, rows, local):
    count, width = rows.shape
    extra = -(-6 * (count // width) // 16) * 16
    shape = (count + extra, width)
    return call(
        functools.partial(pack_body, local),
        [jax.ShapeDtypeStruct(shape, BF), jax.ShapeDtypeStruct((8, count), F32)],
        in_specs=[whole(index.shape), whole(gate.shape), whole(rows.shape)],
        out_specs=[whole(shape), whole((8, count))],
        prefetch=1,
        moved=4 * count * width,
        vmem=60,
    )(pos, index, gate, rows)


def pin_body(in_ref, out_ref):
    pass


def pin(array, after):
    return call(
        pin_body,
        jax.ShapeDtypeStruct(array.shape, array.dtype),
        in_specs=[ANY],
        out_specs=ANY,
        aliases={0: 0},
        after=after,
    )(array)


def unpack_extra(block, count, width, base):
    per = count // width
    vectors = []
    for v in range(6):
        rows = block[v * per : (v + 1) * per, :].astype(F32)
        vectors.append(jnp.concatenate([rows[q : q + 1, :] for q in range(per)], axis=1))
    ids = [vectors[k] * 16.0 + vectors[2 + k] - base for k in range(2)]
    return jnp.concatenate(ids + vectors[4:6] + [jnp.zeros((4, count), F32)], axis=0)


def pick(product, ids, first, rank, kept):
    kept = list(kept)
    for a in range(product.shape[0] // rank):
        rows = product[a * rank : (a + 1) * rank, :]
        here = (first + a).astype(F32) if hasattr(first, "astype") else float(first + a)
        for k in range(2):
            kept[k] = jnp.where(ids[k : k + 1, :] == here, rows, kept[k])
    return kept


def project_out_body(rank, pos_ref, up_ref, *refs):
    blocks, (part_ref, aux_ref) = refs[:-2], refs[-2:]
    count = part_ref.shape[1]
    width = up_ref.shape[1]
    total = up_ref.shape[0]
    step = min(1024, total)
    base = (pos_ref[0] * (total // rank)).astype(F32)
    for s, block in enumerate(blocks):
        aux = unpack_extra(block[count:, :], count, width, base)
        aux_ref[8 * s : 8 * s + 8, :] = aux
        ids = aux[0:2, :]

        def body(b, kept):
            product = lax.dot_general(
                up_ref[pl.ds(pl.multiple_of(b * step, step), step), :], block[:count, :], NT,
                preferred_element_type=F32,
            )
            return tuple(pick(product, ids, b * (step // rank), rank, kept))

        zero = jnp.zeros((rank, count), F32)
        kept = lax.fori_loop(0, total // step, body, (zero, zero))
        part_ref[2 * rank * s : 2 * rank * s + rank, :] = kept[0]
        part_ref[2 * rank * s + rank : 2 * rank * (s + 1), :] = kept[1]


def project_out(pos, up, blocks, count, rank, after):
    slots = len(blocks)
    total, width = up.shape
    shapes = [(slots * 2 * rank, count), (slots * 8, count)]
    return call(
        functools.partial(project_out_body, rank),
        [jax.ShapeDtypeStruct(s, F32) for s in shapes],
        in_specs=[whole(up.shape)] + [whole(b.shape) for b in blocks],
        out_specs=[whole(s) for s in shapes],
        prefetch=1,
        flops=2 * slots * count * total * width,
        moved=2 * (slots * count * width + total * width),
        cost=5,
        after=after,
    )(pos, up, *blocks)


def project_in_body(rank, chunks, size, sources, pos_ref, down_ref, aux_ref, before_ref, *refs):
    rows, (out_ref, kept_ref) = refs[:-2], refs[-2:]
    source, b = pl.program_id(0), pl.program_id(1)
    step = down_ref.shape[0]

    @pl.when((source == 0) & (b == 0))
    def _():
        out_ref[...] = before_ref[...]

    for s, (step_index, a) in enumerate(sources):
        valid, slot = arrival(pos_ref[0], size, step_index, a)

        @pl.when((source == s) & valid)
        def _():
            @pl.when(b == 0)
            def _():
                kept_ref[...] = jnp.zeros_like(kept_ref)

            at = 0
            for c in range(chunks):
                ref = rows[s * chunks + c]
                count = ref.shape[0]
                ids = aux_ref[pl.ds(pl.multiple_of(slot * 8, 8), 8), at : at + count]
                product = lax.dot_general(down_ref[...], ref[...], NT, preferred_element_type=F32)
                kept = [kept_ref[:rank, at : at + count], kept_ref[rank:, at : at + count]]
                kept = pick(product, ids, b * (step // rank), rank, kept)
                kept_ref[:rank, at : at + count] = kept[0]
                kept_ref[rank:, at : at + count] = kept[1]
                at += count

            @pl.when(b == pl.num_programs(1) - 1)
            def _():
                out_ref[pl.ds(pl.multiple_of(slot * 2 * rank, 2 * rank), 2 * rank), :] = kept_ref[...]


def project_in(pos, size, sources, down, aux, before, rows, chunks, rank, after=()):
    total, width = down.shape
    step = min(STEP_IN, total)
    count = aux.shape[1]

    def down_block(s, b, pos):
        use = b
        for i, (step_index, a) in enumerate(sources):
            valid, _ = arrival(pos[0], size, step_index, a)
            use = jnp.where((s == i) & jnp.logical_not(valid), 0, use)
        return use, 0

    return call(
        functools.partial(project_in_body, rank, chunks, size, sources),
        jax.ShapeDtypeStruct(before.shape, F32),
        grid=(len(sources), total // step),
        in_specs=[pl.BlockSpec((step, width), down_block), whole(aux.shape), whole(before.shape)]
        + [whole(r.shape) for r in rows],
        out_specs=whole(before.shape),
        scratch=[pltpu.VMEM((2 * rank, count), F32)],
        prefetch=1,
        aliases={3: 0},
        flops=2 * count * total * width,
        moved=2 * (count * width + total * width),
        after=after,
    )(pos, down, aux, before, *rows)


def adapter_rows_body(rank, size, place, pos_ref, part_ref, aux_ref, down_ref, *refs):
    out_ref, spread_ref = refs[-2:]
    count = aux_ref.shape[1]
    total = down_ref.shape[0]

    @pl.when(pl.program_id(0) == 0)
    def _():
        slot = slot_at(pos_ref[0], size, place)
        low = part_ref[pl.ds(pl.multiple_of(slot * 2 * rank, 2 * rank), 2 * rank), :]
        aux = aux_ref[pl.ds(pl.multiple_of(slot * 8, 8), 8), :]
        repeat = 128 // rank
        group = (lax.broadcasted_iota(jnp.int32, (128, count), 0) // rank).astype(F32)
        keys, values = [], []
        for k in range(2):
            scaled = (aux[2 + k : 3 + k, :] * low[k * rank : (k + 1) * rank, :]).astype(BF).astype(F32)
            values.append(jnp.concatenate([scaled] * repeat, axis=0).T)
            keys.append((aux[k : k + 1, :] - group).T)
        tile = 32
        for t in range(count // tile):
            rows = slice(t * tile, (t + 1) * tile)
            key = [k[rows] for k in keys]
            value = [v[rows] for v in values]
            for g in range(total // 128):
                first = float(g * repeat)
                spread = jnp.where(key[0] == first, value[0], jnp.where(key[1] == first, value[1], 0.0))
                spread_ref[rows, g * 128 : (g + 1) * 128] = spread.astype(BF)

    rows = jnp.dot(spread_ref[...], down_ref[...], preferred_element_type=F32)
    if len(refs) == 3:
        rows = rows + refs[0][...]
    out_ref[...] = rows.astype(out_ref.dtype)


def adapter_rows(pos, size, place, part, aux, down, rank, frozen=None, after=()):
    total, width = down.shape
    count = aux.shape[1]
    step = STEP_ROWS if width % STEP_ROWS == 0 else 256
    block = pl.BlockSpec((count, step), lambda n, pos: (0, n))
    more = [] if frozen is None else [frozen]
    return call(
        functools.partial(adapter_rows_body, rank, size, place),
        jax.ShapeDtypeStruct((count, width), BF if frozen is None else F32),
        grid=(width // step,),
        in_specs=[
            whole(part.shape), whole(aux.shape), pl.BlockSpec((total, step), lambda n, pos: (0, n)),
        ]
        + [block] * len(more),
        out_specs=block,
        scratch=[pltpu.VMEM((count, total), BF)],
        prefetch=1,
        flops=2 * count * total * width,
        moved=2 * (total * width + count * width),
        after=after,
    )(pos, part, aux, down, *more)


def frozen_body(count, share_ref, own_ref, near_ref, far_ref, weight_ref, out_ref):
    width = own_ref.shape[1]
    blocks = [own_ref[...], near_ref[...]]
    blocks += [far_ref[i * count : (i + 1) * count, :] for i in range(far_ref.shape[0] // count)]
    total = 0.0
    for i, block in enumerate(blocks):
        start = pl.multiple_of((share_ref[0] ^ i) * width, width)
        total = total + lax.dot_general(
            block, weight_ref[:, pl.ds(start, width)], NT, preferred_element_type=F32
        )
    out_ref[...] = total


def frozen_product(share, own, near, far, weight, after):
    count = own.shape[0]
    total, width = weight.shape
    step = 512 if total % 512 == 0 else 256
    return call(
        functools.partial(frozen_body, count),
        jax.ShapeDtypeStruct((count, total), F32),
        grid=(total // step,),
        in_specs=[whole(own.shape), whole(near.shape), whole(far.shape)]
        + [pl.BlockSpec((step, width), lambda n, share: (n, 0))],
        out_specs=pl.BlockSpec((count, step), lambda n, share: (0, n)),
        prefetch=1,
        flops=2 * count * width * total,
        moved=4 * count * total,
        after=after,
    )(share, own, near, far, weight)


def add_body(size, step_index, row, pos_ref, first_ref, second_ref, near_ref, far_ref, *refs):
    outs = refs[:2]
    held, terms, in_sem, term_sem, out_sem = refs[2:]
    sources = (first_ref, second_ref)
    pieces = in_sem.shape[1]
    piece = held.shape[1] // pieces
    d = pos_ref[0]

    def get(i, q):
        rows = pl.ds(q * piece, piece)
        return pltpu.make_async_copy(sources[i].at[rows], held.at[i, rows], in_sem.at[i, q])

    def put(i, q):
        rows = pl.ds(q * piece, piece)
        return pltpu.make_async_copy(held.at[i, rows], outs[i].at[rows], out_sem.at[i, q])

    def term(i, q, ref):
        rows = pl.ds(q * piece, piece)
        return pltpu.make_async_copy(
            ref.at[pl.ds(row + q * piece, piece)], terms.at[i, rows], term_sem.at[i, q]
        )

    plans = [departure(d, size, step_index, i == 0) for i in range(2)]
    for i, (do, slot) in enumerate(plans):
        place = place_of(d, size, slot)

        @pl.when(do)
        def _():
            for q in range(pieces):
                get(i, q).start()

                @pl.when(place == 0)
                def _():
                    term(i, q, near_ref).start()

                @pl.when(place != 0)
                def _():
                    term(i, q, far_ref).start()

    for i, (do, _) in enumerate(plans):

        @pl.when(do)
        def _():
            for q in range(pieces):
                get(i, q).wait()
                term(i, q, near_ref).wait()
                rows = pl.ds(q * piece, piece)
                held[i, rows, :] = (held[i, rows, :].astype(F32) + terms[i, rows, :].astype(F32)).astype(BF)
                put(i, q).start()

    for i, (do, _) in enumerate(plans):

        @pl.when(do)
        def _():
            for q in range(pieces):
                put(i, q).wait()


def ring_add(pos, size, step_index, row, first, second, near, far, after):
    shape = first.shape
    pieces = 1
    return call(
        functools.partial(add_body, size, step_index, row),
        [jax.ShapeDtypeStruct(shape, BF)] * 2,
        in_specs=[ANY] * 4,
        out_specs=[ANY] * 2,
        scratch=[
            pltpu.VMEM((2,) + shape, BF),
            pltpu.VMEM((2,) + shape, BF),
            pltpu.SemaphoreType.DMA((2, pieces)),
            pltpu.SemaphoreType.DMA((2, pieces)),
            pltpu.SemaphoreType.DMA((2, pieces)),
        ],
        prefetch=1,
        aliases={1: 0, 2: 1},
        flops=2 * shape[0] * shape[1],
        moved=6 * shape[0] * shape[1],
        after=after,
    )(pos, first, second, near, far)


def spread_rows(values, ids, first, adapters):
    rows = []
    for a in range(adapters):
        here = (first + a).astype(F32)
        rows.append(
            jnp.where(ids[0:1, :] == here, values[0], jnp.where(ids[1:2, :] == here, values[1], 0.0)).astype(BF)
        )
    return jnp.concatenate(rows, axis=0)


def grad_down_body(rank, size, where, pos_ref, part_ref, aux_ref, *refs):
    row_refs = refs[: len(where)]
    out_ref, rows_ref, scaled_ref, ids_ref, sem = refs[-5:]
    b = pl.program_id(0)
    count = aux_ref.shape[1]
    places = rows_ref.shape[0] // count
    step = out_ref.shape[0]

    def copies(act):
        for i, (step_index, a, offset) in enumerate(where):
            height = row_refs[i].shape[0]
            valid, slot = arrival(pos_ref[0], size, step_index, a)
            place = place_of(pos_ref[0], size, slot)

            @pl.when(valid)
            def _():
                start = pl.multiple_of(place * count + offset, height)
                act(pltpu.make_async_copy(row_refs[i], rows_ref.at[pl.ds(start, height)], sem.at[i]))

    @pl.when(b == 0)
    def _():
        copies(lambda c: c.start())
        for p in range(places):
            slot = slot_at(pos_ref[0], size, p)
            low = part_ref[pl.ds(pl.multiple_of(slot * 2 * rank, 2 * rank), 2 * rank), :]
            aux = aux_ref[pl.ds(pl.multiple_of(slot * 8, 8), 8), :]
            columns = slice(p * count, (p + 1) * count)
            ids_ref[:, columns] = aux
            for k in range(2):
                scaled = aux[2 + k : 3 + k, :] * low[k * rank : (k + 1) * rank, :]
                scaled_ref[k, :, columns] = scaled.astype(BF).astype(F32)
        copies(lambda c: c.wait())

    spread = []
    for p in range(places):
        columns = slice(p * count, (p + 1) * count)
        values = [scaled_ref[k, :, columns] for k in range(2)]
        spread.append(spread_rows(values, ids_ref[0:2, columns], b * (step // rank), step // rank))
    spread = spread[0] if places == 1 else jnp.concatenate(spread, axis=1)
    out = jnp.dot(spread, rows_ref[...], preferred_element_type=F32)
    out_ref[...] = out.astype(BF)


def grad_down(pos, size, part, aux, rows, where, total, rank, after):
    places = size
    count = aux.shape[1]
    width = rows[0].shape[1]
    step = min(STEP_DOWN, total)
    block = pl.BlockSpec((step, width), lambda b, pos: (b, 0))
    return call(
        functools.partial(grad_down_body, rank, size, where),
        jax.ShapeDtypeStruct((total, width), BF),
        grid=(total // step,),
        in_specs=[whole(part.shape), whole(aux.shape)] + [ANY] * len(rows),
        out_specs=block,
        scratch=[
            pltpu.VMEM((places * count, width), BF),
            pltpu.VMEM((2, rank, places * count), F32),
            pltpu.VMEM((8, places * count), F32),
            pltpu.SemaphoreType.DMA((len(rows),)),
        ],
        prefetch=1,
        flops=2 * places * count * total * width,
        moved=2 * (total * width + places * count * width),
        vmem=34 if places * count * width <= 1 << 22 else 60,
        after=after,
    )(pos, part, aux, *rows)


def grad_gates_body(rank, in_ref, out_ref, *gate_refs):
    for s, gate_ref in enumerate(gate_refs):
        at = slice(2 * rank * s, 2 * rank * (s + 1))
        both = in_ref[at, :] * out_ref[at, :]
        gates = [jnp.sum(both[k * rank : (k + 1) * rank, :], axis=0, keepdims=True) for k in range(2)]
        gate_ref[...] = jnp.concatenate(gates, axis=0).astype(BF)


def grad_gates(part_in, part_out, slots, rank, after):
    shape = part_in.shape
    return call(
        functools.partial(grad_gates_body, rank),
        [jax.ShapeDtypeStruct((2, shape[1]), BF)] * slots,
        in_specs=[whole(shape)] * 2,
        out_specs=[whole((2, shape[1]))] * slots,
        moved=8 * shape[0] * shape[1],
        after=after,
    )(part_in, part_out)


def grad_up_body(rank, slots, in_ref, aux_ref, *refs):
    blocks, (up_ref, rows_ref, scaled_ref) = refs[:slots], refs[slots:]
    b = pl.program_id(0)
    count = aux_ref.shape[1]
    step = up_ref.shape[0]

    @pl.when(b == 0)
    def _():
        for s in range(slots):
            rows_ref[s * count : (s + 1) * count, :] = blocks[s][:count, :]
            for k in range(2):
                at = slice(2 * rank * s + k * rank, 2 * rank * s + (k + 1) * rank)
                scaled = aux_ref[8 * s + 2 + k : 8 * s + 3 + k, :] * in_ref[at, :]
                scaled_ref[k, :, s * count : (s + 1) * count] = scaled.astype(BF).astype(F32)

    spread = []
    for s in range(slots):
        values = [scaled_ref[k, :, s * count : (s + 1) * count] for k in range(2)]
        spread.append(
            spread_rows(values, aux_ref[8 * s : 8 * s + 2, :], b * (step // rank), step // rank)
        )
    up_ref[...] = jnp.dot(
        jnp.concatenate(spread, axis=1), rows_ref[...], preferred_element_type=F32
    ).astype(BF)


def grad_up(part_in, aux, blocks, total, rank, after=()):
    count = aux.shape[1]
    slots = len(blocks)
    width = blocks[0].shape[1]
    step = min(STEP_UP, total)
    arrays = [part_in, aux, *blocks]
    return call(
        functools.partial(grad_up_body, rank, slots),
        jax.ShapeDtypeStruct((total, width), BF),
        grid=(total // step,),
        in_specs=[whole(a.shape) for a in arrays],
        out_specs=pl.BlockSpec((step, width), lambda b: (b, 0)),
        scratch=[pltpu.VMEM((slots * count, width), BF), pltpu.VMEM((2, rank, slots * count), F32)],
        flops=2 * slots * count * total * width,
        moved=2 * (total * width + slots * count * width),
        after=after,
    )(*arrays)


def finish_body(base_ref, first_ref, second_ref, *refs):
    out_ref = refs[-1]
    out_ref[...] = (
        base_ref[...] + first_ref[...].astype(F32) + second_ref[...].astype(F32)
    ).astype(BF)


def finish(base, first, second, chunk, before, after):
    size, width = first.shape
    step = min(128, size)
    blocks = size // step
    shift = pl.BlockSpec((step, width), lambda i: (i + chunk * blocks, 0))
    local = pl.BlockSpec((step, width), lambda i: (i, 0))
    arrays = [base, first, second] + ([] if before is None else [before])
    return call(
        finish_body,
        jax.ShapeDtypeStruct(base.shape, BF),
        grid=(blocks,),
        in_specs=[shift, local, local] + ([] if before is None else [ANY]),
        out_specs=shift,
        aliases=None if before is None else {3: 0},
        flops=2 * size * width,
        moved=10 * size * width,
        after=after,
    )(*arrays)


def per_device(inputs, output_gradient, frozen_key_weight, adapter_down_factors, adapter_up_factors,
               token_adapter_index, gates):
    count, width = inputs.shape
    out_width = output_gradient.shape[1]
    size = lax.axis_size("dp")
    shares = lax.axis_size("mp")
    local, rank = adapter_down_factors.shape[:2]
    total = local * rank
    d = lax.axis_index("dp")
    odd = d % 2
    half = count // CHUNKS
    down = adapter_down_factors.reshape(total, width)
    up = adapter_up_factors.reshape(total, out_width)
    pairs_a = [p for i in range(0, size - 1, 2) for p in ((i, i + 1), (i + 1, i))]
    pairs_b = [p for i in range(1, size - 1, 2) for p in ((i, i + 1), (i + 1, i))]
    i32 = jnp.int32

    def exchange(part):
        bit = 1
        while bit < shares:
            part = part + lax.ppermute(part, "mp", [(i, i ^ bit) for i in range(shares)])
            bit *= 2
        return part

    pos = d.astype(jnp.int32).reshape(1)

    block, aux_own, _ = pack_rows(pos, token_adapter_index.T, gates.T, output_gradient, local)
    blocks = [block] + [
        lax.ppermute(block, "dp", [(i, (i + s) % size) for i in range(size)]) for s in range(1, size)
    ]
    share = lax.axis_index("mp").astype(jnp.int32).reshape(1)
    swap = lambda rows, bit: lax.ppermute(rows, "mp", [(i, i ^ bit) for i in range(shares)])
    next_out = swap(output_gradient, 1)
    held_out = jnp.concatenate([output_gradient, next_out], axis=0)
    bit = 2
    while bit < shares:
        held_out = jnp.concatenate([held_out, swap(held_out, bit)], axis=0)
        bit *= 2
    far_out = held_out[2 * count :]
    low = jnp.zeros((size * 2 * rank, count), F32)
    low, token = project_in(pos, size, [(-1, True)], down, aux_own, low, [inputs], 1, rank)

    sent, tokens = zip(
        *[pin(inputs[c * half : (c + 1) * half], [token] if c == 0 else blocks[1:]) for c in range(CHUNKS)]
    )
    got = [[lax.ppermute(sent[c], "dp", p) for p in (pairs_a, pairs_b)] for c in range(CHUNKS)]

    frozen, token = frozen_product(share, output_gradient, next_out, far_out, frozen_key_weight, [token])
    part_out, aux, _ = project_out(pos, up, blocks, count, rank, [token, *tokens])
    part_out = exchange(part_out)
    near, token = adapter_rows(pos, size, 0, part_out, aux, down, rank)
    far = near

    def add_projection(low, sources, token):
        return project_in(
            pos, size, [k for k, _ in sources], down, aux, low, sum([v for _, v in sources], []), CHUNKS,
            rank, [token],
        )

    rows, where = [inputs], [(-1, True, 0)]
    result, waiting = None, []
    for j in range(1, size):
        term = far
        arrived = {True: [], False: []}
        for c in range(CHUNKS):
            to_a, to_b, token = ring_add(
                pos, size, j, c * half, got[c][1], got[c][0], near, term, [token]
            )
            rows += [to_b, to_a]
            where += [(j - 1, True, c * half), (j - 1, False, c * half)]
            arrived[True].append(to_b)
            arrived[False].append(to_a)
            got[c] = [lax.ppermute(to_a, "dp", pairs_a), lax.ppermute(to_b, "dp", pairs_b)]
            if c == 0:
                far, token = adapter_rows(
                    pos, size, j, part_out, aux, down, rank, frozen if j == size - 1 else None, [token]
                )
        ready = [((j - 1, True), arrived[True])] + waiting
        waiting = [((j - 1, False), arrived[False])]
        if j == size - 1:
            ready += waiting if size % 2 else []
        low, token = add_projection(low, ready, token)

    part_in = exchange(low)
    down_gradient, token = grad_down(pos, size, part_out, aux, rows, where, total, rank, [token])
    result, token = finish(far, got[0][0], got[0][1], 0, None, [token])
    *gate_rows, token = grad_gates(part_in, part_out, size, rank, [token])
    up_gradient, token = grad_up(part_in, aux, blocks, total, rank, [token])
    for c in range(1, CHUNKS):
        result, token = finish(far, got[c][0], got[c][1], c, result, [token])
    gate_sum = gate_rows[0].astype(F32)
    for s in range(1, size):
        gate_sum = gate_sum + lax.ppermute(
            gate_rows[s], "dp", [(i, (i - s) % size) for i in range(size)]
        ).astype(F32)
    return (
        result,
        gate_sum.astype(BF).T,
        down_gradient.reshape(local, rank, width),
        up_gradient.reshape(local, rank, out_width),
    )


def solution(mesh):
    in_specs = (
        P(("groups", "dp"), "mp"),
        P(("groups", "dp"), "mp"),
        P("mp", None),
        P("dp", None, "mp"),
        P("dp", None, "mp"),
        P(("groups", "dp"), None),
        P(("groups", "dp"), None),
    )
    out_specs = (
        P(("groups", "dp"), "mp"),
        P(("groups", "dp"), None),
        P(("groups", "dp"), None, "mp"),
        P(("groups", "dp"), None, "mp"),
    )
    return jax.shard_map(
        per_device, mesh=mesh, in_specs=in_specs, out_specs=out_specs, check_vma=False
    )
```

```python
import functools

import jax
import jax.numpy as jnp
from jax import lax
from jax.experimental import pallas as pl
from jax.experimental.pallas import tpu as pltpu
from jax.sharding import PartitionSpec as P

BF = jnp.bfloat16
F32 = jnp.float32
CHUNKS = 2
NT = (((1,), (1,)), ((), ()))
ANY = pl.BlockSpec(memory_space=pl.ANY)
COST = 0.02
STEP_IN = 1024
STEP_ROWS = 512
STEP_DOWN = 1024
STEP_UP = 512


def call(body, out_shape, *, grid=None, in_specs=None, out_specs=None, scratch=(), prefetch=0,
         aliases=None, flops=0, moved=0, vmem=16, after=(), cost=COST):
    steps = len(grid) if grid else 0
    several = isinstance(out_shape, (list, tuple))
    shapes = list(out_shape) if several else [out_shape]
    specs = list(out_specs) if several else [out_specs]
    taken = prefetch + len(in_specs)
    skipped = len(after)
    given = taken + skipped + len(shapes)

    def ordered(*refs):
        body(*refs[:taken], *refs[taken + skipped : given], *refs[given + 1 :])

    call_it = pl.pallas_call(
        ordered,
        out_shape=shapes + [jax.ShapeDtypeStruct((8, 128), F32)],
        grid_spec=pltpu.PrefetchScalarGridSpec(
            num_scalar_prefetch=prefetch,
            grid=grid or (1,),
            in_specs=list(in_specs) + [ANY] * skipped,
            out_specs=specs + [ANY],
            scratch_shapes=list(scratch),
        ),
        input_output_aliases=aliases or {},
        compiler_params=pltpu.CompilerParams(
            vmem_limit_bytes=vmem << 20, dimension_semantics=("arbitrary",) * max(steps, 1)
        ),
        cost_estimate=pl.CostEstimate(
            flops=int(flops * cost), bytes_accessed=int(moved * cost), transcendentals=0
        ),
    )
    return lambda *arrays: call_it(*arrays, *after)


def whole(shape):
    return pl.BlockSpec(shape, lambda *_: (0,) * len(shape))


def arrival(d, size, j, a):
    if j < 0:
        return d >= 0, 0 * d
    left = d % 2 == (1 if a else 0)
    slot = jnp.where(left, j + 1, size - 1 - j)
    valid = jnp.where(left, d >= j + 1, d + j + 1 <= size - 1)
    return valid, slot


def departure(d, size, j, a):
    right = d % 2 == (0 if a else 1)
    slot = jnp.where(right, j, size - j)
    do = jnp.where(right, j > d, j > size - 1 - d)
    return do, slot


def place_of(d, size, slot):
    return jnp.where(d < (size + 1) // 2, jnp.where(slot == 0, size - 1, slot - 1), size - 1 - slot)


def slot_at(d, size, place):
    if place == size - 1:
        return 0 * d
    return jnp.where(d < (size + 1) // 2, place + 1, size - 1 - place)


def pack_body(local, pos_ref, index_ref, gate_ref, rows_ref, out_ref, aux_ref):
    count, width = rows_ref.shape
    out_ref[:count, :] = rows_ref[...]
    index = index_ref[...]
    gate = gate_ref[...].astype(F32)
    high, low = (index >> 4).astype(F32), (index & 15).astype(F32)
    pieces = []
    for vector in (high, low, gate):
        for slot in range(2):
            for part in range(count // width):
                pieces.append(vector[slot : slot + 1, part * width : (part + 1) * width])
    extra = out_ref.shape[0] - count
    if extra > len(pieces):
        pieces.append(jnp.zeros((extra - len(pieces), width), F32))
    out_ref[count:, :] = jnp.concatenate(pieces, axis=0).astype(BF)
    aux_ref[...] = jnp.concatenate(
        [(index - pos_ref[0] * local).astype(F32), gate, jnp.zeros((4, count), F32)], axis=0
    )


def pack_rows(pos, index, gate, rows, local):
    count, width = rows.shape
    extra = -(-6 * (count // width) // 16) * 16
    shape = (count + extra, width)
    return call(
        functools.partial(pack_body, local),
        [jax.ShapeDtypeStruct(shape, BF), jax.ShapeDtypeStruct((8, count), F32)],
        in_specs=[whole(index.shape), whole(gate.shape), whole(rows.shape)],
        out_specs=[whole(shape), whole((8, count))],
        prefetch=1,
        moved=4 * count * width,
        vmem=60,
    )(pos, index, gate, rows)


def pin_body(in_ref, out_ref):
    pass


def pin(array, after):
    return call(
        pin_body,
        jax.ShapeDtypeStruct(array.shape, array.dtype),
        in_specs=[ANY],
        out_specs=ANY,
        aliases={0: 0},
        after=after,
    )(array)


def unpack_extra(block, count, width, base):
    per = count // width
    vectors = []
    for v in range(6):
        rows = block[v * per : (v + 1) * per, :].astype(F32)
        vectors.append(jnp.concatenate([rows[q : q + 1, :] for q in range(per)], axis=1))
    ids = [vectors[k] * 16.0 + vectors[2 + k] - base for k in range(2)]
    return jnp.concatenate(ids + vectors[4:6] + [jnp.zeros((4, count), F32)], axis=0)


def pick(product, ids, first, rank, kept):
    kept = list(kept)
    for a in range(product.shape[0] // rank):
        rows = product[a * rank : (a + 1) * rank, :]
        here = (first + a).astype(F32) if hasattr(first, "astype") else float(first + a)
        for k in range(2):
            kept[k] = jnp.where(ids[k : k + 1, :] == here, rows, kept[k])
    return kept


def project_out_body(rank, pos_ref, up_ref, *refs):
    blocks, (part_ref, aux_ref) = refs[:-2], refs[-2:]
    count = part_ref.shape[1]
    width = up_ref.shape[1]
    total = up_ref.shape[0]
    step = min(1024, total)
    base = (pos_ref[0] * (total // rank)).astype(F32)
    for s, block in enumerate(blocks):
        aux = unpack_extra(block[count:, :], count, width, base)
        aux_ref[8 * s : 8 * s + 8, :] = aux
        ids = aux[0:2, :]

        def body(b, kept):
            product = lax.dot_general(
                up_ref[pl.ds(pl.multiple_of(b * step, step), step), :], block[:count, :], NT,
                preferred_element_type=F32,
            )
            return tuple(pick(product, ids, b * (step // rank), rank, kept))

        zero = jnp.zeros((rank, count), F32)
        kept = lax.fori_loop(0, total // step, body, (zero, zero))
        part_ref[2 * rank * s : 2 * rank * s + rank, :] = kept[0]
        part_ref[2 * rank * s + rank : 2 * rank * (s + 1), :] = kept[1]


def project_out(pos, up, blocks, count, rank, after):
    slots = len(blocks)
    total, width = up.shape
    shapes = [(slots * 2 * rank, count), (slots * 8, count)]
    return call(
        functools.partial(project_out_body, rank),
        [jax.ShapeDtypeStruct(s, F32) for s in shapes],
        in_specs=[whole(up.shape)] + [whole(b.shape) for b in blocks],
        out_specs=[whole(s) for s in shapes],
        prefetch=1,
        flops=2 * slots * count * total * width,
        moved=2 * (slots * count * width + total * width),
        cost=5,
        after=after,
    )(pos, up, *blocks)


def project_in_body(rank, chunks, size, sources, pos_ref, down_ref, aux_ref, before_ref, *refs):
    rows, (out_ref, kept_ref) = refs[:-2], refs[-2:]
    source, b = pl.program_id(0), pl.program_id(1)
    step = down_ref.shape[0]

    @pl.when((source == 0) & (b == 0))
    def _():
        out_ref[...] = before_ref[...]

    for s, (step_index, a) in enumerate(sources):
        valid, slot = arrival(pos_ref[0], size, step_index, a)

        @pl.when((source == s) & valid)
        def _():
            @pl.when(b == 0)
            def _():
                kept_ref[...] = jnp.zeros_like(kept_ref)

            at = 0
            for c in range(chunks):
                ref = rows[s * chunks + c]
                count = ref.shape[0]
                ids = aux_ref[pl.ds(pl.multiple_of(slot * 8, 8), 8), at : at + count]
                product = lax.dot_general(down_ref[...], ref[...], NT, preferred_element_type=F32)
                kept = [kept_ref[:rank, at : at + count], kept_ref[rank:, at : at + count]]
                kept = pick(product, ids, b * (step // rank), rank, kept)
                kept_ref[:rank, at : at + count] = kept[0]
                kept_ref[rank:, at : at + count] = kept[1]
                at += count

            @pl.when(b == pl.num_programs(1) - 1)
            def _():
                out_ref[pl.ds(pl.multiple_of(slot * 2 * rank, 2 * rank), 2 * rank), :] = kept_ref[...]


def project_in(pos, size, sources, down, aux, before, rows, chunks, rank, after=()):
    total, width = down.shape
    step = min(STEP_IN, total)
    count = aux.shape[1]

    def down_block(s, b, pos):
        use = b
        for i, (step_index, a) in enumerate(sources):
            valid, _ = arrival(pos[0], size, step_index, a)
            use = jnp.where((s == i) & jnp.logical_not(valid), 0, use)
        return use, 0

    return call(
        functools.partial(project_in_body, rank, chunks, size, sources),
        jax.ShapeDtypeStruct(before.shape, F32),
        grid=(len(sources), total // step),
        in_specs=[pl.BlockSpec((step, width), down_block), whole(aux.shape), whole(before.shape)]
        + [whole(r.shape) for r in rows],
        out_specs=whole(before.shape),
        scratch=[pltpu.VMEM((2 * rank, count), F32)],
        prefetch=1,
        aliases={3: 0},
        flops=2 * count * total * width,
        moved=2 * (count * width + total * width),
        after=after,
    )(pos, down, aux, before, *rows)


def adapter_rows_body(rank, size, place, pos_ref, part_ref, aux_ref, down_ref, *refs):
    out_ref, spread_ref = refs[-2:]
    count = aux_ref.shape[1]
    total = down_ref.shape[0]

    @pl.when(pl.program_id(0) == 0)
    def _():
        slot = slot_at(pos_ref[0], size, place)
        low = part_ref[pl.ds(pl.multiple_of(slot * 2 * rank, 2 * rank), 2 * rank), :]
        aux = aux_ref[pl.ds(pl.multiple_of(slot * 8, 8), 8), :]
        repeat = 128 // rank
        group = (lax.broadcasted_iota(jnp.int32, (128, count), 0) // rank).astype(F32)
        keys, values = [], []
        for k in range(2):
            scaled = (aux[2 + k : 3 + k, :] * low[k * rank : (k + 1) * rank, :]).astype(BF).astype(F32)
            values.append(jnp.concatenate([scaled] * repeat, axis=0).T)
            keys.append((aux[k : k + 1, :] - group).T)
        tile = 32
        for t in range(count // tile):
            rows = slice(t * tile, (t + 1) * tile)
            key = [k[rows] for k in keys]
            value = [v[rows] for v in values]
            for g in range(total // 128):
                first = float(g * repeat)
                spread = jnp.where(key[0] == first, value[0], jnp.where(key[1] == first, value[1], 0.0))
                spread_ref[rows, g * 128 : (g + 1) * 128] = spread.astype(BF)

    rows = jnp.dot(spread_ref[...], down_ref[...], preferred_element_type=F32)
    if len(refs) == 3:
        rows = rows + refs[0][...]
    out_ref[...] = rows.astype(out_ref.dtype)


def adapter_rows(pos, size, place, part, aux, down, rank, frozen=None, after=()):
    total, width = down.shape
    count = aux.shape[1]
    step = STEP_ROWS if width % STEP_ROWS == 0 else 256
    block = pl.BlockSpec((count, step), lambda n, pos: (0, n))
    more = [] if frozen is None else [frozen]
    return call(
        functools.partial(adapter_rows_body, rank, size, place),
        jax.ShapeDtypeStruct((count, width), BF if frozen is None else F32),
        grid=(width // step,),
        in_specs=[
            whole(part.shape), whole(aux.shape), pl.BlockSpec((total, step), lambda n, pos: (0, n)),
        ]
        + [block] * len(more),
        out_specs=block,
        scratch=[pltpu.VMEM((count, total), BF)],
        prefetch=1,
        flops=2 * count * total * width,
        moved=2 * (total * width + count * width),
        after=after,
    )(pos, part, aux, down, *more)


def frozen_body(count, share_ref, own_ref, near_ref, far_ref, weight_ref, out_ref):
    width = own_ref.shape[1]
    blocks = [own_ref[...], near_ref[...]]
    blocks += [far_ref[i * count : (i + 1) * count, :] for i in range(far_ref.shape[0] // count)]
    total = 0.0
    for i, block in enumerate(blocks):
        start = pl.multiple_of((share_ref[0] ^ i) * width, width)
        total = total + lax.dot_general(
            block, weight_ref[:, pl.ds(start, width)], NT, preferred_element_type=F32
        )
    out_ref[...] = total


def frozen_product(share, own, near, far, weight, after):
    count = own.shape[0]
    total, width = weight.shape
    step = 512 if total % 512 == 0 else 256
    return call(
        functools.partial(frozen_body, count),
        jax.ShapeDtypeStruct((count, total), F32),
        grid=(total // step,),
        in_specs=[whole(own.shape), whole(near.shape), whole(far.shape)]
        + [pl.BlockSpec((step, width), lambda n, share: (n, 0))],
        out_specs=pl.BlockSpec((count, step), lambda n, share: (0, n)),
        prefetch=1,
        flops=2 * count * width * total,
        moved=4 * count * total,
        after=after,
    )(share, own, near, far, weight)


def add_body(size, step_index, row, pos_ref, first_ref, second_ref, near_ref, far_ref, *refs):
    outs = refs[:2]
    held, terms, in_sem, term_sem, out_sem = refs[2:]
    sources = (first_ref, second_ref)
    pieces = in_sem.shape[1]
    piece = held.shape[1] // pieces
    d = pos_ref[0]

    def get(i, q):
        rows = pl.ds(q * piece, piece)
        return pltpu.make_async_copy(sources[i].at[rows], held.at[i, rows], in_sem.at[i, q])

    def put(i, q):
        rows = pl.ds(q * piece, piece)
        return pltpu.make_async_copy(held.at[i, rows], outs[i].at[rows], out_sem.at[i, q])

    def term(i, q, ref):
        rows = pl.ds(q * piece, piece)
        return pltpu.make_async_copy(
            ref.at[pl.ds(row + q * piece, piece)], terms.at[i, rows], term_sem.at[i, q]
        )

    plans = [departure(d, size, step_index, i == 0) for i in range(2)]
    for i, (do, slot) in enumerate(plans):
        place = place_of(d, size, slot)

        @pl.when(do)
        def _():
            for q in range(pieces):
                get(i, q).start()

                @pl.when(place == 0)
                def _():
                    term(i, q, near_ref).start()

                @pl.when(place != 0)
                def _():
                    term(i, q, far_ref).start()

    for i, (do, _) in enumerate(plans):

        @pl.when(do)
        def _():
            for q in range(pieces):
                get(i, q).wait()
                term(i, q, near_ref).wait()
                rows = pl.ds(q * piece, piece)
                held[i, rows, :] = (held[i, rows, :].astype(F32) + terms[i, rows, :].astype(F32)).astype(BF)
                put(i, q).start()

    for i, (do, _) in enumerate(plans):

        @pl.when(do)
        def _():
            for q in range(pieces):
                put(i, q).wait()


def ring_add(pos, size, step_index, row, first, second, near, far, after):
    shape = first.shape
    pieces = 1
    return call(
        functools.partial(add_body, size, step_index, row),
        [jax.ShapeDtypeStruct(shape, BF)] * 2,
        in_specs=[ANY] * 4,
        out_specs=[ANY] * 2,
        scratch=[
            pltpu.VMEM((2,) + shape, BF),
            pltpu.VMEM((2,) + shape, BF),
            pltpu.SemaphoreType.DMA((2, pieces)),
            pltpu.SemaphoreType.DMA((2, pieces)),
            pltpu.SemaphoreType.DMA((2, pieces)),
        ],
        prefetch=1,
        aliases={1: 0, 2: 1},
        flops=2 * shape[0] * shape[1],
        moved=6 * shape[0] * shape[1],
        after=after,
    )(pos, first, second, near, far)


def spread_rows(values, ids, first, adapters):
    rows = []
    for a in range(adapters):
        here = (first + a).astype(F32)
        rows.append(
            jnp.where(ids[0:1, :] == here, values[0], jnp.where(ids[1:2, :] == here, values[1], 0.0)).astype(BF)
        )
    return jnp.concatenate(rows, axis=0)


def grad_down_body(rank, size, where, pos_ref, part_ref, aux_ref, *refs):
    row_refs = refs[: len(where)]
    out_ref, rows_ref, scaled_ref, ids_ref, sem = refs[-5:]
    b = pl.program_id(0)
    count = aux_ref.shape[1]
    places = rows_ref.shape[0] // count
    step = out_ref.shape[0]

    def copies(act):
        for i, (step_index, a, offset) in enumerate(where):
            height = row_refs[i].shape[0]
            valid, slot = arrival(pos_ref[0], size, step_index, a)
            place = place_of(pos_ref[0], size, slot)

            @pl.when(valid)
            def _():
                start = pl.multiple_of(place * count + offset, height)
                act(pltpu.make_async_copy(row_refs[i], rows_ref.at[pl.ds(start, height)], sem.at[i]))

    @pl.when(b == 0)
    def _():
        copies(lambda c: c.start())
        for p in range(places):
            slot = slot_at(pos_ref[0], size, p)
            low = part_ref[pl.ds(pl.multiple_of(slot * 2 * rank, 2 * rank), 2 * rank), :]
            aux = aux_ref[pl.ds(pl.multiple_of(slot * 8, 8), 8), :]
            columns = slice(p * count, (p + 1) * count)
            ids_ref[:, columns] = aux
            for k in range(2):
                scaled = aux[2 + k : 3 + k, :] * low[k * rank : (k + 1) * rank, :]
                scaled_ref[k, :, columns] = scaled.astype(BF).astype(F32)
        copies(lambda c: c.wait())

    spread = []
    for p in range(places):
        columns = slice(p * count, (p + 1) * count)
        values = [scaled_ref[k, :, columns] for k in range(2)]
        spread.append(spread_rows(values, ids_ref[0:2, columns], b * (step // rank), step // rank))
    spread = spread[0] if places == 1 else jnp.concatenate(spread, axis=1)
    out = jnp.dot(spread, rows_ref[...], preferred_element_type=F32)
    out_ref[...] = out.astype(BF)


def grad_down(pos, size, part, aux, rows, where, total, rank, after):
    places = size
    count = aux.shape[1]
    width = rows[0].shape[1]
    step = min(STEP_DOWN, total)
    block = pl.BlockSpec((step, width), lambda b, pos: (b, 0))
    return call(
        functools.partial(grad_down_body, rank, size, where),
        jax.ShapeDtypeStruct((total, width), BF),
        grid=(total // step,),
        in_specs=[whole(part.shape), whole(aux.shape)] + [ANY] * len(rows),
        out_specs=block,
        scratch=[
            pltpu.VMEM((places * count, width), BF),
            pltpu.VMEM((2, rank, places * count), F32),
            pltpu.VMEM((8, places * count), F32),
            pltpu.SemaphoreType.DMA((len(rows),)),
        ],
        prefetch=1,
        flops=2 * places * count * total * width,
        moved=2 * (total * width + places * count * width),
        vmem=34 if places * count * width <= 1 << 22 else 60,
        after=after,
    )(pos, part, aux, *rows)


def grad_gates_body(rank, in_ref, out_ref, *gate_refs):
    for s, gate_ref in enumerate(gate_refs):
        at = slice(2 * rank * s, 2 * rank * (s + 1))
        both = in_ref[at, :] * out_ref[at, :]
        gates = [jnp.sum(both[k * rank : (k + 1) * rank, :], axis=0, keepdims=True) for k in range(2)]
        gate_ref[...] = jnp.concatenate(gates, axis=0).astype(BF)


def grad_gates(part_in, part_out, slots, rank, after):
    shape = part_in.shape
    return call(
        functools.partial(grad_gates_body, rank),
        [jax.ShapeDtypeStruct((2, shape[1]), BF)] * slots,
        in_specs=[whole(shape)] * 2,
        out_specs=[whole((2, shape[1]))] * slots,
        moved=8 * shape[0] * shape[1],
        after=after,
    )(part_in, part_out)


def grad_up_body(rank, slots, in_ref, aux_ref, *refs):
    blocks, (up_ref, rows_ref, scaled_ref) = refs[:slots], refs[slots:]
    b = pl.program_id(0)
    count = aux_ref.shape[1]
    step = up_ref.shape[0]

    @pl.when(b == 0)
    def _():
        for s in range(slots):
            rows_ref[s * count : (s + 1) * count, :] = blocks[s][:count, :]
            for k in range(2):
                at = slice(2 * rank * s + k * rank, 2 * rank * s + (k + 1) * rank)
                scaled = aux_ref[8 * s + 2 + k : 8 * s + 3 + k, :] * in_ref[at, :]
                scaled_ref[k, :, s * count : (s + 1) * count] = scaled.astype(BF).astype(F32)

    spread = []
    for s in range(slots):
        values = [scaled_ref[k, :, s * count : (s + 1) * count] for k in range(2)]
        spread.append(
            spread_rows(values, aux_ref[8 * s : 8 * s + 2, :], b * (step // rank), step // rank)
        )
    up_ref[...] = jnp.dot(
        jnp.concatenate(spread, axis=1), rows_ref[...], preferred_element_type=F32
    ).astype(BF)


def grad_up(part_in, aux, blocks, total, rank, after=()):
    count = aux.shape[1]
    slots = len(blocks)
    width = blocks[0].shape[1]
    step = min(STEP_UP, total)
    arrays = [part_in, aux, *blocks]
    return call(
        functools.partial(grad_up_body, rank, slots),
        jax.ShapeDtypeStruct((total, width), BF),
        grid=(total // step,),
        in_specs=[whole(a.shape) for a in arrays],
        out_specs=pl.BlockSpec((step, width), lambda b: (b, 0)),
        scratch=[pltpu.VMEM((slots * count, width), BF), pltpu.VMEM((2, rank, slots * count), F32)],
        flops=2 * slots * count * total * width,
        moved=2 * (total * width + slots * count * width),
        after=after,
    )(*arrays)


def finish_body(base_ref, first_ref, second_ref, *refs):
    out_ref = refs[-1]
    out_ref[...] = (
        base_ref[...] + first_ref[...].astype(F32) + second_ref[...].astype(F32)
    ).astype(BF)


def finish(base, first, second, chunk, before, after):
    size, width = first.shape
    step = min(128, size)
    blocks = size // step
    shift = pl.BlockSpec((step, width), lambda i: (i + chunk * blocks, 0))
    local = pl.BlockSpec((step, width), lambda i: (i, 0))
    arrays = [base, first, second] + ([] if before is None else [before])
    return call(
        finish_body,
        jax.ShapeDtypeStruct(base.shape, BF),
        grid=(blocks,),
        in_specs=[shift, local, local] + ([] if before is None else [ANY]),
        out_specs=shift,
        aliases=None if before is None else {3: 0},
        flops=2 * size * width,
        moved=10 * size * width,
        after=after,
    )(*arrays)


def per_device(inputs, output_gradient, frozen_key_weight, adapter_down_factors, adapter_up_factors,
               token_adapter_index, gates):
    count, width = inputs.shape
    out_width = output_gradient.shape[1]
    size = lax.axis_size("dp")
    shares = lax.axis_size("mp")
    local, rank = adapter_down_factors.shape[:2]
    total = local * rank
    d = lax.axis_index("dp")
    odd = d % 2
    half = count // CHUNKS
    down = adapter_down_factors.reshape(total, width)
    up = adapter_up_factors.reshape(total, out_width)
    pairs_a = [p for i in range(0, size - 1, 2) for p in ((i, i + 1), (i + 1, i))]
    pairs_b = [p for i in range(1, size - 1, 2) for p in ((i, i + 1), (i + 1, i))]
    i32 = jnp.int32

    def exchange(part):
        bit = 1
        while bit < shares:
            part = part + lax.ppermute(part, "mp", [(i, i ^ bit) for i in range(shares)])
            bit *= 2
        return part

    pos = d.astype(jnp.int32).reshape(1)

    block, aux_own, _ = pack_rows(pos, token_adapter_index.T, gates.T, output_gradient, local)
    blocks = [block] + [
        lax.ppermute(block, "dp", [(i, (i + s) % size) for i in range(size)]) for s in range(1, size)
    ]
    share = lax.axis_index("mp").astype(jnp.int32).reshape(1)
    swap = lambda rows, bit: lax.ppermute(rows, "mp", [(i, i ^ bit) for i in range(shares)])
    next_out = swap(output_gradient, 1)
    held_out = jnp.concatenate([output_gradient, next_out], axis=0)
    bit = 2
    while bit < shares:
        held_out = jnp.concatenate([held_out, swap(held_out, bit)], axis=0)
        bit *= 2
    far_out = held_out[2 * count :]
    low = jnp.zeros((size * 2 * rank, count), F32)
    low, token = project_in(pos, size, [(-1, True)], down, aux_own, low, [inputs], 1, rank)

    sent, tokens = zip(
        *[pin(inputs[c * half : (c + 1) * half], [token]) for c in range(CHUNKS)]
    )
    got = [[lax.ppermute(sent[c], "dp", p) for p in (pairs_a, pairs_b)] for c in range(CHUNKS)]

    frozen, token = frozen_product(share, output_gradient, next_out, far_out, frozen_key_weight, [token])
    part_out, aux, _ = project_out(pos, up, blocks, count, rank, [token, *tokens])
    part_out = exchange(part_out)
    near, token = adapter_rows(pos, size, 0, part_out, aux, down, rank)
    far = near

    def add_projection(low, sources, token):
        return project_in(
            pos, size, [k for k, _ in sources], down, aux, low, sum([v for _, v in sources], []), CHUNKS,
            rank, [token],
        )

    rows, where = [inputs], [(-1, True, 0)]
    result, waiting = None, []
    for j in range(1, size):
        term = far
        arrived = {True: [], False: []}
        for c in range(CHUNKS):
            to_a, to_b, token = ring_add(
                pos, size, j, c * half, got[c][1], got[c][0], near, term, [token]
            )
            rows += [to_b, to_a]
            where += [(j - 1, True, c * half), (j - 1, False, c * half)]
            arrived[True].append(to_b)
            arrived[False].append(to_a)
            got[c] = [lax.ppermute(to_a, "dp", pairs_a), lax.ppermute(to_b, "dp", pairs_b)]
            if c == 0:
                far, token = adapter_rows(
                    pos, size, j, part_out, aux, down, rank, frozen if j == size - 1 else None, [token]
                )
        ready = [((j - 1, True), arrived[True])] + waiting
        waiting = [((j - 1, False), arrived[False])]
        if j == size - 1:
            ready += waiting if size % 2 else []
        low, token = add_projection(low, ready, token)

    part_in = exchange(low)
    down_gradient, token = grad_down(pos, size, part_out, aux, rows, where, total, rank, [token])
    result, token = finish(far, got[0][0], got[0][1], 0, None, [token])
    *gate_rows, token = grad_gates(part_in, part_out, size, rank, [token])
    up_gradient, token = grad_up(part_in, aux, blocks, total, rank, [token])
    for c in range(1, CHUNKS):
        result, token = finish(far, got[c][0], got[c][1], c, result, [token])
    gate_sum = gate_rows[0].astype(F32)
    for s in range(1, size):
        gate_sum = gate_sum + lax.ppermute(
            gate_rows[s], "dp", [(i, (i - s) % size) for i in range(size)]
        ).astype(F32)
    return (
        result,
        gate_sum.astype(BF).T,
        down_gradient.reshape(local, rank, width),
        up_gradient.reshape(local, rank, out_width),
    )


def solution(mesh):
    in_specs = (
        P(("groups", "dp"), "mp"),
        P(("groups", "dp"), "mp"),
        P("mp", None),
        P("dp", None, "mp"),
        P("dp", None, "mp"),
        P(("groups", "dp"), None),
        P(("groups", "dp"), None),
    )
    out_specs = (
        P(("groups", "dp"), "mp"),
        P(("groups", "dp"), None),
        P(("groups", "dp"), None, "mp"),
        P(("groups", "dp"), None, "mp"),
    )
    return jax.shard_map(
        per_device, mesh=mesh, in_specs=in_specs, out_specs=out_specs, check_vma=False
    )
```

```python
import functools

import jax
import jax.numpy as jnp
from jax import lax
from jax.experimental import pallas as pl
from jax.experimental.pallas import tpu as pltpu
from jax.sharding import PartitionSpec as P

BF = jnp.bfloat16
F32 = jnp.float32
CHUNKS = 2
NT = (((1,), (1,)), ((), ()))
ANY = pl.BlockSpec(memory_space=pl.ANY)
COST = 0.02
STEP_IN = 1024
STEP_ROWS = 512
STEP_DOWN = 1024
STEP_UP = 1024


def call(body, out_shape, *, grid=None, in_specs=None, out_specs=None, scratch=(), prefetch=0,
         aliases=None, flops=0, moved=0, vmem=16, after=(), cost=COST):
    steps = len(grid) if grid else 0
    several = isinstance(out_shape, (list, tuple))
    shapes = list(out_shape) if several else [out_shape]
    specs = list(out_specs) if several else [out_specs]
    taken = prefetch + len(in_specs)
    skipped = len(after)
    given = taken + skipped + len(shapes)

    def ordered(*refs):
        body(*refs[:taken], *refs[taken + skipped : given], *refs[given + 1 :])

    call_it = pl.pallas_call(
        ordered,
        out_shape=shapes + [jax.ShapeDtypeStruct((8, 128), F32)],
        grid_spec=pltpu.PrefetchScalarGridSpec(
            num_scalar_prefetch=prefetch,
            grid=grid or (1,),
            in_specs=list(in_specs) + [ANY] * skipped,
            out_specs=specs + [ANY],
            scratch_shapes=list(scratch),
        ),
        input_output_aliases=aliases or {},
        compiler_params=pltpu.CompilerParams(
            vmem_limit_bytes=vmem << 20, dimension_semantics=("arbitrary",) * max(steps, 1)
        ),
        cost_estimate=pl.CostEstimate(
            flops=int(flops * cost), bytes_accessed=int(moved * cost), transcendentals=0
        ),
    )
    return lambda *arrays: call_it(*arrays, *after)


def whole(shape):
    return pl.BlockSpec(shape, lambda *_: (0,) * len(shape))


def arrival(d, size, j, a):
    if j < 0:
        return d >= 0, 0 * d
    left = d % 2 == (1 if a else 0)
    slot = jnp.where(left, j + 1, size - 1 - j)
    valid = jnp.where(left, d >= j + 1, d + j + 1 <= size - 1)
    return valid, slot


def departure(d, size, j, a):
    right = d % 2 == (0 if a else 1)
    slot = jnp.where(right, j, size - j)
    do = jnp.where(right, j > d, j > size - 1 - d)
    return do, slot


def place_of(d, size, slot):
    return jnp.where(d < (size + 1) // 2, jnp.where(slot == 0, size - 1, slot - 1), size - 1 - slot)


def slot_at(d, size, place):
    if place == size - 1:
        return 0 * d
    return jnp.where(d < (size + 1) // 2, place + 1, size - 1 - place)


def pack_body(local, pos_ref, index_ref, gate_ref, rows_ref, out_ref, aux_ref):
    count, width = rows_ref.shape
    out_ref[:count, :] = rows_ref[...]
    index = index_ref[...]
    gate = gate_ref[...].astype(F32)
    high, low = (index >> 4).astype(F32), (index & 15).astype(F32)
    pieces = []
    for vector in (high, low, gate):
        for slot in range(2):
            for part in range(count // width):
                pieces.append(vector[slot : slot + 1, part * width : (part + 1) * width])
    extra = out_ref.shape[0] - count
    if extra > len(pieces):
        pieces.append(jnp.zeros((extra - len(pieces), width), F32))
    out_ref[count:, :] = jnp.concatenate(pieces, axis=0).astype(BF)
    aux_ref[...] = jnp.concatenate(
        [(index - pos_ref[0] * local).astype(F32), gate, jnp.zeros((4, count), F32)], axis=0
    )


def pack_rows(pos, index, gate, rows, local):
    count, width = rows.shape
    extra = -(-6 * (count // width) // 16) * 16
    shape = (count + extra, width)
    return call(
        functools.partial(pack_body, local),
        [jax.ShapeDtypeStruct(shape, BF), jax.ShapeDtypeStruct((8, count), F32)],
        in_specs=[whole(index.shape), whole(gate.shape), whole(rows.shape)],
        out_specs=[whole(shape), whole((8, count))],
        prefetch=1,
        moved=4 * count * width,
        vmem=60,
    )(pos, index, gate, rows)


def pin_body(in_ref, out_ref):
    pass


def pin(array, after):
    return call(
        pin_body,
        jax.ShapeDtypeStruct(array.shape, array.dtype),
        in_specs=[ANY],
        out_specs=ANY,
        aliases={0: 0},
        after=after,
    )(array)


def unpack_extra(block, count, width, base):
    per = count // width
    vectors = []
    for v in range(6):
        rows = block[v * per : (v + 1) * per, :].astype(F32)
        vectors.append(jnp.concatenate([rows[q : q + 1, :] for q in range(per)], axis=1))
    ids = [vectors[k] * 16.0 + vectors[2 + k] - base for k in range(2)]
    return jnp.concatenate(ids + vectors[4:6] + [jnp.zeros((4, count), F32)], axis=0)


def pick(product, ids, first, rank, kept):
    kept = list(kept)
    for a in range(product.shape[0] // rank):
        rows = product[a * rank : (a + 1) * rank, :]
        here = (first + a).astype(F32) if hasattr(first, "astype") else float(first + a)
        for k in range(2):
            kept[k] = jnp.where(ids[k : k + 1, :] == here, rows, kept[k])
    return kept


def project_out_body(rank, pos_ref, up_ref, *refs):
    blocks, (part_ref, aux_ref) = refs[:-2], refs[-2:]
    count = part_ref.shape[1]
    width = up_ref.shape[1]
    total = up_ref.shape[0]
    step = min(1024, total)
    base = (pos_ref[0] * (total // rank)).astype(F32)
    for s, block in enumerate(blocks):
        aux = unpack_extra(block[count:, :], count, width, base)
        aux_ref[8 * s : 8 * s + 8, :] = aux
        ids = aux[0:2, :]

        def body(b, kept):
            product = lax.dot_general(
                up_ref[pl.ds(pl.multiple_of(b * step, step), step), :], block[:count, :], NT,
                preferred_element_type=F32,
            )
            return tuple(pick(product, ids, b * (step // rank), rank, kept))

        zero = jnp.zeros((rank, count), F32)
        kept = lax.fori_loop(0, total // step, body, (zero, zero))
        part_ref[2 * rank * s : 2 * rank * s + rank, :] = kept[0]
        part_ref[2 * rank * s + rank : 2 * rank * (s + 1), :] = kept[1]


def project_out(pos, up, blocks, count, rank, after):
    slots = len(blocks)
    total, width = up.shape
    shapes = [(slots * 2 * rank, count), (slots * 8, count)]
    return call(
        functools.partial(project_out_body, rank),
        [jax.ShapeDtypeStruct(s, F32) for s in shapes],
        in_specs=[whole(up.shape)] + [whole(b.shape) for b in blocks],
        out_specs=[whole(s) for s in shapes],
        prefetch=1,
        flops=2 * slots * count * total * width,
        moved=2 * (slots * count * width + total * width),
        cost=5,
        after=after,
    )(pos, up, *blocks)


def project_in_body(rank, chunks, size, sources, pos_ref, down_ref, aux_ref, before_ref, *refs):
    rows, (out_ref, kept_ref) = refs[:-2], refs[-2:]
    source, b = pl.program_id(0), pl.program_id(1)
    step = down_ref.shape[0]

    @pl.when((source == 0) & (b == 0))
    def _():
        out_ref[...] = before_ref[...]

    for s, (step_index, a) in enumerate(sources):
        valid, slot = arrival(pos_ref[0], size, step_index, a)

        @pl.when((source == s) & valid)
        def _():
            @pl.when(b == 0)
            def _():
                kept_ref[...] = jnp.zeros_like(kept_ref)

            at = 0
            for c in range(chunks):
                ref = rows[s * chunks + c]
                count = ref.shape[0]
                ids = aux_ref[pl.ds(pl.multiple_of(slot * 8, 8), 8), at : at + count]
                product = lax.dot_general(down_ref[...], ref[...], NT, preferred_element_type=F32)
                kept = [kept_ref[:rank, at : at + count], kept_ref[rank:, at : at + count]]
                kept = pick(product, ids, b * (step // rank), rank, kept)
                kept_ref[:rank, at : at + count] = kept[0]
                kept_ref[rank:, at : at + count] = kept[1]
                at += count

            @pl.when(b == pl.num_programs(1) - 1)
            def _():
                out_ref[pl.ds(pl.multiple_of(slot * 2 * rank, 2 * rank), 2 * rank), :] = kept_ref[...]


def project_in(pos, size, sources, down, aux, before, rows, chunks, rank, after=()):
    total, width = down.shape
    step = min(STEP_IN, total)
    count = aux.shape[1]

    def down_block(s, b, pos):
        use = b
        for i, (step_index, a) in enumerate(sources):
            valid, _ = arrival(pos[0], size, step_index, a)
            use = jnp.where((s == i) & jnp.logical_not(valid), 0, use)
        return use, 0

    return call(
        functools.partial(project_in_body, rank, chunks, size, sources),
        jax.ShapeDtypeStruct(before.shape, F32),
        grid=(len(sources), total // step),
        in_specs=[pl.BlockSpec((step, width), down_block), whole(aux.shape), whole(before.shape)]
        + [whole(r.shape) for r in rows],
        out_specs=whole(before.shape),
        scratch=[pltpu.VMEM((2 * rank, count), F32)],
        prefetch=1,
        aliases={3: 0},
        flops=2 * count * total * width,
        moved=2 * (count * width + total * width),
        after=after,
    )(pos, down, aux, before, *rows)


def adapter_rows_body(rank, size, place, pos_ref, part_ref, aux_ref, down_ref, *refs):
    out_ref, spread_ref = refs[-2:]
    count = aux_ref.shape[1]
    total = down_ref.shape[0]

    @pl.when(pl.program_id(0) == 0)
    def _():
        slot = slot_at(pos_ref[0], size, place)
        low = part_ref[pl.ds(pl.multiple_of(slot * 2 * rank, 2 * rank), 2 * rank), :]
        aux = aux_ref[pl.ds(pl.multiple_of(slot * 8, 8), 8), :]
        repeat = 128 // rank
        group = (lax.broadcasted_iota(jnp.int32, (128, count), 0) // rank).astype(F32)
        keys, values = [], []
        for k in range(2):
            scaled = (aux[2 + k : 3 + k, :] * low[k * rank : (k + 1) * rank, :]).astype(BF).astype(F32)
            values.append(jnp.concatenate([scaled] * repeat, axis=0).T)
            keys.append((aux[k : k + 1, :] - group).T)
        tile = 32
        for t in range(count // tile):
            rows = slice(t * tile, (t + 1) * tile)
            key = [k[rows] for k in keys]
            value = [v[rows] for v in values]
            for g in range(total // 128):
                first = float(g * repeat)
                spread = jnp.where(key[0] == first, value[0], jnp.where(key[1] == first, value[1], 0.0))
                spread_ref[rows, g * 128 : (g + 1) * 128] = spread.astype(BF)

    rows = jnp.dot(spread_ref[...], down_ref[...], preferred_element_type=F32)
    if len(refs) == 3:
        rows = rows + refs[0][...]
    out_ref[...] = rows.astype(out_ref.dtype)


def adapter_rows(pos, size, place, part, aux, down, rank, frozen=None, after=()):
    total, width = down.shape
    count = aux.shape[1]
    step = STEP_ROWS if width % STEP_ROWS == 0 else 256
    block = pl.BlockSpec((count, step), lambda n, pos: (0, n))
    more = [] if frozen is None else [frozen]
    return call(
        functools.partial(adapter_rows_body, rank, size, place),
        jax.ShapeDtypeStruct((count, width), BF if frozen is None else F32),
        grid=(width // step,),
        in_specs=[
            whole(part.shape), whole(aux.shape), pl.BlockSpec((total, step), lambda n, pos: (0, n)),
        ]
        + [block] * len(more),
        out_specs=block,
        scratch=[pltpu.VMEM((count, total), BF)],
        prefetch=1,
        flops=2 * count * total * width,
        moved=2 * (total * width + count * width),
        after=after,
    )(pos, part, aux, down, *more)


def frozen_body(count, share_ref, own_ref, near_ref, far_ref, weight_ref, out_ref):
    width = own_ref.shape[1]
    blocks = [own_ref[...], near_ref[...]]
    blocks += [far_ref[i * count : (i + 1) * count, :] for i in range(far_ref.shape[0] // count)]
    total = 0.0
    for i, block in enumerate(blocks):
        start = pl.multiple_of((share_ref[0] ^ i) * width, width)
        total = total + lax.dot_general(
            block, weight_ref[:, pl.ds(start, width)], NT, preferred_element_type=F32
        )
    out_ref[...] = total


def frozen_product(share, own, near, far, weight, after):
    count = own.shape[0]
    total, width = weight.shape
    step = 512 if total % 512 == 0 else 256
    return call(
        functools.partial(frozen_body, count),
        jax.ShapeDtypeStruct((count, total), F32),
        grid=(total // step,),
        in_specs=[whole(own.shape), whole(near.shape), whole(far.shape)]
        + [pl.BlockSpec((step, width), lambda n, share: (n, 0))],
        out_specs=pl.BlockSpec((count, step), lambda n, share: (0, n)),
        prefetch=1,
        flops=2 * count * width * total,
        moved=4 * count * total,
        after=after,
    )(share, own, near, far, weight)


def add_body(size, step_index, row, pos_ref, first_ref, second_ref, near_ref, far_ref, *refs):
    outs = refs[:2]
    held, terms, in_sem, term_sem, out_sem = refs[2:]
    sources = (first_ref, second_ref)
    pieces = in_sem.shape[1]
    piece = held.shape[1] // pieces
    d = pos_ref[0]

    def get(i, q):
        rows = pl.ds(q * piece, piece)
        return pltpu.make_async_copy(sources[i].at[rows], held.at[i, rows], in_sem.at[i, q])

    def put(i, q):
        rows = pl.ds(q * piece, piece)
        return pltpu.make_async_copy(held.at[i, rows], outs[i].at[rows], out_sem.at[i, q])

    def term(i, q, ref):
        rows = pl.ds(q * piece, piece)
        return pltpu.make_async_copy(
            ref.at[pl.ds(row + q * piece, piece)], terms.at[i, rows], term_sem.at[i, q]
        )

    plans = [departure(d, size, step_index, i == 0) for i in range(2)]
    for i, (do, slot) in enumerate(plans):
        place = place_of(d, size, slot)

        @pl.when(do)
        def _():
            for q in range(pieces):
                get(i, q).start()

                @pl.when(place == 0)
                def _():
                    term(i, q, near_ref).start()

                @pl.when(place != 0)
                def _():
                    term(i, q, far_ref).start()

    for i, (do, _) in enumerate(plans):

        @pl.when(do)
        def _():
            for q in range(pieces):
                get(i, q).wait()
                term(i, q, near_ref).wait()
                rows = pl.ds(q * piece, piece)
                held[i, rows, :] = (held[i, rows, :].astype(F32) + terms[i, rows, :].astype(F32)).astype(BF)
                put(i, q).start()

    for i, (do, _) in enumerate(plans):

        @pl.when(do)
        def _():
            for q in range(pieces):
                put(i, q).wait()


def ring_add(pos, size, step_index, row, first, second, near, far, after):
    shape = first.shape
    pieces = 1
    return call(
        functools.partial(add_body, size, step_index, row),
        [jax.ShapeDtypeStruct(shape, BF)] * 2,
        in_specs=[ANY] * 4,
        out_specs=[ANY] * 2,
        scratch=[
            pltpu.VMEM((2,) + shape, BF),
            pltpu.VMEM((2,) + shape, BF),
            pltpu.SemaphoreType.DMA((2, pieces)),
            pltpu.SemaphoreType.DMA((2, pieces)),
            pltpu.SemaphoreType.DMA((2, pieces)),
        ],
        prefetch=1,
        aliases={1: 0, 2: 1},
        flops=2 * shape[0] * shape[1],
        moved=6 * shape[0] * shape[1],
        after=after,
    )(pos, first, second, near, far)


def spread_rows(values, ids, first, adapters):
    rows = []
    for a in range(adapters):
        here = (first + a).astype(F32)
        rows.append(
            jnp.where(ids[0:1, :] == here, values[0], jnp.where(ids[1:2, :] == here, values[1], 0.0)).astype(BF)
        )
    return jnp.concatenate(rows, axis=0)


def grad_down_body(rank, size, where, pos_ref, part_ref, aux_ref, *refs):
    row_refs = refs[: len(where)]
    out_ref, rows_ref, scaled_ref, ids_ref, sem = refs[-5:]
    b = pl.program_id(0)
    count = aux_ref.shape[1]
    places = rows_ref.shape[0] // count
    step = out_ref.shape[0]

    def copies(act):
        for i, (step_index, a, offset) in enumerate(where):
            height = row_refs[i].shape[0]
            valid, slot = arrival(pos_ref[0], size, step_index, a)
            place = place_of(pos_ref[0], size, slot)

            @pl.when(valid)
            def _():
                start = pl.multiple_of(place * count + offset, height)
                act(pltpu.make_async_copy(row_refs[i], rows_ref.at[pl.ds(start, height)], sem.at[i]))

    @pl.when(b == 0)
    def _():
        copies(lambda c: c.start())
        for p in range(places):
            slot = slot_at(pos_ref[0], size, p)
            low = part_ref[pl.ds(pl.multiple_of(slot * 2 * rank, 2 * rank), 2 * rank), :]
            aux = aux_ref[pl.ds(pl.multiple_of(slot * 8, 8), 8), :]
            columns = slice(p * count, (p + 1) * count)
            ids_ref[:, columns] = aux
            for k in range(2):
                scaled = aux[2 + k : 3 + k, :] * low[k * rank : (k + 1) * rank, :]
                scaled_ref[k, :, columns] = scaled.astype(BF).astype(F32)
        copies(lambda c: c.wait())

    spread = []
    for p in range(places):
        columns = slice(p * count, (p + 1) * count)
        values = [scaled_ref[k, :, columns] for k in range(2)]
        spread.append(spread_rows(values, ids_ref[0:2, columns], b * (step // rank), step // rank))
    spread = spread[0] if places == 1 else jnp.concatenate(spread, axis=1)
    out = jnp.dot(spread, rows_ref[...], preferred_element_type=F32)
    out_ref[...] = out.astype(BF)


def grad_down(pos, size, part, aux, rows, where, total, rank, after):
    places = size
    count = aux.shape[1]
    width = rows[0].shape[1]
    step = min(STEP_DOWN, total)
    block = pl.BlockSpec((step, width), lambda b, pos: (b, 0))
    return call(
        functools.partial(grad_down_body, rank, size, where),
        jax.ShapeDtypeStruct((total, width), BF),
        grid=(total // step,),
        in_specs=[whole(part.shape), whole(aux.shape)] + [ANY] * len(rows),
        out_specs=block,
        scratch=[
            pltpu.VMEM((places * count, width), BF),
            pltpu.VMEM((2, rank, places * count), F32),
            pltpu.VMEM((8, places * count), F32),
            pltpu.SemaphoreType.DMA((len(rows),)),
        ],
        prefetch=1,
        flops=2 * places * count * total * width,
        moved=2 * (total * width + places * count * width),
        vmem=34 if places * count * width <= 1 << 22 else 60,
        after=after,
    )(pos, part, aux, *rows)


def grad_gates_body(rank, in_ref, out_ref, *gate_refs):
    for s, gate_ref in enumerate(gate_refs):
        at = slice(2 * rank * s, 2 * rank * (s + 1))
        both = in_ref[at, :] * out_ref[at, :]
        gates = [jnp.sum(both[k * rank : (k + 1) * rank, :], axis=0, keepdims=True) for k in range(2)]
        gate_ref[...] = jnp.concatenate(gates, axis=0).astype(BF)


def grad_gates(part_in, part_out, slots, rank, after):
    shape = part_in.shape
    return call(
        functools.partial(grad_gates_body, rank),
        [jax.ShapeDtypeStruct((2, shape[1]), BF)] * slots,
        in_specs=[whole(shape)] * 2,
        out_specs=[whole((2, shape[1]))] * slots,
        moved=8 * shape[0] * shape[1],
        after=after,
    )(part_in, part_out)


def grad_up_body(rank, slots, in_ref, aux_ref, *refs):
    blocks, (up_ref, rows_ref, scaled_ref) = refs[:slots], refs[slots:]
    b = pl.program_id(0)
    count = aux_ref.shape[1]
    step = up_ref.shape[0]

    @pl.when(b == 0)
    def _():
        for s in range(slots):
            rows_ref[s * count : (s + 1) * count, :] = blocks[s][:count, :]
            for k in range(2):
                at = slice(2 * rank * s + k * rank, 2 * rank * s + (k + 1) * rank)
                scaled = aux_ref[8 * s + 2 + k : 8 * s + 3 + k, :] * in_ref[at, :]
                scaled_ref[k, :, s * count : (s + 1) * count] = scaled.astype(BF).astype(F32)

    spread = []
    for s in range(slots):
        values = [scaled_ref[k, :, s * count : (s + 1) * count] for k in range(2)]
        spread.append(
            spread_rows(values, aux_ref[8 * s : 8 * s + 2, :], b * (step // rank), step // rank)
        )
    up_ref[...] = jnp.dot(
        jnp.concatenate(spread, axis=1), rows_ref[...], preferred_element_type=F32
    ).astype(BF)


def grad_up(part_in, aux, blocks, total, rank, after=()):
    count = aux.shape[1]
    slots = len(blocks)
    width = blocks[0].shape[1]
    step = min(STEP_UP, total)
    arrays = [part_in, aux, *blocks]
    return call(
        functools.partial(grad_up_body, rank, slots),
        jax.ShapeDtypeStruct((total, width), BF),
        grid=(total // step,),
        in_specs=[whole(a.shape) for a in arrays],
        out_specs=pl.BlockSpec((step, width), lambda b: (b, 0)),
        scratch=[pltpu.VMEM((slots * count, width), BF), pltpu.VMEM((2, rank, slots * count), F32)],
        flops=2 * slots * count * total * width,
        moved=2 * (total * width + slots * count * width),
        vmem=24,
        after=after,
    )(*arrays)


def finish_body(base_ref, first_ref, second_ref, *refs):
    out_ref = refs[-1]
    out_ref[...] = (
        base_ref[...] + first_ref[...].astype(F32) + second_ref[...].astype(F32)
    ).astype(BF)


def finish(base, first, second, chunk, before, after):
    size, width = first.shape
    step = min(128, size)
    blocks = size // step
    shift = pl.BlockSpec((step, width), lambda i: (i + chunk * blocks, 0))
    local = pl.BlockSpec((step, width), lambda i: (i, 0))
    arrays = [base, first, second] + ([] if before is None else [before])
    return call(
        finish_body,
        jax.ShapeDtypeStruct(base.shape, BF),
        grid=(blocks,),
        in_specs=[shift, local, local] + ([] if before is None else [ANY]),
        out_specs=shift,
        aliases=None if before is None else {3: 0},
        flops=2 * size * width,
        moved=10 * size * width,
        after=after,
    )(*arrays)


def per_device(inputs, output_gradient, frozen_key_weight, adapter_down_factors, adapter_up_factors,
               token_adapter_index, gates):
    count, width = inputs.shape
    out_width = output_gradient.shape[1]
    size = lax.axis_size("dp")
    shares = lax.axis_size("mp")
    local, rank = adapter_down_factors.shape[:2]
    total = local * rank
    d = lax.axis_index("dp")
    odd = d % 2
    half = count // CHUNKS
    down = adapter_down_factors.reshape(total, width)
    up = adapter_up_factors.reshape(total, out_width)
    pairs_a = [p for i in range(0, size - 1, 2) for p in ((i, i + 1), (i + 1, i))]
    pairs_b = [p for i in range(1, size - 1, 2) for p in ((i, i + 1), (i + 1, i))]
    i32 = jnp.int32

    def exchange(part):
        bit = 1
        while bit < shares:
            part = part + lax.ppermute(part, "mp", [(i, i ^ bit) for i in range(shares)])
            bit *= 2
        return part

    pos = d.astype(jnp.int32).reshape(1)

    block, aux_own, _ = pack_rows(pos, token_adapter_index.T, gates.T, output_gradient, local)
    blocks = [block] + [
        lax.ppermute(block, "dp", [(i, (i + s) % size) for i in range(size)]) for s in range(1, size)
    ]
    share = lax.axis_index("mp").astype(jnp.int32).reshape(1)
    swap = lambda rows, bit: lax.ppermute(rows, "mp", [(i, i ^ bit) for i in range(shares)])
    next_out = swap(output_gradient, 1)
    held_out = jnp.concatenate([output_gradient, next_out], axis=0)
    bit = 2
    while bit < shares:
        held_out = jnp.concatenate([held_out, swap(held_out, bit)], axis=0)
        bit *= 2
    far_out = held_out[2 * count :]
    low = jnp.zeros((size * 2 * rank, count), F32)
    low, token = project_in(pos, size, [(-1, True)], down, aux_own, low, [inputs], 1, rank)

    sent, tokens = zip(
        *[pin(inputs[c * half : (c + 1) * half], [token]) for c in range(CHUNKS)]
    )
    got = [[lax.ppermute(sent[c], "dp", p) for p in (pairs_a, pairs_b)] for c in range(CHUNKS)]

    frozen, token = frozen_product(share, output_gradient, next_out, far_out, frozen_key_weight, [token])
    part_out, aux, _ = project_out(pos, up, blocks, count, rank, [token, *tokens])
    part_out = exchange(part_out)
    near, token = adapter_rows(pos, size, 0, part_out, aux, down, rank)
    far = near

    def add_projection(low, sources, token):
        return project_in(
            pos, size, [k for k, _ in sources], down, aux, low, sum([v for _, v in sources], []), CHUNKS,
            rank, [token],
        )

    rows, where = [inputs], [(-1, True, 0)]
    result, waiting = None, []
    for j in range(1, size):
        term = far
        arrived = {True: [], False: []}
        for c in range(CHUNKS):
            to_a, to_b, token = ring_add(
                pos, size, j, c * half, got[c][1], got[c][0], near, term, [token]
            )
            rows += [to_b, to_a]
            where += [(j - 1, True, c * half), (j - 1, False, c * half)]
            arrived[True].append(to_b)
            arrived[False].append(to_a)
            got[c] = [lax.ppermute(to_a, "dp", pairs_a), lax.ppermute(to_b, "dp", pairs_b)]
            if c == 0:
                far, token = adapter_rows(
                    pos, size, j, part_out, aux, down, rank, frozen if j == size - 1 else None, [token]
                )
        ready = [((j - 1, True), arrived[True])] + waiting
        waiting = [((j - 1, False), arrived[False])]
        if j == size - 1:
            ready += waiting if size % 2 else []
        low, token = add_projection(low, ready, token)

    part_in = exchange(low)
    down_gradient, token = grad_down(pos, size, part_out, aux, rows, where, total, rank, [token])
    result, token = finish(far, got[0][0], got[0][1], 0, None, [token])
    *gate_rows, token = grad_gates(part_in, part_out, size, rank, [token])
    up_gradient, token = grad_up(part_in, aux, blocks, total, rank, [token])
    for c in range(1, CHUNKS):
        result, token = finish(far, got[c][0], got[c][1], c, result, [token])
    gate_sum = gate_rows[0].astype(F32)
    for s in range(1, size):
        gate_sum = gate_sum + lax.ppermute(
            gate_rows[s], "dp", [(i, (i - s) % size) for i in range(size)]
        ).astype(F32)
    return (
        result,
        gate_sum.astype(BF).T,
        down_gradient.reshape(local, rank, width),
        up_gradient.reshape(local, rank, out_width),
    )


def solution(mesh):
    in_specs = (
        P(("groups", "dp"), "mp"),
        P(("groups", "dp"), "mp"),
        P("mp", None),
        P("dp", None, "mp"),
        P("dp", None, "mp"),
        P(("groups", "dp"), None),
        P(("groups", "dp"), None),
    )
    out_specs = (
        P(("groups", "dp"), "mp"),
        P(("groups", "dp"), None),
        P(("groups", "dp"), None, "mp"),
        P(("groups", "dp"), None, "mp"),
    )
    return jax.shard_map(
        per_device, mesh=mesh, in_specs=in_specs, out_specs=out_specs, check_vma=False
    )
```
